512 devices in a mesh: row: 16 (over z, core), col: 32 (over y, x).
Axes of the slice: x: 4, y: 8, z: 8, core: 2. Of those that a mesh axis runs over, the one named last changes fastest.
Arguments:
- points: float32 [32768, 128], P(('row', 'col')), may hold values from -6 to 6
- start_panel: float32 [32768, 64], P('row'), may hold values from -6 to 6
Outputs:
- panels: float32 [32768, 64], P('row')
- ritz_sum: float32 [64, 64], replicated
The draws below stay inside these ranges and needn't reach their ends.
All inputs are finite; a program needn't handle non-finite values.
Results may differ from the reference program's by a relative error of at most 0.0075.
Values may be sent and summed in bfloat16 or wider, within the bound.
A program may use at most 64 MiB of HBM per device.

```python
import math
import jax
import jax.numpy as jnp
from jax import lax

F = 128
VEC = 64
PASSES = 2
N = 32768
RB = 2048


def draw_points(key, part):
    key = jax.random.fold_in(key, 11)
    noise_key, sign_key, amp_key = jax.random.split(key, 3)
    block_count = N // RB
    signs = jnp.where(jax.random.bernoulli(sign_key, 0.5, (block_count, F)), 1.0, -1.0).astype(jnp.float32)
    amplitude = jax.random.uniform(amp_key, (block_count, 1), jnp.float32, 0.45, 1.0)
    centers = jnp.repeat(amplitude * signs, RB, axis=0)
    noise = jax.random.normal(noise_key, (N, F), jnp.float32)
    values = noise + centers
    return jnp.clip(values, -6.0, 6.0)


def levels(key, shape, pieces, low, largest):
    def one(position, parts):
        draws = jax.random.uniform(jax.random.fold_in(jax.random.fold_in(key, 6), position), (parts,), jnp.float32, low / len(pieces), largest / len(pieces))
        return jnp.repeat(jnp.exp(draws), shape[position] // parts).reshape((-1,) + (1,) * (len(shape) - position - 1))

    gain = one(*pieces[0])
    for cut in pieces[1:]:
        gain = gain * one(*cut)
    return gain


def bell_draw(stream_key, shape, width, bound, pieces=(), held_as=jnp.bfloat16):
    loudness = levels(stream_key, shape, pieces, -0.22, 0.18) if pieces else 1.0
    values = jax.random.normal(stream_key, shape, jnp.float32) * width * loudness
    return jnp.minimum(jnp.maximum(values, -bound), bound).astype(held_as)


def setup_inputs(seed: int = 0) -> dict:
    splits = jax.random.split(jax.random.key(seed), 3)
    points = draw_points(jax.random.fold_in(splits[2], 71), 0)
    start_panel = bell_draw(splits[1], (N, VEC), 1.0, 6.0, ((0, 16),), jnp.float32)
    return {"points": points, "start_panel": start_panel}


sharpness = 5.0

def unit_rows(values):
    return values * lax.rsqrt(lax.optimization_barrier(jnp.mean(values * values, axis=1, keepdims=True)) + 1e-06) / math.sqrt(values.shape[1])

def affinity(left_pts, right_pts):
    inner_prod = jnp.dot(left_pts.astype(jnp.float32), right_pts.T.astype(jnp.float32), precision=lax.Precision.HIGHEST, preferred_element_type=jnp.float32)
    return jnp.exp(sharpness * (inner_prod - 1.0))

def orthonormal(gram_sum, product_rows):
    factor = jnp.linalg.cholesky(gram_sum)
    return lax.linalg.triangular_solve(factor, product_rows, left_side=False, lower=True, transpose_a=True)

def reference(points, start_panel):
    unit_points = unit_rows(points)
    block_size = min(1024, N)
    point_blocks = unit_points.reshape(N // block_size, block_size, F)
    degrees = lax.map(lambda group_pts: lax.optimization_barrier(jnp.sum(affinity(group_pts, unit_points), axis=1)), point_blocks).reshape(N)
    inv_root = lax.rsqrt(degrees)
    panels = start_panel
    ritz_sum = jnp.zeros((VEC, VEC), jnp.float32)
    for pass_index in range(PASSES):
        scaled = (inv_root[:, None] * panels).astype(jnp.bfloat16)
        product_rows = lax.map(lambda group_pts: jnp.dot(affinity(group_pts, unit_points).astype(jnp.bfloat16).astype(jnp.float32), scaled.astype(jnp.float32), preferred_element_type=jnp.float32), point_blocks).reshape(N, VEC)
        product_rows = inv_root[:, None] * product_rows
        gram_sum = jnp.dot(product_rows.T.astype(jnp.float32), product_rows.astype(jnp.float32), precision=lax.Precision.HIGHEST, preferred_element_type=jnp.float32) / N
        ritz_sum = jnp.dot(panels.T.astype(jnp.float32), product_rows.astype(jnp.float32), precision=lax.Precision.HIGHEST, preferred_element_type=jnp.float32) / N
        panels = orthonormal(gram_sum, product_rows)
    return (panels, ritz_sum)
```

```python
import functools
import math

import jax
import jax.numpy as jnp
from jax import lax
from jax.experimental import pallas as pl
from jax.experimental.pallas import tpu as pltpu
from jax.sharding import PartitionSpec as P

MESH = pl.DeviceIdType.MESH
NX = 4
HALF = 32
SHARPNESS = 5.0
LOG2E = math.log2(math.e)
f32 = jnp.float32
bf16 = jnp.bfloat16


def dot(a, b, contract=((1,), (0,)), precision=None):
    return lax.dot_general(
        a, b, (contract, ((), ())), precision=precision, preferred_element_type=f32
    )


def full(a, b, contract=((1,), (0,))):
    return dot(a, b, contract, lax.Precision.HIGHEST)


def inverse_factor(gram):
    n = gram.shape[0]
    rows = lax.broadcasted_iota(jnp.int32, (n, 2 * n), 0)
    lanes = lax.broadcasted_iota(jnp.int32, (n, 2 * n), 1)
    sub = lax.broadcasted_iota(jnp.int32, (n, 1), 0)
    eye = jnp.where(rows[:, :n] == lanes[:, :n], 1.0, 0.0).astype(f32)

    def step(k, carry):
        mat, diag = carry
        col = jnp.sum(jnp.where(lanes == k, mat, 0.0), axis=1, keepdims=True)
        row = jnp.sum(jnp.where(rows == k, mat, 0.0), axis=0, keepdims=True)
        pivot = jnp.sum(jnp.where(sub == k, col, 0.0), axis=0, keepdims=True)
        mat = mat - jnp.where(sub > k, col / pivot, 0.0) * row
        return mat, jnp.where(sub == k, pivot, diag)

    start = (jnp.concatenate([gram, eye], axis=1), jnp.ones((n, 1), f32))
    mat, diag = lax.fori_loop(0, n, step, start)
    return mat[:, n:] * lax.rsqrt(diag)


def pack(mat):
    n = mat.shape[0] // 2
    return jnp.concatenate([mat[:n], mat[n:]], axis=1)


def unpack(mat):
    n = mat.shape[1] // 2
    return jnp.concatenate([mat[:, :n], mat[:, n:]], axis=0)


def kernel(
    nz, ny, points_ref, start_ref, out_ref, ritz_ref,
    rowpts, colpts, tile, startT, scaledT, deg, deg_x, deg_y, turn,
    half_c, recv_c, send_z, recv_z, scaled, send_p, recv_px, send_y, recv_py,
    gram, gram_x, gram_y, gram_c, gram_z, whole, send_sem, recv_sem,
):
    r, c = lax.axis_index("row"), lax.axis_index("col")
    z, core = r // 2, lax.rem(r, 2)
    y, x = c // NX, lax.rem(c, NX)
    axes = {
        "x": (NX, x, lambda p: (r, y * NX + p)),
        "y": (ny, y, lambda p: (r, p * NX + x)),
        "z": (nz, z, lambda p: (p * 2 + core, c)),
        "c": (2, core, lambda p: (z * 2 + p, c)),
    }
    count = (NX - 1) + (ny - 1) + (nz - 1) + 1
    total = nz * ny * NX * 2 * 2 * HALF

    barrier = pltpu.get_barrier_semaphore()
    for n, me, device in axes.values():
        def greet(i, carry):
            pl.semaphore_signal(
                barrier, inc=1, device_id=device(lax.rem(me + i, n)), device_id_type=MESH
            )
            return carry
        lax.fori_loop(1, n, greet, 0)

    sent = []

    def send(slot, axis, src, dst):
        n, me, device = axes[axis]

        def one(i, carry):
            p = lax.rem(me + i, n)
            pltpu.make_async_remote_copy(
                src_ref=src(p), dst_ref=dst, send_sem=send_sem.at[slot],
                recv_sem=recv_sem.at[slot], device_id=device(p), device_id_type=MESH,
            ).start()
            return carry
        lax.fori_loop(1, n, one, 0)

    def arrive(slot, ref):
        pltpu.make_async_copy(ref, ref, recv_sem.at[slot]).wait()
        sent.append((slot, ref))

    def all_sum(slot, axis, value, buf):
        n, me, _ = axes[axis]
        buf[me] = value
        send(slot, axis, lambda p: buf.at[me], buf.at[me])
        def done():
            arrive(slot, buf.at[pl.ds(0, n - 1)])
            return functools.reduce(lambda a, b: a + b, [buf[i] for i in range(n)])
        return done

    pts = points_ref[...]
    width = pts.shape[1]
    unit = pts * lax.rsqrt(jnp.mean(pts * pts, axis=1, keepdims=True) + 1e-06)
    unit = unit * math.sqrt(SHARPNESS * LOG2E / width)
    unit = unit.astype(bf16).reshape(2, HALF, width)
    rowpts[:, y, x] = unit
    colpts[core, :, z] = unit

    pl.semaphore_wait(barrier, count)

    send(0, "y", lambda p: rowpts.at[:, y, x], rowpts.at[:, y, x])
    send(1, "z", lambda p: colpts.at[core, :, z], colpts.at[core, :, z])

    def turn_start(t, carry):
        h, yy = t // ny, lax.rem(t, ny)
        part = start_ref[yy, :, h]
        startT[t] = part.reshape(NX * HALF, part.shape[2]).T
        return carry
    lax.fori_loop(0, 2 * ny, turn_start, 0)

    arrive(0, rowpts.at[:, pl.ds(0, ny - 1), 0])
    send(2, "x", lambda p: rowpts.at[:, :, x], rowpts.at[:, :, x])
    arrive(1, colpts.at[0, :, pl.ds(0, nz - 1)])
    send(3, "c", lambda p: colpts.at[core], colpts.at[core])
    arrive(2, rowpts.at[:, :, pl.ds(0, NX - 1)])
    arrive(3, colpts.at[0])

    ncols = 4 * nz * HALF
    wide = NX * HALF
    ones = jnp.ones((8, wide), f32)
    shift = SHARPNESS * LOG2E

    def affinity(t, carry):
        h, yy = t // ny, lax.rem(t, ny)
        left = rowpts[h, yy].reshape(wide, width)
        right = colpts[...].reshape(ncols, width)
        value = jnp.exp2(dot(left, right, ((1,), (1,))) - shift)
        tile[h, yy] = value.astype(bf16)
        part = value[:, :128]
        for j in range(1, ncols // 128):
            part = part + value[:, j * 128:(j + 1) * 128]
        sums = full(ones, part, ((1,), (1,)))
        deg[pl.ds(t, 1), :] = sums[:1]
        return carry
    lax.fori_loop(0, 2 * ny, affinity, 0)

    degrees = all_sum(4, "x", deg[...], deg_x)()
    degrees = all_sum(5, "y", degrees, deg_y)()
    inv_root = lax.rsqrt(degrees)
    deg[...] = inv_root
    for h in range(2):
        line = deg[pl.ds(h * ny + y, 1), :]
        turn[h] = jnp.broadcast_to(line, (wide, wide)).T
    low = lax.broadcasted_iota(jnp.int32, (HALF, 4 * HALF), 1) < 2 * HALF
    mine = pl.ds(x * HALF, HALF)
    inv_packed = jnp.where(low, turn[0, mine, :2 * 2 * HALF], turn[1, mine, :2 * 2 * HALF])

    for t in range(2 * ny):
        scaledT[:, t * wide:(t + 1) * wide] = (startT[t] * inv_root[t:t + 1]).astype(bf16)
    for k in range(2):
        part = tile[...].reshape(2 * ny * wide, ncols)[:, k * ncols // 2:(k + 1) * ncols // 2]
        half_c[k] = dot(scaledT[...], part)
    send(6, "c", lambda p: half_c.at[p], recv_c)
    arrive(6, recv_c)
    both = half_c[core] + recv_c[...]
    mid = both.shape[1] // 2
    both = jnp.concatenate([both[:, :mid], both[:, mid:]], axis=0).T
    send_z[...] = both.reshape(send_z.shape)
    send(7, "z", lambda p: send_z.at[p], recv_z.at[z])
    recv_z[z] = send_z[z]
    arrive(7, recv_z.at[pl.ds(0, nz - 1)])
    panel = functools.reduce(lambda a, b: a + b, [recv_z[i] for i in range(nz)])
    first_packed = panel * inv_packed
    first = unpack(first_packed)

    second_in = unpack(first_packed * inv_packed)
    high = second_in.astype(bf16)
    rest = (second_in - high.astype(f32)).astype(bf16)
    scaled[core, :, z] = jnp.concatenate([high, rest], axis=1).reshape(2, HALF, -1)
    send(8, "z", lambda p: scaled.at[core, :, z], scaled.at[core, :, z])
    gram_sum = pack(full(first.T, first))
    sum_x = all_sum(9, "x", gram_sum, gram_x.at[0])
    arrive(8, scaled.at[0, :, pl.ds(0, nz - 1)])
    send(10, "c", lambda p: scaled.at[core], scaled.at[core])
    sum_y = all_sum(11, "y", sum_x(), gram_y.at[0])
    arrive(10, scaled.at[0])

    lane = lax.broadcasted_iota(jnp.int32, (wide, 4 * HALF), 1) < 2 * HALF

    def product(yy, carry):
        panel_in = scaled[...].reshape(ncols, 4 * HALF)
        parts = []
        for h in range(2):
            out = dot(tile[h, yy], panel_in)
            parts.append(out + pltpu.roll(out, 2 * HALF, 1))
        send_p[yy] = jnp.where(lane, parts[0], parts[1]).reshape(NX, HALF, 4 * HALF)
        return carry
    lax.fori_loop(0, ny, product, 0)
    send(12, "x", lambda p: send_p.at[:, p], recv_px.at[x])
    recv_px[x] = send_p[:, x]
    sum_c = all_sum(13, "c", sum_y(), gram_c.at[0])
    sum_z = all_sum(14, "z", sum_c(), gram_z.at[0])
    arrive(12, recv_px.at[pl.ds(0, NX - 1)])
    send_y[...] = functools.reduce(lambda a, b: a + b, [recv_px[i] for i in range(NX)])
    send(15, "y", lambda p: send_y.at[p], recv_py.at[y])
    recv_py[y] = send_y[y]
    inv_first = inverse_factor(unpack(sum_z()) / total)
    arrive(15, recv_py.at[pl.ds(0, ny - 1)])
    panel = functools.reduce(lambda a, b: a + b, [recv_py[i] for i in range(ny)])
    second = full(unpack(panel * inv_packed), inv_first, ((1,), (1,)))
    basis = full(first, inv_first, ((1,), (1,)))

    whole[y, x] = pack(second)
    n = second.shape[1]
    sums = jnp.concatenate([full(second.T, second), full(basis.T, second)], axis=1)
    sum_x = all_sum(16, "x", sums, gram.at[0])
    send(17, "y", lambda p: whole.at[y, x], whole.at[y, x])
    sum_y = all_sum(18, "y", sum_x(), gram.at[1])
    arrive(17, whole.at[pl.ds(0, ny - 1), 0])
    send(19, "x", lambda p: whole.at[:, x], whole.at[:, x])
    sum_c = all_sum(20, "c", sum_y(), gram.at[2])
    sum_z = all_sum(21, "z", sum_c(), gram.at[3])
    sums = sum_z() / total
    ritz_ref[...] = sums[:, n:]
    last = inverse_factor(sums[:, :n]).T
    none = jnp.zeros_like(last)
    last = jnp.concatenate(
        [jnp.concatenate([last, none], axis=0), jnp.concatenate([none, last], axis=0)], axis=1
    )
    arrive(19, whole.at[:, pl.ds(0, NX - 1)])

    def finish(yy, carry):
        block = full(whole[yy].reshape(wide, 4 * HALF), last)
        for h in range(2):
            out_ref[yy, :, h] = block[:, h * n:(h + 1) * n].reshape(NX, HALF, n)
        return carry
    lax.fori_loop(0, ny, finish, 0)

    for slot, ref in sent:
        pltpu.make_async_copy(ref, ref, send_sem.at[slot]).wait()


def local(points, start_panel):
    nz = lax.axis_size("row") // 2
    ny = lax.axis_size("col") // NX
    rows, vec = start_panel.shape
    width = points.shape[1]
    wide = NX * HALF
    lanes = 2 * vec
    ncols = 4 * nz * HALF
    vmem = pltpu.VMEM
    panels, ritz_sum = pl.pallas_call(
        functools.partial(kernel, nz, ny),
        out_shape=(
            jax.ShapeDtypeStruct((ny, NX, 2, HALF, vec), f32),
            jax.ShapeDtypeStruct((vec, vec), f32),
        ),
        in_specs=[pl.BlockSpec(memory_space=vmem)] * 2,
        out_specs=(pl.BlockSpec(memory_space=vmem),) * 2,
        scratch_shapes=[
            vmem((2, ny, NX, HALF, width), bf16),
            vmem((2, 2, nz, HALF, width), bf16),
            vmem((2, ny, wide, ncols), bf16),
            vmem((2 * ny, vec, wide), f32),
            vmem((vec, 2 * ny * wide), bf16),
            vmem((2 * ny, wide), f32),
            vmem((NX, 2 * ny, wide), f32),
            vmem((ny, 2 * ny, wide), f32),
            vmem((2, wide, wide), f32),
            vmem((2, vec, ncols // 2), f32),
            vmem((vec, ncols // 2), f32),
            vmem((nz, HALF, lanes), f32),
            vmem((nz, HALF, lanes), f32),
            vmem((2, 2, nz, HALF, lanes), bf16),
            vmem((ny, NX, HALF, lanes), f32),
            vmem((NX, ny, HALF, lanes), f32),
            vmem((ny, HALF, lanes), f32),
            vmem((ny, HALF, lanes), f32),
            vmem((4, max(nz, ny, NX), vec, lanes), f32),
            vmem((1, NX, vec // 2, lanes), f32),
            vmem((1, ny, vec // 2, lanes), f32),
            vmem((1, 2, vec // 2, lanes), f32),
            vmem((1, nz, vec // 2, lanes), f32),
            vmem((ny, NX, HALF, lanes), f32),
            pltpu.SemaphoreType.DMA((22,)),
            pltpu.SemaphoreType.DMA((22,)),
        ],
        compiler_params=pltpu.CompilerParams(
            collective_id=0, has_side_effects=True, vmem_limit_bytes=40 << 20
        ),
        name="embed",
    )(points, start_panel.reshape(ny, NX, 2, HALF, vec))
    return panels.reshape(rows, vec), ritz_sum


def solution(mesh):
    in_specs = (P(("row", "col"), None), P("row", None))
    out_specs = (P("row", None), P())
    return jax.shard_map(local, mesh=mesh, in_specs=in_specs, out_specs=out_specs, check_vma=False)
```

```python
import functools
import math

import jax
import jax.numpy as jnp
from jax import lax
from jax.experimental import pallas as pl
from jax.experimental.pallas import tpu as pltpu
from jax.sharding import PartitionSpec as P

MESH = pl.DeviceIdType.MESH
NX = 4
HALF = 32
OWN = 2 * HALF
LANES = 128
SHARPNESS = 5.0
LOG2E = math.log2(math.e)
f32 = jnp.float32
bf16 = jnp.bfloat16


def dot(a, b, contract=((1,), (0,)), precision=None):
    return lax.dot_general(
        a, b, (contract, ((), ())), precision=precision, preferred_element_type=f32
    )


def full(a, b, contract=((1,), (0,))):
    return dot(a, b, contract, lax.Precision.HIGHEST)


def iota(shape, axis):
    return lax.broadcasted_iota(jnp.int32, shape, axis)


def add(parts):
    return functools.reduce(lambda a, b: a + b, parts)


def inverse_factor(gram, width=16):
    n = gram.shape[0]
    eye = jnp.where(iota((n, n), 0) == iota((n, n), 1), 1.0, 0.0).astype(f32)
    mat = jnp.concatenate([gram, eye], axis=1)
    done = []
    for b in range(0, n, width):
        m = n - b
        cols = [jnp.broadcast_to(mat[:, b + j:b + j + 1], (m, 2 * n)) for j in range(width)]
        rows = [mat[j:j + 1] for j in range(width)]
        for j in range(width):
            root = lax.rsqrt(cols[j][j:j + 1])
            cols[j], rows[j] = cols[j] * root, rows[j] * root
            for i in range(j + 1, width):
                factor = cols[j][i:i + 1]
                cols[i], rows[i] = cols[i] - factor * cols[j], rows[i] - factor * rows[j]
        done += rows
        mat = mat[width:]
        for j in range(width if m > width else 0):
            mat = mat - cols[j][width:] * rows[j]
    return jnp.concatenate(done, axis=0)[:, n:]


def pack(mat):
    n = mat.shape[0] // 2
    return jnp.concatenate([mat[:n], mat[n:]], axis=1)


def unpack(mat):
    n = mat.shape[1] // 2
    return jnp.concatenate([mat[:, :n], mat[:, n:]], axis=0)


def kernel(
    nz, ny, points_ref, start_ref, out_ref, ritz_ref,
    startT, rowpts, colpts, tile, partial, scaledT, deg, deg_x, deg_y, turn,
    half_c, recv_c, send_z, recv_z, scaled, send_p, recv_px, send_y, recv_py,
    first_x, first_y, first_c, first_z, gram_x, gram_y, gram_c, gram_z,
    ritz_x, ritz_y, ritz_c, ritz_z, whole,
    load_sem, send_sem, recv_sem, from_y, from_x, part_x,
):
    r, c = lax.axis_index("row"), lax.axis_index("col")
    z, core = r // 2, lax.rem(r, 2)
    y, x = c // NX, lax.rem(c, NX)
    axes = {
        "x": (NX, x, lambda p: (r, y * NX + p)),
        "y": (ny, y, lambda p: (r, p * NX + x)),
        "z": (nz, z, lambda p: (p * 2 + core, c)),
        "c": (2, core, lambda p: (z * 2 + p, c)),
    }
    count = (NX - 1) + (ny - 1) + (nz - 1) + 1
    total = nz * ny * NX * 2 * OWN
    chunk = NX * OWN
    lines = chunk // LANES
    ncols = 2 * nz * OWN
    width = points_ref.shape[1]
    vec = ritz_ref.shape[0]

    load = pltpu.make_async_copy(start_ref, startT, load_sem)
    load.start()
    barrier = pltpu.get_barrier_semaphore()
    for n, me, device in axes.values():
        def greet(i, carry):
            pl.semaphore_signal(
                barrier, inc=1, device_id=device(lax.rem(me + i, n)), device_id_type=MESH
            )
            return carry
        lax.fori_loop(1, n, greet, 0)

    sent = {}
    pending = {}

    def send(slot, axis, src, dst, got, recv=None):
        n, me, device = axes[axis]
        arrival = recv_sem.at[slot] if recv is None else recv

        def one(i, carry):
            p = lax.rem(me + i, n)
            pltpu.make_async_remote_copy(
                src_ref=src(p), dst_ref=dst, send_sem=send_sem.at[slot],
                recv_sem=arrival, device_id=device(p), device_id_type=MESH,
            ).start()
            return carry
        lax.fori_loop(1, n, one, 0)
        sent[slot] = got
        if recv is None:
            pending[slot] = got

    def wait(ref, sem):
        pltpu.make_async_copy(ref, ref, sem).wait()

    def arrive(slot):
        wait(pending.pop(slot), recv_sem.at[slot])

    def drain():
        for slot in list(pending):
            arrive(slot)
        for slot, ref in sent.items():
            wait(ref, send_sem.at[slot])

    def all_sum(slot, axis, value, buf):
        n, me, _ = axes[axis]
        buf[me] = value
        send(slot, axis, lambda p: buf.at[me], buf.at[me], buf.at[pl.ds(0, n - 1)])

        def done():
            arrive(slot)
            return add([buf[i] for i in range(n)])
        return done

    def near(i):
        return lax.rem(y + 2 * ny + (2 * lax.rem(i, 2) - 1) * ((i + 1) // 2), ny)

    shift = SHARPNESS * LOG2E
    pts = points_ref[...]
    unit = pts * lax.rsqrt(jnp.mean(pts * pts, axis=1, keepdims=True) + 1e-06)
    unit = (unit * math.sqrt(shift / width)).astype(bf16)
    rowpts[y, x] = unit
    colpts[core, :, z] = unit.reshape(2, HALF, width)

    pl.semaphore_wait(barrier, count)
    send(0, "y", lambda p: rowpts.at[y, x], rowpts.at[y, x],
         rowpts.at[pl.ds(0, ny - 1), 0], from_y.at[y])
    send(1, "z", lambda p: colpts.at[core, :, z], colpts.at[core, :, z],
         colpts.at[0, :, pl.ds(0, nz - 1)])

    def forward(i, carry):
        yy = near(i)

        @pl.when(i > 0)
        def _():
            wait(rowpts.at[yy, x], from_y.at[yy])
        send(2, "x", lambda p: rowpts.at[yy, x], rowpts.at[yy, x],
             rowpts.at[:, pl.ds(0, NX - 1)], from_x.at[yy])
        return carry
    lax.fori_loop(0, ny, forward, 0)
    sent[2] = rowpts.at[:, pl.ds(0, NX - 1)]
    arrive(1)
    send(3, "c", lambda p: colpts.at[core], colpts.at[core], colpts.at[0])

    def affinity(yy, k):
        left = rowpts[yy].reshape(chunk, width)
        right = colpts[k].reshape(ncols // 2, width)
        value = jnp.exp2(dot(left, right, ((1,), (1,))) - shift)
        tile[k, yy] = value.astype(bf16)
        return add([value[:, j:j + LANES] for j in range(0, ncols // 2, LANES)])

    def near_half(i, carry):
        yy = near(i)
        wait(rowpts.at[yy, pl.ds(0, NX - 1)], from_x.at[yy])
        partial[yy] = affinity(yy, core)
        return carry
    lax.fori_loop(0, ny, near_half, 0)
    arrive(3)

    def far_half(i, carry):
        for b in range(pair):
            yy = pair * i + b
            part = partial[yy] + affinity(yy, 1 - core)
            for h in range(lines):
                deg[pl.ds(yy * lines + h, 1), :] = jnp.sum(
                    part[h * LANES:(h + 1) * LANES].T, axis=0, keepdims=True
                )
        return carry
    pair = 2 if ny % 2 == 0 else 1
    lax.fori_loop(0, ny // pair, far_half, 0)
    degrees = all_sum(4, "x", deg[...], deg_x)()
    degrees = all_sum(5, "y", degrees, deg_y)()
    inv_root = lax.rsqrt(degrees)
    deg[...] = inv_root
    load.wait()
    for t in range(ny * chunk // LANES):
        here = slice(t * LANES, (t + 1) * LANES)
        scaledT[:, here] = (startT[:, here] * inv_root[t:t + 1]).astype(bf16)

    def transposed(k):
        half_c[k] = dot(scaledT[...], tile[k].reshape(ny * chunk, ncols // 2))
    transposed(1 - core)
    send(6, "c", lambda p: half_c.at[p], recv_c, recv_c)
    transposed(core)
    odd = lax.rem(x, 2)
    line = pl.ds(y * lines + x // 2, 1)
    turn[...] = jnp.broadcast_to(deg[line, :], (LANES, LANES)).T
    low = iota((HALF, LANES), 1) < vec
    inv_packed = jnp.where(
        low, turn[pl.ds(odd * OWN, HALF)], turn[pl.ds(odd * OWN + HALF, HALF)]
    )
    arrive(6)
    both = half_c[core] + recv_c[...]
    mid = both.shape[1] // 2
    both = jnp.concatenate([both[:, :mid], both[:, mid:]], axis=0).T
    send_z[...] = both.reshape(send_z.shape)
    send(7, "z", lambda p: send_z.at[p], recv_z.at[z], recv_z.at[pl.ds(0, nz - 1)])
    recv_z[z] = send_z[z]
    arrive(7)
    first_packed = add([recv_z[i] for i in range(nz)]) * inv_packed

    second_in = unpack(first_packed * inv_packed)
    high = second_in.astype(bf16)
    rest = (second_in - high.astype(f32)).astype(bf16)
    scaled[core, :, z] = jnp.concatenate([high, rest], axis=1).reshape(2, HALF, LANES)
    send(8, "z", lambda p: scaled.at[core, :, z], scaled.at[core, :, z],
         scaled.at[0, :, pl.ds(0, nz - 1)])
    first = unpack(first_packed)
    first_sum = all_sum(13, "c", pack(full(first, first, ((0,), (0,)))), first_c)
    first_sum = all_sum(9, "x", first_sum(), first_x)
    first_sum = all_sum(10, "y", first_sum(), first_y)
    arrive(8)
    send(11, "c", lambda p: scaled.at[core], scaled.at[core], scaled.at[0])

    def product(yy, k):
        return dot(tile[k, yy], scaled[k].reshape(ncols // 2, LANES))

    def near_product(i, carry):
        for b in range(pair):
            partial[pair * i + b] = product(pair * i + b, core)
        return carry
    lax.fori_loop(0, ny // pair, near_product, 0)
    arrive(11)
    keep = iota((HALF, LANES), 1) < vec

    def far_product(j, carry):
        yy = near(ny - 1 - j)
        out = partial[yy] + product(yy, 1 - core)
        out = out + pltpu.roll(out, vec, 1)
        for s in range(NX):
            send_p[yy, s] = jnp.where(
                keep, out[s * OWN:s * OWN + HALF], out[s * OWN + HALF:(s + 1) * OWN]
            )
        send(12, "x", lambda p: send_p.at[yy, p], recv_px.at[yy, x],
             send_p.at[:, pl.ds(0, NX - 1)], part_x.at[yy])
        recv_px[yy, x] = send_p[yy, x]
        return carry
    lax.fori_loop(0, ny, far_product, 0)
    sent[12] = send_p.at[:, pl.ds(0, NX - 1)]
    first_sum = all_sum(14, "z", first_sum(), first_z)

    def collect(j, carry):
        yy = near(ny - 1 - j)
        wait(recv_px.at[yy, pl.ds(0, NX - 1)], part_x.at[yy])
        send_y[yy] = add([recv_px[yy, i] for i in range(NX)])

        @pl.when(j < ny - 1)
        def _():
            pltpu.make_async_remote_copy(
                src_ref=send_y.at[yy], dst_ref=recv_py.at[y], send_sem=send_sem.at[15],
                recv_sem=recv_sem.at[15], device_id=(r, yy * NX + x), device_id_type=MESH,
            ).start()
        return carry
    lax.fori_loop(0, ny, collect, 0)
    sent[15] = pending[15] = recv_py.at[pl.ds(0, ny - 1)]
    recv_py[y] = send_y[y]
    inv_first = inverse_factor(unpack(first_sum()) / total)
    basis = full(first, inv_first, ((1,), (1,)))
    arrive(15)
    second_packed = add([recv_py[i] for i in range(ny)]) * inv_packed
    second = full(unpack(second_packed), inv_first, ((1,), (1,)))

    whole[y, x] = pack(second)
    gram = all_sum(16, "x", pack(full(second.T, second)), gram_x)
    ritz = all_sum(17, "x", pack(full(basis.T, second)), ritz_x)
    gram = all_sum(18, "y", gram(), gram_y)
    ritz = all_sum(19, "y", ritz(), ritz_y)
    send(20, "y", lambda p: whole.at[y, x], whole.at[y, x], whole.at[pl.ds(0, ny - 1), 0])
    gram = all_sum(21, "c", gram(), gram_c)
    gram = all_sum(22, "z", gram(), gram_z)
    ritz = all_sum(23, "c", ritz(), ritz_c)
    ritz = all_sum(24, "z", ritz(), ritz_z)
    arrive(20)
    send(25, "x", lambda p: whole.at[:, x], whole.at[:, x], whole.at[:, pl.ds(0, NX - 1)])
    gram = unpack(gram()) / total
    last = inverse_factor(gram)
    last = jnp.concatenate([last, jnp.zeros_like(last)], axis=1)
    arrive(25)

    group = 4 if ny % 4 == 0 else 1

    def finish(t, carry):
        parts = []
        for s in range(group * NX):
            block = whole[t * group + s // NX, s % NX]
            parts += [block, pltpu.roll(block, vec, 1)]
        here = pl.ds(pl.multiple_of(t * group * chunk, group * chunk), group * chunk)
        out_ref[:, here] = full(last, jnp.concatenate(parts, axis=0), ((1,), (1,)))
        return carry
    lax.fori_loop(0, ny // group, finish, 0)
    ritz_ref[...] = unpack(ritz()) / total
    drain()


def local(points, start_panel):
    nz = lax.axis_size("row") // 2
    ny = lax.axis_size("col") // NX
    rows, vec = start_panel.shape
    width = points.shape[1]
    chunk = NX * OWN
    lines = rows // LANES
    ncols = 2 * nz * OWN
    vmem = pltpu.VMEM
    dma = pltpu.SemaphoreType.DMA
    sums = [vmem((n, vec // 2, 2 * vec), f32) for n in (NX, ny, 2, nz)]
    panels, ritz_sum = pl.pallas_call(
        functools.partial(kernel, nz, ny),
        out_shape=(
            jax.ShapeDtypeStruct((vec, rows), f32),
            jax.ShapeDtypeStruct((vec, vec), f32),
        ),
        in_specs=[pl.BlockSpec(memory_space=vmem), pl.BlockSpec(memory_space=pl.ANY)],
        out_specs=(pl.BlockSpec(memory_space=vmem),) * 2,
        scratch_shapes=[
            vmem((vec, rows), f32),
            vmem((ny, NX, OWN, width), bf16),
            vmem((2, 2, nz, HALF, width), bf16),
            vmem((2, ny, chunk, ncols // 2), bf16),
            vmem((ny, chunk, LANES), f32),
            vmem((vec, rows), bf16),
            vmem((lines, LANES), f32),
            vmem((NX, lines, LANES), f32),
            vmem((ny, lines, LANES), f32),
            vmem((LANES, LANES), f32),
            vmem((2, vec, ncols // 2), f32),
            vmem((vec, ncols // 2), f32),
            vmem((nz, HALF, LANES), f32),
            vmem((nz, HALF, LANES), f32),
            vmem((2, 2, nz, HALF, LANES), bf16),
            vmem((ny, NX, HALF, LANES), f32),
            vmem((ny, NX, HALF, LANES), f32),
            vmem((ny, HALF, LANES), f32),
            vmem((ny, HALF, LANES), f32),
            *sums, *sums, *sums,
            vmem((ny, NX, HALF, LANES), f32),
            dma, dma((26,)), dma((26,)), dma((ny,)), dma((ny,)), dma((ny,)),
        ],
        compiler_params=pltpu.CompilerParams(
            collective_id=0, has_side_effects=True, vmem_limit_bytes=40 << 20
        ),
        name="embed",
    )(points, start_panel.T)
    return panels.T, ritz_sum


def solution(mesh):
    in_specs = (P(("row", "col"), None), P("row", None))
    out_specs = (P("row", None), P())
    return jax.shard_map(local, mesh=mesh, in_specs=in_specs, out_specs=out_specs, check_vma=False)
```

```python
import functools
import math

import jax
import jax.numpy as jnp
from jax import lax
from jax.experimental import pallas as pl
from jax.experimental.pallas import tpu as pltpu
from jax.sharding import PartitionSpec as P

MESH = pl.DeviceIdType.MESH
NX = 4
HALF = 32
OWN = 2 * HALF
LANES = 128
SHARPNESS = 5.0
LOG2E = math.log2(math.e)
f32 = jnp.float32
bf16 = jnp.bfloat16


def dot(a, b, contract=((1,), (0,)), precision=None):
    return lax.dot_general(
        a, b, (contract, ((), ())), precision=precision, preferred_element_type=f32
    )


def full(a, b, contract=((1,), (0,))):
    return dot(a, b, contract, lax.Precision.HIGHEST)


def iota(shape, axis):
    return lax.broadcasted_iota(jnp.int32, shape, axis)


def add(parts):
    return functools.reduce(lambda a, b: a + b, parts)


def inverse_factor(gram, width=16):
    n = gram.shape[0]
    eye = jnp.where(iota((n, n), 0) == iota((n, n), 1), 1.0, 0.0).astype(f32)
    mat = jnp.concatenate([gram, eye], axis=1)
    done = []
    for b in range(0, n, width):
        m = n - b
        cols = [jnp.broadcast_to(mat[:, b + j:b + j + 1], (m, 2 * n)) for j in range(width)]
        rows = [mat[j:j + 1] for j in range(width)]
        for j in range(width):
            root = lax.rsqrt(cols[j][j:j + 1])
            cols[j], rows[j] = cols[j] * root, rows[j] * root
            for i in range(j + 1, width):
                factor = cols[j][i:i + 1]
                cols[i], rows[i] = cols[i] - factor * cols[j], rows[i] - factor * rows[j]
        done += rows
        mat = mat[width:]
        for j in range(width if m > width else 0):
            mat = mat - cols[j][width:] * rows[j]
    return jnp.concatenate(done, axis=0)[:, n:]


def pack(mat):
    n = mat.shape[0] // 2
    return jnp.concatenate([mat[:n], mat[n:]], axis=1)


def unpack(mat):
    n = mat.shape[1] // 2
    return jnp.concatenate([mat[:, :n], mat[:, n:]], axis=0)


def kernel(
    nz, ny, points_ref, start_ref, out_ref, ritz_ref,
    pointsV, startT, rowpts, colpts, tile, partial, scaledT, deg, deg_x, deg_y, turn,
    half_c, recv_c, send_z, recv_z, scaled, send_p, recv_px, send_y, recv_py,
    first_x, first_y, first_z, gram_x, gram_y, gram_z, ritz_x, ritz_y, ritz_z, whole,
    load_sem, points_sem, send_sem, recv_sem, from_y, from_x, part_x,
):
    r, c = lax.axis_index("row"), lax.axis_index("col")
    z, core = r // 2, lax.rem(r, 2)
    y, x = c // NX, lax.rem(c, NX)
    axes = {
        "x": (NX, x, lambda p: (r, y * NX + p)),
        "y": (ny, y, lambda p: (r, p * NX + x)),
        "z": (nz, z, lambda p: (p * 2 + core, c)),
        "c": (2, core, lambda p: (z * 2 + p, c)),
        "xc": (2 * NX, x * 2 + core, lambda p: (z * 2 + lax.rem(p, 2), y * NX + p // 2)),
    }
    met = ("xc", "y", "z")
    count = sum(axes[axis][0] - 1 for axis in met)
    total = nz * ny * NX * 2 * OWN
    chunk = NX * OWN
    lines = chunk // LANES
    ncols = 2 * nz * OWN
    width = points_ref.shape[1]
    vec = ritz_ref.shape[0]

    load_points = pltpu.make_async_copy(points_ref, pointsV, points_sem)
    load_points.start()
    load = pltpu.make_async_copy(start_ref, startT, load_sem)
    load.start()
    barrier = pltpu.get_barrier_semaphore()
    for axis in met:
        n, me, device = axes[axis]

        def greet(i, carry):
            pl.semaphore_signal(
                barrier, inc=1, device_id=device(lax.rem(me + i, n)), device_id_type=MESH
            )
            return carry
        lax.fori_loop(1, n, greet, 0)

    sent = {}
    pending = {}

    def send(slot, axis, src, dst, got, recv=None):
        n, me, device = axes[axis]
        arrival = recv_sem.at[slot] if recv is None else recv

        def one(i, carry):
            p = lax.rem(me + i, n)
            pltpu.make_async_remote_copy(
                src_ref=src(p), dst_ref=dst, send_sem=send_sem.at[slot],
                recv_sem=arrival, device_id=device(p), device_id_type=MESH,
            ).start()
            return carry
        lax.fori_loop(1, n, one, 0)
        sent[slot] = got
        if recv is None:
            pending[slot] = got

    def wait(ref, sem):
        pltpu.make_async_copy(ref, ref, sem).wait()

    def arrive(slot):
        wait(pending.pop(slot), recv_sem.at[slot])

    def drain():
        for slot in list(pending):
            arrive(slot)
        for slot, ref in sent.items():
            wait(ref, send_sem.at[slot])

    def all_sum(slot, axis, value, buf):
        n, me, _ = axes[axis]
        buf[me] = value
        send(slot, axis, lambda p: buf.at[me], buf.at[me], buf.at[pl.ds(0, n - 1)])

        def done():
            arrive(slot)
            return add([buf[i] for i in range(n)])
        return done

    def near(i):
        return lax.rem(y + 2 * ny + (2 * lax.rem(i, 2) - 1) * ((i + 1) // 2), ny)

    shift = SHARPNESS * LOG2E
    load_points.wait()
    pts = pointsV[...]
    unit = pts * lax.rsqrt(jnp.mean(pts * pts, axis=1, keepdims=True) + 1e-06)
    unit = (unit * math.sqrt(shift / width)).astype(bf16)
    rowpts[y, x] = unit
    colpts[core, :, z] = unit.reshape(2, HALF, width)

    pl.semaphore_wait(barrier, count)
    send(0, "y", lambda p: rowpts.at[y, x], rowpts.at[y, x],
         rowpts.at[pl.ds(0, ny - 1), 0], from_y.at[y])
    send(1, "z", lambda p: colpts.at[core, :, z], colpts.at[core, :, z],
         colpts.at[0, :, pl.ds(0, nz - 1)])

    def forward(i, carry):
        yy = near(i)

        @pl.when(i > 0)
        def _():
            wait(rowpts.at[yy, x], from_y.at[yy])
        send(2, "x", lambda p: rowpts.at[yy, x], rowpts.at[yy, x],
             rowpts.at[:, pl.ds(0, NX - 1)], from_x.at[yy])
        return carry
    lax.fori_loop(0, ny, forward, 0)
    sent[2] = rowpts.at[:, pl.ds(0, NX - 1)]
    arrive(1)
    send(3, "c", lambda p: colpts.at[core], colpts.at[core], colpts.at[0])

    def affinity(yy, k):
        left = rowpts[yy].reshape(chunk, width)
        right = colpts[k].reshape(ncols // 2, width)
        value = jnp.exp2(dot(left, right, ((1,), (1,))) - shift)
        tile[k, yy] = value.astype(bf16)
        return add([value[:, j:j + LANES] for j in range(0, ncols // 2, LANES)])

    def line_sums(yy, part):
        for h in range(lines):
            deg[pl.ds(yy * lines + h, 1), :] = jnp.sum(
                part[h * LANES:(h + 1) * LANES].T, axis=0, keepdims=True
            )

    def chunk_here(i):
        yy = near(i)
        wait(rowpts.at[yy, pl.ds(0, NX - 1)], from_x.at[yy])
        return yy

    def near_half(i, carry):
        yy = chunk_here(i)
        partial[yy] = affinity(yy, core)
        return carry

    def far_half(i, carry):
        yy = near(i)
        line_sums(yy, partial[yy] + affinity(yy, 1 - core))
        return carry

    def both_halves(i, carry):
        yy = chunk_here(i)
        line_sums(yy, affinity(yy, core) + affinity(yy, 1 - core))
        return carry
    early = ny - ny // 4
    lax.fori_loop(0, early, near_half, 0)
    arrive(3)
    lax.fori_loop(0, early, far_half, 0)
    lax.fori_loop(early, ny, both_halves, 0)
    degrees = all_sum(4, "x", deg[...], deg_x)()
    degrees = all_sum(5, "y", degrees, deg_y)()
    inv_root = lax.rsqrt(degrees)
    deg[...] = inv_root
    load.wait()
    for t in range(ny * chunk // LANES):
        here = slice(t * LANES, (t + 1) * LANES)
        scaledT[:, here] = (startT[:, here] * inv_root[t:t + 1]).astype(bf16)

    def transposed(k):
        half_c[k] = dot(scaledT[...], tile[k].reshape(ny * chunk, ncols // 2))
    transposed(1 - core)
    send(6, "c", lambda p: half_c.at[p], recv_c, recv_c)
    transposed(core)
    odd = lax.rem(x, 2)
    line = pl.ds(y * lines + x // 2, 1)
    turn[...] = jnp.broadcast_to(deg[line, :], (LANES, LANES)).T
    low = iota((HALF, LANES), 1) < vec
    inv_packed = jnp.where(
        low, turn[pl.ds(odd * OWN, HALF)], turn[pl.ds(odd * OWN + HALF, HALF)]
    )
    arrive(6)
    both = half_c[core] + recv_c[...]
    mid = both.shape[1] // 2
    both = jnp.concatenate([both[:, :mid], both[:, mid:]], axis=0).T
    send_z[...] = both.reshape(send_z.shape)
    send(7, "z", lambda p: send_z.at[p], recv_z.at[z], recv_z.at[pl.ds(0, nz - 1)])
    recv_z[z] = send_z[z]
    arrive(7)
    first_packed = add([recv_z[i] for i in range(nz)]) * inv_packed

    second_in = unpack(first_packed * inv_packed)
    high = second_in.astype(bf16)
    rest = (second_in - high.astype(f32)).astype(bf16)
    scaled[core, :, z] = jnp.concatenate([high, rest], axis=1).reshape(2, HALF, LANES)
    send(8, "z", lambda p: scaled.at[core, :, z], scaled.at[core, :, z],
         scaled.at[0, :, pl.ds(0, nz - 1)])
    first = unpack(first_packed)
    first_sum = all_sum(9, "xc", pack(full(first, first, ((0,), (0,)))), first_x)
    first_sum = all_sum(10, "y", first_sum(), first_y)
    arrive(8)
    send(11, "c", lambda p: scaled.at[core], scaled.at[core], scaled.at[0])

    pair = 2 if ny % 2 == 0 else 1

    def product(yy, k):
        return dot(tile[k, yy], scaled[k].reshape(ncols // 2, LANES))

    def near_product(i, carry):
        for b in range(pair):
            partial[pair * i + b] = product(pair * i + b, core)
        return carry
    lax.fori_loop(0, ny // pair, near_product, 0)
    arrive(11)
    keep = iota((HALF, LANES), 1) < vec

    def far_product(j, carry):
        yy = near(ny - 1 - j)
        out = partial[yy] + product(yy, 1 - core)
        out = out + pltpu.roll(out, vec, 1)
        for s in range(NX):
            send_p[yy, s] = jnp.where(
                keep, out[s * OWN:s * OWN + HALF], out[s * OWN + HALF:(s + 1) * OWN]
            )
        send(12, "x", lambda p: send_p.at[yy, p], recv_px.at[yy, x],
             send_p.at[:, pl.ds(0, NX - 1)], part_x.at[yy])
        recv_px[yy, x] = send_p[yy, x]
        return carry
    lax.fori_loop(0, ny, far_product, 0)
    sent[12] = send_p.at[:, pl.ds(0, NX - 1)]
    first_sum = all_sum(14, "z", first_sum(), first_z)

    def collect(j, carry):
        yy = near(ny - 1 - j)
        wait(recv_px.at[yy, pl.ds(0, NX - 1)], part_x.at[yy])
        send_y[yy] = add([recv_px[yy, i] for i in range(NX)])

        @pl.when(j < ny - 1)
        def _():
            pltpu.make_async_remote_copy(
                src_ref=send_y.at[yy], dst_ref=recv_py.at[y], send_sem=send_sem.at[15],
                recv_sem=recv_sem.at[15], device_id=(r, yy * NX + x), device_id_type=MESH,
            ).start()
        return carry
    lax.fori_loop(0, ny, collect, 0)
    sent[15] = pending[15] = recv_py.at[pl.ds(0, ny - 1)]
    recv_py[y] = send_y[y]
    inv_first = inverse_factor(unpack(first_sum()) / total)
    basis = full(first, inv_first, ((1,), (1,)))
    arrive(15)
    second_packed = add([recv_py[i] for i in range(ny)]) * inv_packed
    second = full(unpack(second_packed), inv_first, ((1,), (1,)))

    whole[y, x] = pack(second)
    send(20, "y", lambda p: whole.at[y, x], whole.at[y, x], whole.at[pl.ds(0, ny - 1), 0])
    gram = all_sum(16, "xc", pack(full(second, second, ((0,), (0,)))), gram_x)
    ritz = all_sum(17, "z", pack(full(basis, second, ((0,), (0,)))), ritz_z)
    gram = all_sum(18, "y", gram(), gram_y)
    arrive(20)
    send(25, "x", lambda p: whole.at[:, x], whole.at[:, x], whole.at[:, pl.ds(0, NX - 1)])
    ritz = all_sum(23, "xc", ritz(), ritz_x)
    gram = all_sum(22, "z", gram(), gram_z)
    ritz = all_sum(19, "y", ritz(), ritz_y)
    gram = unpack(gram()) / total
    last = inverse_factor(gram)
    last = jnp.concatenate([last, jnp.zeros_like(last)], axis=1)
    arrive(25)

    group = 4 if ny % 4 == 0 else 1

    def finish(t, carry):
        parts = []
        for s in range(group * NX):
            block = whole[t * group + s // NX, s % NX]
            parts += [block, pltpu.roll(block, vec, 1)]
        here = pl.ds(pl.multiple_of(t * group * chunk, group * chunk), group * chunk)
        out_ref[:, here] = full(last, jnp.concatenate(parts, axis=0), ((1,), (1,)))
        return carry
    lax.fori_loop(0, ny // group, finish, 0)
    ritz_ref[...] = unpack(ritz()) / total
    drain()


def local(points, start_panel):
    nz = lax.axis_size("row") // 2
    ny = lax.axis_size("col") // NX
    rows, vec = start_panel.shape
    width = points.shape[1]
    chunk = NX * OWN
    lines = rows // LANES
    ncols = 2 * nz * OWN
    vmem = pltpu.VMEM
    dma = pltpu.SemaphoreType.DMA
    sums = [vmem((n, vec // 2, 2 * vec), f32) for n in (2 * NX, ny, nz)]
    panels, ritz_sum = pl.pallas_call(
        functools.partial(kernel, nz, ny),
        out_shape=(
            jax.ShapeDtypeStruct((vec, rows), f32),
            jax.ShapeDtypeStruct((vec, vec), f32),
        ),
        in_specs=[pl.BlockSpec(memory_space=pl.ANY)] * 2,
        out_specs=(pl.BlockSpec(memory_space=vmem),) * 2,
        scratch_shapes=[
            vmem(points.shape, f32),
            vmem((vec, rows), f32),
            vmem((ny, NX, OWN, width), bf16),
            vmem((2, 2, nz, HALF, width), bf16),
            vmem((2, ny, chunk, ncols // 2), bf16),
            vmem((ny, chunk, LANES), f32),
            vmem((vec, rows), bf16),
            vmem((lines, LANES), f32),
            vmem((NX, lines, LANES), f32),
            vmem((ny, lines, LANES), f32),
            vmem((LANES, LANES), f32),
            vmem((2, vec, ncols // 2), f32),
            vmem((vec, ncols // 2), f32),
            vmem((nz, HALF, LANES), f32),
            vmem((nz, HALF, LANES), f32),
            vmem((2, 2, nz, HALF, LANES), bf16),
            vmem((ny, NX, HALF, LANES), f32),
            vmem((ny, NX, HALF, LANES), f32),
            vmem((ny, HALF, LANES), f32),
            vmem((ny, HALF, LANES), f32),
            *sums, *sums, *sums,
            vmem((ny, NX, HALF, LANES), f32),
            dma, dma, dma((26,)), dma((26,)), dma((ny,)), dma((ny,)), dma((ny,)),
        ],
        compiler_params=pltpu.CompilerParams(
            collective_id=0, has_side_effects=True, vmem_limit_bytes=60 << 20
        ),
        name="embed",
    )(points, start_panel.T)
    return panels.T, ritz_sum


def solution(mesh):
    in_specs = (P(("row", "col"), None), P("row", None))
    out_specs = (P("row", None), P())
    return jax.shard_map(local, mesh=mesh, in_specs=in_specs, out_specs=out_specs, check_vma=False)
```

```python
import functools
import math

import jax
import jax.numpy as jnp
from jax import lax
from jax.experimental import pallas as pl
from jax.experimental.pallas import tpu as pltpu
from jax.sharding import PartitionSpec as P

MESH = pl.DeviceIdType.MESH
NX = 4
HALF = 32
OWN = 2 * HALF
LANES = 128
SHARPNESS = 5.0
LOG2E = math.log2(math.e)
f32 = jnp.float32
bf16 = jnp.bfloat16


def dot(a, b, contract=((1,), (0,)), precision=None):
    return lax.dot_general(
        a, b, (contract, ((), ())), precision=precision, preferred_element_type=f32
    )


def full(a, b, contract=((1,), (0,))):
    return dot(a, b, contract, lax.Precision.HIGHEST)


def iota(shape, axis):
    return lax.broadcasted_iota(jnp.int32, shape, axis)


def add(parts):
    return functools.reduce(lambda a, b: a + b, parts)


def inverse_factor(gram, width=16):
    n = gram.shape[0]
    eye = jnp.where(iota((n, n), 0) == iota((n, n), 1), 1.0, 0.0).astype(f32)
    mat = jnp.concatenate([gram, eye], axis=1)
    done = []
    for b in range(0, n, width):
        m = n - b
        cols = [jnp.broadcast_to(mat[:, b + j:b + j + 1], (m, 2 * n)) for j in range(width)]
        rows = [mat[j:j + 1] for j in range(width)]
        for j in range(width):
            root = lax.rsqrt(cols[j][j:j + 1])
            cols[j], rows[j] = cols[j] * root, rows[j] * root
            for i in range(j + 1, width):
                factor = cols[j][i:i + 1]
                cols[i], rows[i] = cols[i] - factor * cols[j], rows[i] - factor * rows[j]
        done += rows
        mat = mat[width:]
        for j in range(width if m > width else 0):
            mat = mat - cols[j][width:] * rows[j]
    return jnp.concatenate(done, axis=0)[:, n:]


def pack(mat):
    n = mat.shape[0] // 2
    return jnp.concatenate([mat[:n], mat[n:]], axis=1)


def unpack(mat):
    n = mat.shape[1] // 2
    return jnp.concatenate([mat[:, :n], mat[:, n:]], axis=0)


def split(value, parts):
    out = []
    for _ in range(parts):
        out.append(value.astype(bf16))
        value = value - out[-1].astype(f32)
    return out


def kernel(
    nz, ny, points_ref, start_ref, out_ref, ritz_ref,
    points, pair_rows, pair_cols, start, rowpts, colpts, tile, colsum, deg, deg_c, deg_z, inv_col,
    panel, send_p, recv_px, send_y, recv_py, scaled, total_c, half_c, recv_c, send_z, recv_z,
    first_x, first_y, first_z, gram_x, gram_y, gram_z, ritz_x, ritz_y, ritz_z, whole, stack,
    load_sem, points_sem, send_sem, recv_sem, from_y, from_x, part_x, again_y, again_x,
):
    r, c = lax.axis_index("row"), lax.axis_index("col")
    z, core = r // 2, lax.rem(r, 2)
    y, x = c // NX, lax.rem(c, NX)
    axes = {
        "x": (NX, x, lambda p: (r, y * NX + p)),
        "y": (ny, y, lambda p: (r, p * NX + x)),
        "z": (nz, z, lambda p: (p * 2 + core, c)),
        "c": (2, core, lambda p: (z * 2 + p, c)),
        "xc": (2 * NX, x * 2 + core, lambda p: (z * 2 + lax.rem(p, 2), y * NX + p // 2)),
    }
    met = ("xc", "y", "z")
    count = sum(axes[axis][0] - 1 for axis in met)
    chunk = NX * OWN
    mid = nz * HALF
    ncols = 2 * mid
    total = 2 * ny * chunk * nz
    width = points_ref.shape[1]
    vec = ritz_ref.shape[0]

    load_points = pltpu.make_async_copy(points_ref, points, points_sem)
    load_points.start()
    here = pl.ds(pl.multiple_of(c // 2 * LANES, LANES), LANES)
    load = pltpu.make_async_copy(start_ref.at[:, here], pair_cols, load_sem)
    load.start()
    barrier = pltpu.get_barrier_semaphore()
    for axis in met:
        n, me, device = axes[axis]

        def greet(i, carry):
            pl.semaphore_signal(
                barrier, inc=1, device_id=device(lax.rem(me + i, n)), device_id_type=MESH
            )
            return carry
        lax.fori_loop(1, n, greet, 0)

    sent = {}
    pending = {}

    def send(slot, axis, src, dst, got, recv=None):
        n, me, device = axes[axis]
        arrival = recv_sem.at[slot] if recv is None else recv

        def one(i, carry):
            p = lax.rem(me + i, n)
            pltpu.make_async_remote_copy(
                src_ref=src(p), dst_ref=dst, send_sem=send_sem.at[slot],
                recv_sem=arrival, device_id=device(p), device_id_type=MESH,
            ).start()
            return carry
        lax.fori_loop(1, n, one, 0)
        sent[slot] = got
        if recv is None:
            pending[slot] = got

    def wait(ref, sem):
        pltpu.make_async_copy(ref, ref, sem).wait()

    def arrive(slot):
        wait(pending.pop(slot), recv_sem.at[slot])

    def drain():
        for slot in list(pending):
            arrive(slot)
        for slot, ref in sent.items():
            wait(ref, send_sem.at[slot])

    def all_sum(slot, axis, value, buf):
        n, me, _ = axes[axis]
        buf[me] = value
        send(slot, axis, lambda p: buf.at[me], buf.at[me], buf.at[pl.ds(0, n - 1)])

        def done():
            arrive(slot)
            return add([buf[i] for i in range(n)])
        return done

    def near(i):
        return lax.rem(y + 2 * ny + (2 * lax.rem(i, 2) - 1) * ((i + 1) // 2), ny)

    def spread(slot, buf, sems_y, sems_x):
        send(slot, "y", lambda p: buf.at[y, x], buf.at[y, x],
             buf.at[pl.ds(0, ny - 1), 0], sems_y.at[y])

        def forward(i, carry):
            yy = near(i)

            @pl.when(i > 0)
            def _():
                wait(buf.at[yy, x], sems_y.at[yy])
            send(slot + 1, "x", lambda p: buf.at[yy, x], buf.at[yy, x],
                 buf.at[:, pl.ds(0, NX - 1)], sems_x.at[yy])
            return carry

        def on():
            lax.fori_loop(0, ny, forward, 0)
            sent[slot + 1] = buf.at[:, pl.ds(0, NX - 1)]
        return on

    shift = SHARPNESS * LOG2E
    load_points.wait()
    pts = points[...]
    unit = pts * lax.rsqrt(jnp.mean(pts * pts, axis=1, keepdims=True) + 1e-06)
    unit = (unit * math.sqrt(shift / width)).astype(bf16)
    rowpts[y, x] = unit
    colpts[core, :, z] = unit.reshape(2, HALF, width)
    colsum[...] = jnp.zeros_like(colsum)

    load.wait()
    pair_rows[...] = pair_cols[...].T
    odd = lax.rem(x, 2) * OWN
    start[core, z] = jnp.concatenate(
        [pair_rows[pl.ds(odd, HALF)], pair_rows[pl.ds(odd + HALF, HALF)]], axis=1
    )

    pl.semaphore_wait(barrier, count)
    rows_on = spread(0, rowpts, from_y, from_x)
    send(2, "z", lambda p: colpts.at[core, :, z], colpts.at[core, :, z],
         colpts.at[0, :, pl.ds(0, nz - 1)])
    rows_on()
    arrive(2)
    send(3, "c", lambda p: colpts.at[core], colpts.at[core], colpts.at[0])
    send(4, "z", lambda p: start.at[core, z], start.at[core, z], start.at[0, pl.ds(0, nz - 1)])

    def affinity(yy, k):
        left = rowpts[yy].reshape(chunk, width)
        right = colpts[k].reshape(ncols, width)
        value = jnp.exp2(dot(left, right, ((1,), (1,))) - shift)
        tile[k, yy] = value.astype(bf16)
        colsum[k] = colsum[k] + jnp.sum(value.reshape(chunk // 8, 8, ncols), axis=0)

    def chunk_here(i):
        yy = near(i)
        wait(rowpts.at[yy, pl.ds(0, NX - 1)], from_x.at[yy])
        return yy

    def near_half(i, carry):
        affinity(chunk_here(i), core)
        return carry

    def far_half(i, carry):
        affinity(near(i), 1 - core)
        return carry

    def both_halves(i, carry):
        yy = chunk_here(i)
        affinity(yy, core)
        affinity(yy, 1 - core)
        return carry
    early = ny - ny // 4
    lax.fori_loop(0, early, near_half, 0)
    arrive(3)
    lax.fori_loop(0, early, far_half, 0)
    lax.fori_loop(early, ny, both_halves, 0)
    lines = ncols // LANES
    for k in range(2):
        line = jnp.sum(colsum[k], axis=0, keepdims=True)
        for j in range(lines):
            deg[k * lines + j:k * lines + j + 1] = line[:, j * LANES:(j + 1) * LANES]

    degrees = all_sum(5, "c", deg[...], deg_c)
    arrive(4)
    send(6, "c", lambda p: start.at[core], start.at[core], start.at[0])
    degrees = all_sum(7, "z", degrees(), deg_z)
    arrive(6)
    inv_root = lax.rsqrt(degrees())
    for k in range(2):
        for j in range(lines):
            row = inv_root[k * lines + j:k * lines + j + 1]
            inv_col[k, j * LANES:(j + 1) * LANES] = jnp.broadcast_to(row, (LANES, LANES)).T
    low = iota((mid, LANES), 1) < vec
    for k in range(2):
        one = start[k].reshape(mid, LANES)
        two = pltpu.roll(one, vec, 1)
        panel[k, :mid] = (jnp.where(low, one, two) * inv_col[k, :mid]).astype(bf16)
        panel[k, mid:] = (jnp.where(low, two, one) * inv_col[k, mid:]).astype(bf16)
    keep = iota((HALF, LANES), 1) < vec
    inv_packed = jnp.where(
        keep, inv_col[core, pl.ds(z * HALF, HALF)], inv_col[core, pl.ds(mid + z * HALF, HALF)]
    )

    def product(j, carry):
        yy = near(ny - 1 - j)
        out = dot(tile[0, yy], panel[0]) + dot(tile[1, yy], panel[1])
        for s in range(NX):
            send_p[yy, s] = jnp.where(
                keep, out[s * OWN:s * OWN + HALF], out[s * OWN + HALF:(s + 1) * OWN]
            ).astype(bf16)
        send(8, "x", lambda p: send_p.at[yy, p], recv_px.at[yy, x],
             send_p.at[:, pl.ds(0, NX - 1)], part_x.at[yy])
        recv_px[yy, x] = send_p[yy, x]
        return carry
    lax.fori_loop(0, ny, product, 0)
    sent[8] = send_p.at[:, pl.ds(0, NX - 1)]

    def collect(j, carry):
        yy = near(ny - 1 - j)
        wait(recv_px.at[yy, pl.ds(0, NX - 1)], part_x.at[yy])
        send_y[yy] = add([recv_px[yy, i].astype(f32) for i in range(NX)])

        @pl.when(j < ny - 1)
        def _():
            pltpu.make_async_remote_copy(
                src_ref=send_y.at[yy], dst_ref=recv_py.at[y], send_sem=send_sem.at[9],
                recv_sem=recv_sem.at[9], device_id=(r, yy * NX + x), device_id_type=MESH,
            ).start()
        return carry
    lax.fori_loop(0, ny, collect, 0)
    sent[9] = pending[9] = recv_py.at[pl.ds(0, ny - 1)]
    recv_py[y] = send_y[y]
    arrive(9)
    first_packed = add([recv_py[i] for i in range(ny)]) * inv_packed

    scaled[y, x] = jnp.concatenate(split(unpack(first_packed * inv_packed), 2), axis=1)
    scaled_on = spread(10, scaled, again_y, again_x)
    first = unpack(first_packed)
    first_sum = all_sum(12, "z", pack(full(first, first, ((0,), (0,)))), first_z)
    scaled_on()
    first_sum = all_sum(13, "xc", first_sum(), first_x)

    def transposed(i, k):
        yy = near(i)
        left = scaled[yy].reshape(chunk, 2 * vec).T
        return dot(left, tile[k, yy])

    def chunk_there(i):
        yy = near(i)
        wait(scaled.at[yy, pl.ds(0, NX - 1)], again_x.at[yy])

    def gather(i, carry):
        chunk_there(i)
        for k in range(2):
            total_c[k] = total_c[k] + transposed(i, k)
        return carry
    chunk_there(0)
    for k in range(2):
        total_c[k] = transposed(0, k)
    lax.fori_loop(1, ny, gather, 0)
    for k in range(2):
        half_c[k] = total_c[k, :vec] + total_c[k, vec:]
    send(14, "c", lambda p: half_c.at[p], recv_c, recv_c)
    first_sum = all_sum(15, "y", first_sum(), first_y)
    arrive(14)
    both = half_c[core] + recv_c[...]
    both = jnp.concatenate([both[:, :mid], both[:, mid:]], axis=0).T
    send_z[...] = both.reshape(send_z.shape)
    send(16, "z", lambda p: send_z.at[p], recv_z.at[z], recv_z.at[pl.ds(0, nz - 1)])
    recv_z[z] = send_z[z]
    inv_first = inverse_factor(unpack(first_sum()) / total)
    basis = full(first, inv_first, ((1,), (1,)))
    arrive(16)
    second_packed = add([recv_z[i] for i in range(nz)]) * inv_packed
    second = full(unpack(second_packed), inv_first, ((1,), (1,)))

    whole[y, x] = pack(second)
    send(20, "y", lambda p: whole.at[y, x], whole.at[y, x], whole.at[pl.ds(0, ny - 1), 0])
    gram = all_sum(17, "xc", pack(full(second, second, ((0,), (0,)))), gram_x)
    ritz = all_sum(18, "z", pack(full(basis, second, ((0,), (0,)))), ritz_z)
    gram = all_sum(19, "y", gram(), gram_y)
    arrive(20)
    send(21, "x", lambda p: whole.at[:, x], whole.at[:, x], whole.at[:, pl.ds(0, NX - 1)])
    ritz = all_sum(22, "xc", ritz(), ritz_x)
    gram = all_sum(23, "z", gram(), gram_z)
    ritz = all_sum(24, "y", ritz(), ritz_y)
    arrive(21)

    def prepare(yy, carry):
        parts = []
        for s in range(NX):
            block = whole[yy, s]
            parts += [block, pltpu.roll(block, vec, 1)]
        high, middle, low = split(jnp.concatenate(parts, axis=0).T[:vec], 3)
        columns = pl.ds(pl.multiple_of(yy * chunk, chunk), chunk)
        stack[:, columns] = jnp.concatenate([high, middle, low, high, middle, high], axis=0)
        return carry
    lax.fori_loop(0, ny, prepare, 0)
    last = inverse_factor(unpack(gram()) / total)
    high, middle, low = [part.astype(f32) for part in split(last, 3)]
    last = jnp.concatenate([high, high, high, middle, middle, low], axis=1).astype(bf16)
    block = min(4 * chunk, ny * chunk)
    for j in range(0, ny * chunk, block):
        out_ref[:, j:j + block] = dot(last, stack[:, j:j + block])
    ritz_ref[...] = unpack(ritz()) / total
    drain()


def hand_over(panels_ref, ritz_ref, panels_out, ritz_out, sems):
    copies = [
        pltpu.make_async_copy(panels_ref, panels_out, sems.at[0]),
        pltpu.make_async_copy(ritz_ref, ritz_out, sems.at[1]),
    ]
    for copy in copies:
        copy.start()
    for copy in copies:
        copy.wait()


def local(points, start_panel):
    nz = lax.axis_size("row") // 2
    ny = lax.axis_size("col") // NX
    rows, vec = start_panel.shape
    width = points.shape[1]
    chunk = NX * OWN
    mid = nz * HALF
    ncols = 2 * mid
    lines = 2 * ncols // LANES
    vmem = pltpu.VMEM
    dma = pltpu.SemaphoreType.DMA
    anywhere = pl.BlockSpec(memory_space=pl.ANY)
    sums = [vmem((n, vec // 2, 2 * vec), f32) for n in (2 * NX, ny, nz)]
    out_shape = (
        jax.ShapeDtypeStruct((vec, rows), f32),
        jax.ShapeDtypeStruct((vec, vec), f32),
    )
    results = pl.pallas_call(
        functools.partial(kernel, nz, ny),
        out_shape=out_shape,
        in_specs=[anywhere] * 2,
        out_specs=(pl.BlockSpec(memory_space=vmem),) * 2,
        scratch_shapes=[
            vmem(points.shape, f32),
            vmem((LANES, vec), f32),
            vmem((vec, LANES), f32),
            vmem((2, nz, HALF, LANES), f32),
            vmem((ny, NX, OWN, width), bf16),
            vmem((2, 2, nz, HALF, width), bf16),
            vmem((2, ny, chunk, ncols), bf16),
            vmem((2, 8, ncols), f32),
            vmem((lines, LANES), f32),
            vmem((2, lines, LANES), f32),
            vmem((nz, lines, LANES), f32),
            vmem((2, ncols, LANES), f32),
            vmem((2, ncols, LANES), bf16),
            vmem((ny, NX, HALF, LANES), bf16),
            vmem((ny, NX, HALF, LANES), bf16),
            vmem((ny, HALF, LANES), f32),
            vmem((ny, HALF, LANES), f32),
            vmem((ny, NX, OWN, LANES), bf16),
            vmem((2, LANES, ncols), f32),
            vmem((2, vec, ncols), f32),
            vmem((vec, ncols), f32),
            vmem((nz, HALF, LANES), f32),
            vmem((nz, HALF, LANES), f32),
            *sums, *sums, *sums,
            vmem((ny, NX, HALF, LANES), f32),
            vmem((6 * vec, rows), bf16),
            dma, dma, dma((25,)), dma((25,)), dma((ny,)), dma((ny,)), dma((ny,)), dma((ny,)), dma((ny,)),
        ],
        compiler_params=pltpu.CompilerParams(
            collective_id=0, has_side_effects=True, vmem_limit_bytes=60 << 20
        ),
        name="embed",
    )(points, start_panel.T)
    panels, ritz_sum = pl.pallas_call(
        hand_over,
        out_shape=out_shape,
        in_specs=[anywhere] * 2,
        out_specs=(anywhere,) * 2,
        scratch_shapes=[dma((2,))],
        compiler_params=pltpu.CompilerParams(vmem_limit_bytes=60 << 20),
        name="hand_over",
    )(*results)
    return panels.T, ritz_sum


def solution(mesh):
    in_specs = (P(("row", "col"), None), P("row", None))
    out_specs = (P("row", None), P())
    return jax.shard_map(local, mesh=mesh, in_specs=in_specs, out_specs=out_specs, check_vma=False)
```

```python
import functools
import math

import jax
import jax.numpy as jnp
from jax import lax
from jax.experimental import pallas as pl
from jax.experimental.pallas import tpu as pltpu
from jax.sharding import PartitionSpec as P

MESH = pl.DeviceIdType.MESH
NX = 4
HALF = 32
OWN = 2 * HALF
LANES = 128
SHARPNESS = 5.0
LOG2E = math.log2(math.e)
f32 = jnp.float32
bf16 = jnp.bfloat16


def dot(a, b, contract=((1,), (0,)), precision=None):
    return lax.dot_general(
        a, b, (contract, ((), ())), precision=precision, preferred_element_type=f32
    )


def full(a, b, contract=((1,), (0,))):
    return dot(a, b, contract, lax.Precision.HIGHEST)


def iota(shape, axis):
    return lax.broadcasted_iota(jnp.int32, shape, axis)


def add(parts):
    return functools.reduce(lambda a, b: a + b, parts)


def inverse_factor(gram, width=16):
    n = gram.shape[0]
    eye = jnp.where(iota((n, n), 0) == iota((n, n), 1), 1.0, 0.0).astype(f32)
    mat = jnp.concatenate([gram, eye], axis=1)
    done = []
    for b in range(0, n, width):
        m = n - b
        cols = [jnp.broadcast_to(mat[:, b + j:b + j + 1], (m, 2 * n)) for j in range(width)]
        rows = [mat[j:j + 1] for j in range(width)]
        for j in range(width):
            root = lax.rsqrt(cols[j][j:j + 1])
            cols[j], rows[j] = cols[j] * root, rows[j] * root
            for i in range(j + 1, width):
                factor = cols[j][i:i + 1]
                cols[i], rows[i] = cols[i] - factor * cols[j], rows[i] - factor * rows[j]
        done += rows
        mat = mat[width:]
        for j in range(width if m > width else 0):
            mat = mat - cols[j][width:] * rows[j]
    return jnp.concatenate(done, axis=0)[:, n:]


def pack(mat):
    n = mat.shape[0] // 2
    return jnp.concatenate([mat[:n], mat[n:]], axis=1)


def unpack(mat):
    n = mat.shape[1] // 2
    return jnp.concatenate([mat[:, :n], mat[:, n:]], axis=0)


def split(value, parts):
    out = []
    for _ in range(parts):
        out.append(value.astype(bf16))
        value = value - out[-1].astype(f32)
    return out


def kernel(
    nz, ny, points_ref, start_ref, out_ref, ritz_ref,
    points, pair_rows, pair_cols, start, rowpts, colpts, tile, colsum, deg, deg_c, deg_z, inv_col,
    panel, send_p, recv_px, send_y, recv_py, scaled, total_c, half_c, recv_c, send_z, recv_z,
    first_x, first_y, first_z, gram_x, gram_y, gram_z, ritz_x, ritz_y, ritz_z, whole, stack,
    load_sem, points_sem, send_sem, recv_sem, from_y, from_x, part_x, again_y, again_x,
):
    r, c = lax.axis_index("row"), lax.axis_index("col")
    z, core = r // 2, lax.rem(r, 2)
    y, x = c // NX, lax.rem(c, NX)
    axes = {
        "x": (NX, x, lambda p: (r, y * NX + p)),
        "y": (ny, y, lambda p: (r, p * NX + x)),
        "z": (nz, z, lambda p: (p * 2 + core, c)),
        "c": (2, core, lambda p: (z * 2 + p, c)),
        "xc": (2 * NX, x * 2 + core, lambda p: (z * 2 + lax.rem(p, 2), y * NX + p // 2)),
    }
    met = ("xc", "y", "z")
    count = sum(axes[axis][0] - 1 for axis in met)
    chunk = NX * OWN
    mid = nz * HALF
    ncols = 2 * mid
    total = 2 * ny * chunk * nz
    width = points_ref.shape[1]
    vec = ritz_ref.shape[0]

    load_points = pltpu.make_async_copy(points_ref, points, points_sem)
    load_points.start()
    here = pl.ds(pl.multiple_of(c // 2 * LANES, LANES), LANES)
    load = pltpu.make_async_copy(start_ref.at[:, here], pair_cols, load_sem)
    load.start()
    barrier = pltpu.get_barrier_semaphore()
    for axis in met:
        n, me, device = axes[axis]

        def greet(i, carry):
            pl.semaphore_signal(
                barrier, inc=1, device_id=device(lax.rem(me + i, n)), device_id_type=MESH
            )
            return carry
        lax.fori_loop(1, n, greet, 0)

    sent = {}
    pending = {}

    def send(slot, axis, src, dst, got, recv=None):
        n, me, device = axes[axis]
        arrival = recv_sem.at[slot] if recv is None else recv

        def one(i, carry):
            p = lax.rem(me + i, n)
            pltpu.make_async_remote_copy(
                src_ref=src(p), dst_ref=dst, send_sem=send_sem.at[slot],
                recv_sem=arrival, device_id=device(p), device_id_type=MESH,
            ).start()
            return carry
        lax.fori_loop(1, n, one, 0)
        sent[slot] = got
        if recv is None:
            pending[slot] = got

    def wait(ref, sem):
        pltpu.make_async_copy(ref, ref, sem).wait()

    def arrive(slot):
        wait(pending.pop(slot), recv_sem.at[slot])

    def drain():
        for slot in list(pending):
            arrive(slot)
        for slot, ref in sent.items():
            wait(ref, send_sem.at[slot])

    def all_sum(slot, axis, value, buf):
        n, me, _ = axes[axis]
        buf[me] = value
        send(slot, axis, lambda p: buf.at[me], buf.at[me], buf.at[pl.ds(0, n - 1)])

        def done():
            arrive(slot)
            return add([buf[i] for i in range(n)])
        return done

    def near(i):
        return lax.rem(y + 2 * ny + (2 * lax.rem(i, 2) - 1) * ((i + 1) // 2), ny)

    def spread(slot, buf, sems_y, sems_x):
        send(slot, "y", lambda p: buf.at[y, x], buf.at[y, x],
             buf.at[pl.ds(0, ny - 1), 0], sems_y.at[y])

        def forward(i, carry):
            yy = near(i)

            @pl.when(i > 0)
            def _():
                wait(buf.at[yy, x], sems_y.at[yy])
            send(slot + 1, "x", lambda p: buf.at[yy, x], buf.at[yy, x],
                 buf.at[:, pl.ds(0, NX - 1)], sems_x.at[yy])
            return carry

        def on():
            lax.fori_loop(0, ny, forward, 0)
            sent[slot + 1] = buf.at[:, pl.ds(0, NX - 1)]
        return on

    shift = SHARPNESS * LOG2E
    load_points.wait()
    pts = points[...]
    unit = pts * lax.rsqrt(jnp.mean(pts * pts, axis=1, keepdims=True) + 1e-06)
    unit = (unit * math.sqrt(shift / width)).astype(bf16)
    rowpts[y, x] = unit
    colpts[core, :, z] = unit.reshape(2, HALF, width)
    colsum[...] = jnp.zeros_like(colsum)

    load.wait()
    pair_rows[...] = pair_cols[...].T
    odd = lax.rem(x, 2) * OWN
    start[core, z] = jnp.concatenate(
        [pair_rows[pl.ds(odd, HALF)], pair_rows[pl.ds(odd + HALF, HALF)]], axis=1
    )

    pl.semaphore_wait(barrier, count)
    rows_on = spread(0, rowpts, from_y, from_x)
    send(2, "z", lambda p: colpts.at[core, :, z], colpts.at[core, :, z],
         colpts.at[0, :, pl.ds(0, nz - 1)])
    rows_on()
    arrive(2)
    send(3, "c", lambda p: colpts.at[core], colpts.at[core], colpts.at[0])
    send(4, "z", lambda p: start.at[core, z], start.at[core, z], start.at[0, pl.ds(0, nz - 1)])

    def affinity(yy, k):
        left = rowpts[yy].reshape(chunk, width)
        right = colpts[k].reshape(ncols, width)
        value = jnp.exp2(dot(left, right, ((1,), (1,))) - shift)
        tile[k, yy] = value.astype(bf16)
        colsum[k] = colsum[k] + jnp.sum(value.reshape(chunk // 8, 8, ncols), axis=0)

    def chunk_here(i):
        yy = near(i)
        wait(rowpts.at[yy, pl.ds(0, NX - 1)], from_x.at[yy])
        return yy

    def near_half(i, carry):
        affinity(chunk_here(i), core)
        return carry

    def far_half(i, carry):
        affinity(near(i), 1 - core)
        return carry

    def both_halves(i, carry):
        yy = chunk_here(i)
        affinity(yy, core)
        affinity(yy, 1 - core)
        return carry
    early = ny - ny // 4
    lax.fori_loop(0, early, near_half, 0)
    arrive(3)
    lax.fori_loop(0, early, far_half, 0)
    lax.fori_loop(early, ny, both_halves, 0)
    lines = ncols // LANES
    for k in range(2):
        line = jnp.sum(colsum[k], axis=0, keepdims=True)
        for j in range(lines):
            deg[k * lines + j:k * lines + j + 1] = line[:, j * LANES:(j + 1) * LANES]

    degrees = all_sum(5, "c", deg[...], deg_c)
    arrive(4)
    send(6, "c", lambda p: start.at[core], start.at[core], start.at[0])
    degrees = all_sum(7, "z", degrees(), deg_z)
    arrive(6)
    inv_root = lax.rsqrt(degrees())
    for k in range(2):
        for j in range(lines):
            row = inv_root[k * lines + j:k * lines + j + 1]
            inv_col[k, j * LANES:(j + 1) * LANES] = jnp.broadcast_to(row, (LANES, LANES)).T
    low = iota((mid, LANES), 1) < vec
    for k in range(2):
        one = start[k].reshape(mid, LANES)
        two = pltpu.roll(one, vec, 1)
        panel[k, :mid] = (jnp.where(low, one, two) * inv_col[k, :mid]).astype(bf16)
        panel[k, mid:] = (jnp.where(low, two, one) * inv_col[k, mid:]).astype(bf16)
    keep = iota((HALF, LANES), 1) < vec
    inv_packed = jnp.where(
        keep, inv_col[core, pl.ds(z * HALF, HALF)], inv_col[core, pl.ds(mid + z * HALF, HALF)]
    )

    def product(j, carry):
        yy = near(ny - 1 - j)
        out = dot(tile[0, yy], panel[0]) + dot(tile[1, yy], panel[1])
        for s in range(NX):
            send_p[yy, s] = jnp.where(
                keep, out[s * OWN:s * OWN + HALF], out[s * OWN + HALF:(s + 1) * OWN]
            ).astype(bf16)
        send(8, "x", lambda p: send_p.at[yy, p], recv_px.at[yy, x],
             send_p.at[:, pl.ds(0, NX - 1)], part_x.at[yy])
        recv_px[yy, x] = send_p[yy, x]
        return carry
    lax.fori_loop(0, ny, product, 0)
    sent[8] = send_p.at[:, pl.ds(0, NX - 1)]

    def collect(j, carry):
        yy = near(ny - 1 - j)
        wait(recv_px.at[yy, pl.ds(0, NX - 1)], part_x.at[yy])
        send_y[yy] = add([recv_px[yy, i].astype(f32) for i in range(NX)]).astype(bf16)

        @pl.when(j < ny - 1)
        def _():
            pltpu.make_async_remote_copy(
                src_ref=send_y.at[yy], dst_ref=recv_py.at[y], send_sem=send_sem.at[9],
                recv_sem=recv_sem.at[9], device_id=(r, yy * NX + x), device_id_type=MESH,
            ).start()
        return carry
    lax.fori_loop(0, ny, collect, 0)
    sent[9] = pending[9] = recv_py.at[pl.ds(0, ny - 1)]
    recv_py[y] = send_y[y]
    arrive(9)
    first_packed = add([recv_py[i].astype(f32) for i in range(ny)]) * inv_packed

    scaled[y, x] = jnp.concatenate(split(unpack(first_packed * inv_packed), 2), axis=1)
    scaled_on = spread(10, scaled, again_y, again_x)
    first = unpack(first_packed)
    first_sum = all_sum(12, "z", pack(full(first, first, ((0,), (0,)))), first_z)
    scaled_on()
    first_sum = all_sum(13, "xc", first_sum(), first_x)

    def transposed(i, k):
        yy = near(i)
        left = scaled[yy].reshape(chunk, 2 * vec).T
        return dot(left, tile[k, yy])

    def chunk_there(i):
        yy = near(i)
        wait(scaled.at[yy, pl.ds(0, NX - 1)], again_x.at[yy])

    def gather(i, carry):
        chunk_there(i)
        for k in range(2):
            total_c[k] = total_c[k] + transposed(i, k)
        return carry
    chunk_there(0)
    for k in range(2):
        total_c[k] = transposed(0, k)
    late = max(ny - 2, 1)
    lax.fori_loop(1, late, gather, 0)
    first_sum = all_sum(15, "y", first_sum(), first_y)
    lax.fori_loop(late, ny, gather, 0)
    for k in range(2):
        half_c[k] = total_c[k, :vec] + total_c[k, vec:]
    send(14, "c", lambda p: half_c.at[p], recv_c, recv_c)
    arrive(14)
    both = half_c[core] + recv_c[...]
    both = jnp.concatenate([both[:, :mid], both[:, mid:]], axis=0).T
    send_z[...] = both.reshape(send_z.shape)
    send(16, "z", lambda p: send_z.at[p], recv_z.at[z], recv_z.at[pl.ds(0, nz - 1)])
    recv_z[z] = send_z[z]
    inv_first = inverse_factor(unpack(first_sum()) / total)
    none = jnp.zeros_like(inv_first)
    twice = jnp.concatenate(
        [jnp.concatenate([inv_first, none], axis=1), jnp.concatenate([none, inv_first], axis=1)],
        axis=0,
    )
    basis_packed = full(first_packed, twice, ((1,), (1,)))

    def product_sums(left, right):
        both = full(left, right, ((0,), (0,)))
        return pack(both[:vec, :vec] + both[vec:, vec:])
    arrive(16)
    second_packed = add([recv_z[i] for i in range(nz)]) * inv_packed
    second_packed = full(second_packed, twice, ((1,), (1,)))

    whole[y, x] = second_packed
    send(20, "y", lambda p: whole.at[y, x], whole.at[y, x], whole.at[pl.ds(0, ny - 1), 0])
    gram = all_sum(17, "xc", product_sums(second_packed, second_packed), gram_x)
    ritz = all_sum(18, "z", product_sums(basis_packed, second_packed), ritz_z)
    gram = all_sum(19, "y", gram(), gram_y)
    ritz = all_sum(22, "xc", ritz(), ritz_x)
    arrive(20)
    send(21, "x", lambda p: whole.at[:, x], whole.at[:, x], whole.at[:, pl.ds(0, NX - 1)])
    gram = all_sum(23, "z", gram(), gram_z)
    ritz = all_sum(24, "y", ritz(), ritz_y)
    arrive(21)

    def prepare(yy, carry):
        parts = []
        for s in range(NX):
            block = whole[yy, s]
            parts += [block, pltpu.roll(block, vec, 1)]
        high, middle, low = split(jnp.concatenate(parts, axis=0).T[:vec], 3)
        columns = pl.ds(pl.multiple_of(yy * chunk, chunk), chunk)
        stack[:, columns] = jnp.concatenate([high, middle, low, high, middle, high], axis=0)
        return carry
    lax.fori_loop(0, ny, prepare, 0)
    last = inverse_factor(unpack(gram()) / total)
    high, middle, low = [part.astype(f32) for part in split(last, 3)]
    last = jnp.concatenate([high, high, high, middle, middle, low], axis=1).astype(bf16)
    block = min(4 * chunk, ny * chunk)
    for j in range(0, ny * chunk, block):
        out_ref[:, j:j + block] = dot(last, stack[:, j:j + block])
    ritz_ref[...] = unpack(ritz()) / total
    drain()


def hand_over(panels_ref, ritz_ref, panels_out, ritz_out, sems):
    copies = [
        pltpu.make_async_copy(panels_ref, panels_out, sems.at[0]),
        pltpu.make_async_copy(ritz_ref, ritz_out, sems.at[1]),
    ]
    for copy in copies:
        copy.start()
    for copy in copies:
        copy.wait()


def local(points, start_panel):
    nz = lax.axis_size("row") // 2
    ny = lax.axis_size("col") // NX
    rows, vec = start_panel.shape
    width = points.shape[1]
    chunk = NX * OWN
    mid = nz * HALF
    ncols = 2 * mid
    lines = 2 * ncols // LANES
    vmem = pltpu.VMEM
    dma = pltpu.SemaphoreType.DMA
    hbm = pl.BlockSpec(memory_space=pltpu.HBM)
    sums = [vmem((n, vec // 2, 2 * vec), f32) for n in (2 * NX, ny, nz)]
    out_shape = (
        jax.ShapeDtypeStruct((vec, rows), f32),
        jax.ShapeDtypeStruct((vec, vec), f32),
    )
    results = pl.pallas_call(
        functools.partial(kernel, nz, ny),
        out_shape=out_shape,
        in_specs=[hbm] * 2,
        out_specs=(pl.BlockSpec(memory_space=vmem),) * 2,
        scratch_shapes=[
            vmem(points.shape, f32),
            vmem((LANES, vec), f32),
            vmem((vec, LANES), f32),
            vmem((2, nz, HALF, LANES), f32),
            vmem((ny, NX, OWN, width), bf16),
            vmem((2, 2, nz, HALF, width), bf16),
            vmem((2, ny, chunk, ncols), bf16),
            vmem((2, 8, ncols), f32),
            vmem((lines, LANES), f32),
            vmem((2, lines, LANES), f32),
            vmem((nz, lines, LANES), f32),
            vmem((2, ncols, LANES), f32),
            vmem((2, ncols, LANES), bf16),
            vmem((ny, NX, HALF, LANES), bf16),
            vmem((ny, NX, HALF, LANES), bf16),
            vmem((ny, HALF, LANES), bf16),
            vmem((ny, HALF, LANES), bf16),
            vmem((ny, NX, OWN, LANES), bf16),
            vmem((2, LANES, ncols), f32),
            vmem((2, vec, ncols), f32),
            vmem((vec, ncols), f32),
            vmem((nz, HALF, LANES), f32),
            vmem((nz, HALF, LANES), f32),
            *sums, *sums, *sums,
            vmem((ny, NX, HALF, LANES), f32),
            vmem((6 * vec, rows), bf16),
            dma, dma, dma((25,)), dma((25,)), dma((ny,)), dma((ny,)), dma((ny,)), dma((ny,)), dma((ny,)),
        ],
        compiler_params=pltpu.CompilerParams(
            collective_id=0, has_side_effects=True, vmem_limit_bytes=53 << 20
        ),
        name="embed",
    )(points, start_panel.T)
    panels, ritz_sum = pl.pallas_call(
        hand_over,
        out_shape=out_shape,
        in_specs=[pl.BlockSpec(memory_space=pl.ANY)] * 2,
        out_specs=(hbm,) * 2,
        scratch_shapes=[dma((2,))],
        compiler_params=pltpu.CompilerParams(vmem_limit_bytes=4 << 20),
        name="hand_over",
    )(*results)
    return panels.T, ritz_sum


def solution(mesh):
    in_specs = (P(("row", "col"), None), P("row", None))
    out_specs = (P("row", None), P())
    return jax.shard_map(local, mesh=mesh, in_specs=in_specs, out_specs=out_specs, check_vma=False)
```

```python
import functools
import math

import jax
import jax.numpy as jnp
from jax import lax
from jax.experimental import pallas as pl
from jax.experimental.pallas import tpu as pltpu
from jax.sharding import PartitionSpec as P

MESH = pl.DeviceIdType.MESH
NX = 4
HALF = 32
OWN = 2 * HALF
LANES = 128
SHARPNESS = 5.0
LOG2E = math.log2(math.e)
f32 = jnp.float32
bf16 = jnp.bfloat16


def dot(a, b, contract=((1,), (0,)), precision=None):
    return lax.dot_general(
        a, b, (contract, ((), ())), precision=precision, preferred_element_type=f32
    )


def full(a, b, contract=((1,), (0,))):
    return dot(a, b, contract, lax.Precision.HIGHEST)


def iota(shape, axis):
    return lax.broadcasted_iota(jnp.int32, shape, axis)


def add(parts):
    return functools.reduce(lambda a, b: a + b, parts)


def inverse_factor(gram, width=16):
    n = gram.shape[0]
    eye = jnp.where(iota((n, n), 0) == iota((n, n), 1), 1.0, 0.0).astype(f32)
    mat = jnp.concatenate([gram, eye], axis=1)
    done = []
    for b in range(0, n, width):
        m = n - b
        cols = [jnp.broadcast_to(mat[:, b + j:b + j + 1], (m, 2 * n)) for j in range(width)]
        rows = [mat[j:j + 1] for j in range(width)]
        for j in range(width):
            root = lax.rsqrt(cols[j][j:j + 1])
            cols[j], rows[j] = cols[j] * root, rows[j] * root
            for i in range(j + 1, width):
                factor = cols[j][i:i + 1]
                cols[i], rows[i] = cols[i] - factor * cols[j], rows[i] - factor * rows[j]
        done += rows
        mat = mat[width:]
        for j in range(width if m > width else 0):
            mat = mat - cols[j][width:] * rows[j]
    return jnp.concatenate(done, axis=0)[:, n:]


def pack(mat):
    n = mat.shape[0] // 2
    return jnp.concatenate([mat[:n], mat[n:]], axis=1)


def unpack(mat):
    n = mat.shape[1] // 2
    return jnp.concatenate([mat[:, :n], mat[:, n:]], axis=0)


def split(value, parts):
    out = []
    for _ in range(parts):
        out.append(value.astype(bf16))
        value = value - out[-1].astype(f32)
    return out


def kernel(
    nz, ny, points_ref, start_ref, out_ref, ritz_ref,
    points, pair_rows, pair_cols, start, rowpts, colpts, tile, colsum, deg, deg_zc, inv_col,
    panel, send_p, recv_px, send_y, recv_py, scaled, total_c, half_c, recv_c, send_z, recv_z,
    first_x, first_y, first_z, gram_x, gram_y, gram_z, ritz_x, ritz_y, ritz_z, whole, stack,
    load_sem, points_sem, send_sem, recv_sem, from_y, from_x, part_x, again_y, again_x,
):
    r, c = lax.axis_index("row"), lax.axis_index("col")
    z, core = r // 2, lax.rem(r, 2)
    y, x = c // NX, lax.rem(c, NX)
    axes = {
        "x": (NX, x, lambda p: (r, y * NX + p)),
        "y": (ny, y, lambda p: (r, p * NX + x)),
        "z": (nz, z, lambda p: (p * 2 + core, c)),
        "c": (2, core, lambda p: (z * 2 + p, c)),
        "xc": (2 * NX, x * 2 + core, lambda p: (z * 2 + lax.rem(p, 2), y * NX + p // 2)),
    }
    axes["zc"] = (2 * nz, r, lambda p: (p, c))
    axes["other core"] = (nz, z, lambda p: (p * 2 + 1 - core, c))
    beside = [lax.rem(y + step, ny) for step in ((1, ny - 1) if ny > 2 else range(1, ny))]
    for i, yy in enumerate(beside):
        axes[i] = (NX, x, lambda p, yy=yy: (r, yy * NX + p))
    met = ["xc", "y", "z", "other core", *range(len(beside))]
    count = sum(axes[axis][0] - 1 for axis in met)
    chunk = NX * OWN
    mid = nz * HALF
    ncols = 2 * mid
    total = 2 * ny * chunk * nz
    width = points_ref.shape[1]
    vec = ritz_ref.shape[0]

    load_points = pltpu.make_async_copy(points_ref, points, points_sem)
    load_points.start()
    here = pl.ds(pl.multiple_of(c // 2 * LANES, LANES), LANES)
    load = pltpu.make_async_copy(start_ref.at[:, here], pair_cols, load_sem)
    load.start()
    barrier = pltpu.get_barrier_semaphore()
    for axis in met:
        n, me, device = axes[axis]

        def greet(i, carry):
            pl.semaphore_signal(
                barrier, inc=1, device_id=device(lax.rem(me + i, n)), device_id_type=MESH
            )
            return carry
        lax.fori_loop(1, n, greet, 0)

    sent = {}
    pending = {}

    def send(slot, axis, src, dst, got, recv=None):
        n, me, device = axes[axis]
        arrival = recv_sem.at[slot] if recv is None else recv

        def one(i, carry):
            p = lax.rem(me + i, n)
            pltpu.make_async_remote_copy(
                src_ref=src(p), dst_ref=dst, send_sem=send_sem.at[slot],
                recv_sem=arrival, device_id=device(p), device_id_type=MESH,
            ).start()
            return carry
        lax.fori_loop(1, n, one, 0)
        sent[slot] = got
        if recv is None:
            pending[slot] = got

    def wait(ref, sem):
        pltpu.make_async_copy(ref, ref, sem).wait()

    def arrive(slot):
        wait(pending.pop(slot), recv_sem.at[slot])

    def drain():
        for slot in list(pending):
            arrive(slot)
        for slot, ref in sent.items():
            wait(ref, send_sem.at[slot])

    def all_sum(slot, axis, value, buf):
        n, me, _ = axes[axis]
        buf[me] = value
        send(slot, axis, lambda p: buf.at[me], buf.at[me], buf.at[pl.ds(0, n - 1)])

        def done():
            arrive(slot)
            return add([buf[i] for i in range(n)])
        return done

    def near(i):
        return lax.rem(y + 2 * ny + (2 * lax.rem(i, 2) - 1) * ((i + 1) // 2), ny)

    def spread(slot, buf, sems_y, sems_x):
        send(slot, "y", lambda p: buf.at[y, x], buf.at[y, x],
             buf.at[pl.ds(0, ny - 1), 0], sems_y.at[y])
        for axis in ("x", *range(len(beside))):
            send(slot + 1, axis, lambda p: buf.at[y, x], buf.at[y, x],
                 buf.at[:, pl.ds(0, NX - 1)], sems_x.at[y])

        def forward(i, carry):
            yy = near(i)
            wait(buf.at[yy, x], sems_y.at[yy])
            send(slot + 1, "x", lambda p: buf.at[yy, x], buf.at[yy, x],
                 buf.at[:, pl.ds(0, NX - 1)], sems_x.at[yy])
            return carry

        def on():
            lax.fori_loop(1 + len(beside), ny, forward, 0)
            for yy in beside:
                wait(buf.at[yy, x], sems_y.at[yy])
            sent[slot + 1] = buf.at[:, pl.ds(0, NX - 1)]
        return on

    shift = SHARPNESS * LOG2E
    load_points.wait()
    pts = points[...]
    unit = pts * lax.rsqrt(jnp.mean(pts * pts, axis=1, keepdims=True) + 1e-06)
    unit = (unit * math.sqrt(shift / width)).astype(bf16)
    rowpts[y, x] = unit
    colpts[core, :, z] = unit.reshape(2, HALF, width)
    colsum[...] = jnp.zeros_like(colsum)

    load.wait()
    pair_rows[...] = pair_cols[...].T
    odd = lax.rem(x, 2) * OWN
    start[core, z] = jnp.concatenate(
        [pair_rows[pl.ds(odd, HALF)], pair_rows[pl.ds(odd + HALF, HALF)]], axis=1
    )

    pl.semaphore_wait(barrier, count)
    rows_on = spread(0, rowpts, from_y, from_x)
    send(2, "z", lambda p: colpts.at[core, :, z], colpts.at[core, :, z],
         colpts.at[0, :, pl.ds(0, nz - 1)])
    rows_on()
    arrive(2)
    send(3, "c", lambda p: colpts.at[core], colpts.at[core], colpts.at[0])
    send(4, "z", lambda p: start.at[core, z], start.at[core, z], start.at[0, pl.ds(0, nz - 1)])

    def affinity(yy, k):
        left = rowpts[yy].reshape(chunk, width)
        right = colpts[k].reshape(ncols, width)
        value = jnp.exp2(dot(left, right, ((1,), (1,))) - shift)
        tile[k, yy] = value.astype(bf16)
        colsum[k] = colsum[k] + jnp.sum(value.reshape(chunk // 8, 8, ncols), axis=0)

    def chunk_here(i):
        yy = near(i)
        wait(rowpts.at[yy, pl.ds(0, NX - 1)], from_x.at[yy])
        return yy

    def near_half(i, carry):
        affinity(chunk_here(i), core)
        return carry

    def far_half(i, carry):
        affinity(near(i), 1 - core)
        return carry

    def both_halves(i, carry):
        yy = chunk_here(i)
        affinity(yy, core)
        affinity(yy, 1 - core)
        return carry
    early = ny - ny // 4
    lax.fori_loop(0, early, near_half, 0)
    arrive(3)
    lax.fori_loop(0, early, far_half, 0)
    lax.fori_loop(early, ny, both_halves, 0)
    lines = ncols // LANES
    for k in range(2):
        line = jnp.sum(colsum[k], axis=0, keepdims=True)
        for j in range(lines):
            deg[k * lines + j:k * lines + j + 1] = line[:, j * LANES:(j + 1) * LANES]

    degrees = all_sum(5, "zc", deg[...], deg_zc)
    arrive(4)
    send(6, "c", lambda p: start.at[core], start.at[core], start.at[0])
    arrive(6)
    inv_root = lax.rsqrt(degrees())
    for k in range(2):
        for j in range(lines):
            row = inv_root[k * lines + j:k * lines + j + 1]
            inv_col[k, j * LANES:(j + 1) * LANES] = jnp.broadcast_to(row, (LANES, LANES)).T
    low = iota((mid, LANES), 1) < vec
    for k in range(2):
        one = start[k].reshape(mid, LANES)
        two = pltpu.roll(one, vec, 1)
        panel[k, :mid] = (jnp.where(low, one, two) * inv_col[k, :mid]).astype(bf16)
        panel[k, mid:] = (jnp.where(low, two, one) * inv_col[k, mid:]).astype(bf16)
    keep = iota((HALF, LANES), 1) < vec
    inv_packed = jnp.where(
        keep, inv_col[core, pl.ds(z * HALF, HALF)], inv_col[core, pl.ds(mid + z * HALF, HALF)]
    )

    pair = 2 if ny % 2 == 0 else 1

    def product(j):
        yy = near(ny - 1 - j)
        out = dot(tile[0, yy], panel[0]) + dot(tile[1, yy], panel[1])
        for s in range(NX):
            send_p[yy, s] = jnp.where(
                keep, out[s * OWN:s * OWN + HALF], out[s * OWN + HALF:(s + 1) * OWN]
            ).astype(bf16)

    def hand_on(j):
        yy = near(ny - 1 - j)
        send(8, "x", lambda p: send_p.at[yy, p], recv_px.at[yy, x],
             send_p.at[:, pl.ds(0, NX - 1)], part_x.at[yy])
        recv_px[yy, x] = send_p[yy, x]

    def products(j, carry):
        for b in range(pair):
            product(pair * j + b)
        for b in range(pair):
            hand_on(pair * j + b)
        return carry
    lax.fori_loop(0, ny // pair, products, 0)
    sent[8] = send_p.at[:, pl.ds(0, NX - 1)]

    def collect(j, carry):
        yy = near(ny - 1 - j)
        wait(recv_px.at[yy, pl.ds(0, NX - 1)], part_x.at[yy])
        send_y[yy] = add([recv_px[yy, i].astype(f32) for i in range(NX)]).astype(bf16)

        @pl.when(j < ny - 1)
        def _():
            pltpu.make_async_remote_copy(
                src_ref=send_y.at[yy], dst_ref=recv_py.at[y], send_sem=send_sem.at[9],
                recv_sem=recv_sem.at[9], device_id=(r, yy * NX + x), device_id_type=MESH,
            ).start()
        return carry
    lax.fori_loop(0, ny, collect, 0)
    sent[9] = pending[9] = recv_py.at[pl.ds(0, ny - 1)]
    recv_py[y] = send_y[y]
    arrive(9)
    first_packed = add([recv_py[i].astype(f32) for i in range(ny)]) * inv_packed

    scaled[y, x] = jnp.concatenate(split(unpack(first_packed * inv_packed), 2), axis=1)
    scaled_on = spread(10, scaled, again_y, again_x)
    first = unpack(first_packed)
    first_sum = all_sum(12, "z", pack(full(first, first, ((0,), (0,)))), first_z)
    scaled_on()
    first_sum = all_sum(15, "y", first_sum(), first_y)

    def transposed(i, k):
        yy = near(i)
        left = scaled[yy].reshape(chunk, 2 * vec).T
        return dot(left, tile[k, yy])

    def chunk_there(i):
        yy = near(i)
        wait(scaled.at[yy, pl.ds(0, NX - 1)], again_x.at[yy])

    def gather(i, carry):
        chunk_there(i)
        for k in range(2):
            total_c[k] = total_c[k] + transposed(i, k)
        return carry
    chunk_there(0)
    for k in range(2):
        total_c[k] = transposed(0, k)
    lax.fori_loop(1, ny, gather, 0)
    for k in range(2):
        half_c[k] = total_c[k, :vec] + total_c[k, vec:]
    send(14, "c", lambda p: half_c.at[p], recv_c, recv_c)
    first_sum = all_sum(13, "xc", first_sum(), first_x)
    arrive(14)
    both = half_c[core] + recv_c[...]
    both = jnp.concatenate([both[:, :mid], both[:, mid:]], axis=0).T
    send_z[...] = both.reshape(send_z.shape)
    send(16, "z", lambda p: send_z.at[p], recv_z.at[z], recv_z.at[pl.ds(0, nz - 1)])
    recv_z[z] = send_z[z]
    inv_first = inverse_factor(unpack(first_sum()) / total)
    none = jnp.zeros_like(inv_first)
    twice = jnp.concatenate(
        [jnp.concatenate([inv_first, none], axis=1), jnp.concatenate([none, inv_first], axis=1)],
        axis=0,
    )
    basis_packed = full(first_packed, twice, ((1,), (1,)))

    def product_sums(left, right):
        both = full(left, right, ((0,), (0,)))
        return pack(both[:vec, :vec] + both[vec:, vec:])
    arrive(16)
    second_packed = add([recv_z[i] for i in range(nz)]) * inv_packed
    second_packed = full(second_packed, twice, ((1,), (1,)))

    whole[y, x] = second_packed
    send(20, "y", lambda p: whole.at[y, x], whole.at[y, x], whole.at[pl.ds(0, ny - 1), 0])
    gram = all_sum(17, "xc", product_sums(second_packed, second_packed), gram_x)
    ritz = all_sum(18, "z", product_sums(basis_packed, second_packed), ritz_z)
    gram = all_sum(19, "y", gram(), gram_y)
    ritz = all_sum(22, "xc", ritz(), ritz_x)
    arrive(20)
    send(21, "x", lambda p: whole.at[:, x], whole.at[:, x], whole.at[:, pl.ds(0, NX - 1)])
    gram = all_sum(23, "z", gram(), gram_z)
    ritz = all_sum(24, "y", ritz(), ritz_y)
    arrive(21)

    def prepare(yy, carry):
        parts = []
        for s in range(NX):
            block = whole[yy, s]
            parts += [block, pltpu.roll(block, vec, 1)]
        high, middle, low = split(jnp.concatenate(parts, axis=0).T[:vec], 3)
        columns = pl.ds(pl.multiple_of(yy * chunk, chunk), chunk)
        stack[:, columns] = jnp.concatenate([high, middle, low, high, middle, high], axis=0)
        return carry
    lax.fori_loop(0, ny, prepare, 0)
    last = inverse_factor(unpack(gram()) / total)
    high, middle, low = [part.astype(f32) for part in split(last, 3)]
    last = jnp.concatenate([high, high, high, middle, middle, low], axis=1).astype(bf16)
    block = min(4 * chunk, ny * chunk)
    for j in range(0, ny * chunk, block):
        out_ref[:, j:j + block] = dot(last, stack[:, j:j + block])
    ritz_ref[...] = unpack(ritz()) / total
    drain()


def hand_over(panels_ref, ritz_ref, panels_out, ritz_out, sems):
    copies = [
        pltpu.make_async_copy(panels_ref, panels_out, sems.at[0]),
        pltpu.make_async_copy(ritz_ref, ritz_out, sems.at[1]),
    ]
    for copy in copies:
        copy.start()
    for copy in copies:
        copy.wait()


def local(points, start_panel):
    nz = lax.axis_size("row") // 2
    ny = lax.axis_size("col") // NX
    rows, vec = start_panel.shape
    width = points.shape[1]
    chunk = NX * OWN
    mid = nz * HALF
    ncols = 2 * mid
    lines = 2 * ncols // LANES
    vmem = pltpu.VMEM
    dma = pltpu.SemaphoreType.DMA
    hbm = pl.BlockSpec(memory_space=pltpu.HBM)
    sums = [vmem((n, vec // 2, 2 * vec), f32) for n in (2 * NX, ny, nz)]
    out_shape = (
        jax.ShapeDtypeStruct((vec, rows), f32),
        jax.ShapeDtypeStruct((vec, vec), f32),
    )
    results = pl.pallas_call(
        functools.partial(kernel, nz, ny),
        out_shape=out_shape,
        in_specs=[hbm] * 2,
        out_specs=(pl.BlockSpec(memory_space=vmem),) * 2,
        scratch_shapes=[
            vmem(points.shape, f32),
            vmem((LANES, vec), f32),
            vmem((vec, LANES), f32),
            vmem((2, nz, HALF, LANES), f32),
            vmem((ny, NX, OWN, width), bf16),
            vmem((2, 2, nz, HALF, width), bf16),
            vmem((2, ny, chunk, ncols), bf16),
            vmem((2, 8, ncols), f32),
            vmem((lines, LANES), f32),
            vmem((2 * nz, lines, LANES), f32),
            vmem((2, ncols, LANES), f32),
            vmem((2, ncols, LANES), bf16),
            vmem((ny, NX, HALF, LANES), bf16),
            vmem((ny, NX, HALF, LANES), bf16),
            vmem((ny, HALF, LANES), bf16),
            vmem((ny, HALF, LANES), bf16),
            vmem((ny, NX, OWN, LANES), bf16),
            vmem((2, LANES, ncols), f32),
            vmem((2, vec, ncols), f32),
            vmem((vec, ncols), f32),
            vmem((nz, HALF, LANES), f32),
            vmem((nz, HALF, LANES), f32),
            *sums, *sums, *sums,
            vmem((ny, NX, HALF, LANES), f32),
            vmem((6 * vec, rows), bf16),
            dma, dma, dma((25,)), dma((25,)), dma((ny,)), dma((ny,)), dma((ny,)), dma((ny,)), dma((ny,)),
        ],
        compiler_params=pltpu.CompilerParams(
            collective_id=0, has_side_effects=True, vmem_limit_bytes=53 << 20
        ),
        name="embed",
    )(points, start_panel.T)
    panels, ritz_sum = pl.pallas_call(
        hand_over,
        out_shape=out_shape,
        in_specs=[pl.BlockSpec(memory_space=pl.ANY)] * 2,
        out_specs=(hbm,) * 2,
        scratch_shapes=[dma((2,))],
        compiler_params=pltpu.CompilerParams(vmem_limit_bytes=4 << 20),
        name="hand_over",
    )(*results)
    return panels.T, ritz_sum


def solution(mesh):
    in_specs = (P(("row", "col"), None), P("row", None))
    out_specs = (P("row", None), P())
    return jax.shard_map(local, mesh=mesh, in_specs=in_specs, out_specs=out_specs, check_vma=False)
```

```python
import functools
import math

import jax
import jax.numpy as jnp
from jax import lax
from jax.experimental import pallas as pl
from jax.experimental.pallas import tpu as pltpu
from jax.sharding import PartitionSpec as P

MESH = pl.DeviceIdType.MESH
NX = 4
HALF = 32
OWN = 2 * HALF
LANES = 128
SHARPNESS = 5.0
LOG2E = math.log2(math.e)
f32 = jnp.float32
bf16 = jnp.bfloat16


def dot(a, b, contract=((1,), (0,)), precision=None):
    return lax.dot_general(
        a, b, (contract, ((), ())), precision=precision, preferred_element_type=f32
    )


def full(a, b, contract=((1,), (0,))):
    return dot(a, b, contract, lax.Precision.HIGHEST)


def iota(shape, axis):
    return lax.broadcasted_iota(jnp.int32, shape, axis)


def add(parts):
    return functools.reduce(lambda a, b: a + b, parts)


def inverse_factor(gram, width=16):
    n = gram.shape[0]
    eye = jnp.where(iota((n, n), 0) == iota((n, n), 1), 1.0, 0.0).astype(f32)
    mat = jnp.concatenate([gram, eye], axis=1)
    done = []
    for b in range(0, n, width):
        m = n - b
        cols = [jnp.broadcast_to(mat[:, b + j:b + j + 1], (m, 2 * n)) for j in range(width)]
        rows = [mat[j:j + 1] for j in range(width)]
        for j in range(width):
            root = lax.rsqrt(cols[j][j:j + 1])
            cols[j], rows[j] = cols[j] * root, rows[j] * root
            for i in range(j + 1, width):
                factor = cols[j][i:i + 1]
                cols[i], rows[i] = cols[i] - factor * cols[j], rows[i] - factor * rows[j]
        done += rows
        mat = mat[width:]
        for j in range(width if m > width else 0):
            mat = mat - cols[j][width:] * rows[j]
    return jnp.concatenate(done, axis=0)[:, n:]


def pack(mat):
    n = mat.shape[0] // 2
    return jnp.concatenate([mat[:n], mat[n:]], axis=1)


def unpack(mat):
    n = mat.shape[1] // 2
    return jnp.concatenate([mat[:, :n], mat[:, n:]], axis=0)


def split(value, parts):
    out = []
    for _ in range(parts):
        out.append(value.astype(bf16))
        value = value - out[-1].astype(f32)
    return out


def far(i, me, n):
    return lax.rem(me + n // 2 + (1 - 2 * lax.rem(i, 2)) * ((i + 1) // 2), n)


def kernel(
    nz, ny, points_ref, start_ref, out_ref, ritz_ref,
    points, pair_rows, pair_cols, start, rowpts, colpts, tile, colsum, deg, deg_zc, inv_col,
    panel, send_p, recv_px, send_y, recv_py, scaled, total_c, half_c, recv_c, send_z, recv_z,
    first_x, first_y, first_z, gram_x, gram_y, gram_z, ritz_x, ritz_y, ritz_z, whole, stack,
    load_sem, points_sem, send_sem, recv_sem, from_y, from_x, part_x, again_y, again_x,
):
    r, c = lax.axis_index("row"), lax.axis_index("col")
    z, core = r // 2, lax.rem(r, 2)
    y, x = c // NX, lax.rem(c, NX)
    axes = {
        "x": (NX, x, lambda p: (r, y * NX + p)),
        "y": (ny, y, lambda p: (r, p * NX + x)),
        "z": (nz, z, lambda p: (p * 2 + core, c)),
        "c": (2, core, lambda p: (z * 2 + p, c)),
        "xc": (2 * NX, x * 2 + core, lambda p: (z * 2 + lax.rem(p, 2), y * NX + p // 2)),
    }
    axes["zc"] = (2 * nz, r, lambda p: (p, c))
    axes["other core"] = (nz, z, lambda p: (p * 2 + 1 - core, c))
    beside = [lax.rem(y + step, ny) for step in ((1, ny - 1) if ny > 2 else range(1, ny))]
    for i, yy in enumerate(beside):
        axes[i] = (NX, x, lambda p, yy=yy: (r, yy * NX + p))
    met = ["xc", "y", "z", "other core", *range(len(beside))]
    count = sum(axes[axis][0] - 1 for axis in met)
    chunk = NX * OWN
    mid = nz * HALF
    ncols = 2 * mid
    total = 2 * ny * chunk * nz
    width = points_ref.shape[1]
    vec = ritz_ref.shape[0]

    load_points = pltpu.make_async_copy(points_ref, points, points_sem)
    load_points.start()
    here = pl.ds(pl.multiple_of(c // 2 * LANES, LANES), LANES)
    load = pltpu.make_async_copy(start_ref.at[:, here], pair_cols, load_sem)
    load.start()
    barrier = pltpu.get_barrier_semaphore()
    for axis in met:
        n, me, device = axes[axis]

        def greet(i, carry):
            pl.semaphore_signal(
                barrier, inc=1, device_id=device(far(i, me, n)), device_id_type=MESH
            )
            return carry
        lax.fori_loop(0, n - 1, greet, 0)

    sent = {}
    pending = {}

    def send(slot, axis, src, dst, got, recv=None):
        n, me, device = axes[axis]
        arrival = recv_sem.at[slot] if recv is None else recv

        def one(i, carry):
            p = far(i, me, n)
            pltpu.make_async_remote_copy(
                src_ref=src(p), dst_ref=dst, send_sem=send_sem.at[slot],
                recv_sem=arrival, device_id=device(p), device_id_type=MESH,
            ).start()
            return carry
        lax.fori_loop(0, n - 1, one, 0)
        sent[slot] = got
        if recv is None:
            pending[slot] = got

    def wait(ref, sem):
        pltpu.make_async_copy(ref, ref, sem).wait()

    def arrive(slot):
        wait(pending.pop(slot), recv_sem.at[slot])

    def drain():
        for slot in list(pending):
            arrive(slot)
        for slot, ref in sent.items():
            wait(ref, send_sem.at[slot])

    def all_sum(slot, axis, value, buf):
        n, me, _ = axes[axis]
        buf[me] = value
        send(slot, axis, lambda p: buf.at[me], buf.at[me], buf.at[pl.ds(0, n - 1)])

        def done():
            arrive(slot)
            return add([buf[i] for i in range(n)])
        return done

    def near(i):
        return lax.rem(y + 2 * ny + (2 * lax.rem(i, 2) - 1) * ((i + 1) // 2), ny)

    def spread(slot, buf, sems_y, sems_x):
        send(slot, "y", lambda p: buf.at[y, x], buf.at[y, x],
             buf.at[pl.ds(0, ny - 1), 0], sems_y.at[y])
        for axis in ("x", *range(len(beside))):
            send(slot + 1, axis, lambda p: buf.at[y, x], buf.at[y, x],
                 buf.at[:, pl.ds(0, NX - 1)], sems_x.at[y])

        def forward(i, carry):
            yy = near(i)
            wait(buf.at[yy, x], sems_y.at[yy])
            send(slot + 1, "x", lambda p: buf.at[yy, x], buf.at[yy, x],
                 buf.at[:, pl.ds(0, NX - 1)], sems_x.at[yy])
            return carry

        def on():
            lax.fori_loop(1 + len(beside), ny, forward, 0)
            for yy in beside:
                wait(buf.at[yy, x], sems_y.at[yy])
            sent[slot + 1] = buf.at[:, pl.ds(0, NX - 1)]
        return on

    shift = SHARPNESS * LOG2E
    load_points.wait()
    pts = points[...]
    unit = pts * lax.rsqrt(jnp.mean(pts * pts, axis=1, keepdims=True) + 1e-06)
    unit = (unit * math.sqrt(shift / width)).astype(bf16)
    rowpts[y, x] = unit
    colpts[core, :, z] = unit.reshape(2, HALF, width)
    colsum[...] = jnp.zeros_like(colsum)

    load.wait()
    pair_rows[...] = pair_cols[...].T
    odd = lax.rem(x, 2) * OWN
    start[core, z] = jnp.concatenate(
        [pair_rows[pl.ds(odd, HALF)], pair_rows[pl.ds(odd + HALF, HALF)]], axis=1
    )

    pl.semaphore_wait(barrier, count)
    rows_on = spread(0, rowpts, from_y, from_x)
    send(2, "z", lambda p: colpts.at[core, :, z], colpts.at[core, :, z],
         colpts.at[0, :, pl.ds(0, nz - 1)])
    rows_on()
    arrive(2)
    send(3, "c", lambda p: colpts.at[core], colpts.at[core], colpts.at[0])
    send(4, "z", lambda p: start.at[core, z], start.at[core, z], start.at[0, pl.ds(0, nz - 1)])

    def affinity(yy, k):
        left = rowpts[yy].reshape(chunk, width)
        right = colpts[k].reshape(ncols, width)
        value = jnp.exp2(dot(left, right, ((1,), (1,))) - shift)
        tile[k, yy] = value.astype(bf16)
        colsum[k] = colsum[k] + jnp.sum(value.reshape(chunk // 8, 8, ncols), axis=0)

    def chunk_here(i):
        yy = near(i)
        wait(rowpts.at[yy, pl.ds(0, NX - 1)], from_x.at[yy])
        return yy

    def near_half(i, carry):
        affinity(chunk_here(i), core)
        return carry

    def far_half(i, carry):
        affinity(near(i), 1 - core)
        return carry

    def both_halves(i, carry):
        yy = chunk_here(i)
        affinity(yy, core)
        affinity(yy, 1 - core)
        return carry
    early = ny - ny // 4
    lax.fori_loop(0, early, near_half, 0)
    arrive(3)
    lax.fori_loop(0, early, far_half, 0)
    lax.fori_loop(early, ny, both_halves, 0)
    lines = ncols // LANES
    for k in range(2):
        line = jnp.sum(colsum[k], axis=0, keepdims=True)
        for j in range(lines):
            deg[k * lines + j:k * lines + j + 1] = line[:, j * LANES:(j + 1) * LANES]

    degrees = all_sum(5, "zc", deg[...], deg_zc)
    arrive(4)
    send(6, "c", lambda p: start.at[core], start.at[core], start.at[0])
    arrive(6)
    inv_root = lax.rsqrt(degrees())
    for k in range(2):
        for j in range(lines):
            row = inv_root[k * lines + j:k * lines + j + 1]
            inv_col[k, j * LANES:(j + 1) * LANES] = jnp.broadcast_to(row, (LANES, LANES)).T
    low = iota((mid, LANES), 1) < vec
    for k in range(2):
        one = start[k].reshape(mid, LANES)
        two = pltpu.roll(one, vec, 1)
        panel[k, :mid] = (jnp.where(low, one, two) * inv_col[k, :mid]).astype(bf16)
        panel[k, mid:] = (jnp.where(low, two, one) * inv_col[k, mid:]).astype(bf16)
    keep = iota((HALF, LANES), 1) < vec
    inv_packed = jnp.where(
        keep, inv_col[core, pl.ds(z * HALF, HALF)], inv_col[core, pl.ds(mid + z * HALF, HALF)]
    )

    pair = 2 if ny % 2 == 0 else 1

    def product(j):
        yy = near(ny - 1 - j)
        out = dot(tile[0, yy], panel[0]) + dot(tile[1, yy], panel[1])
        for s in range(NX):
            send_p[yy, s] = jnp.where(
                keep, out[s * OWN:s * OWN + HALF], out[s * OWN + HALF:(s + 1) * OWN]
            ).astype(bf16)

    def hand_on(j):
        yy = near(ny - 1 - j)
        send(8, "x", lambda p: send_p.at[yy, p], recv_px.at[yy, x],
             send_p.at[:, pl.ds(0, NX - 1)], part_x.at[yy])
        recv_px[yy, x] = send_p[yy, x]

    def products(j, carry):
        for b in range(pair):
            product(pair * j + b)
        for b in range(pair):
            hand_on(pair * j + b)
        return carry
    lax.fori_loop(0, ny // pair, products, 0)
    sent[8] = send_p.at[:, pl.ds(0, NX - 1)]

    def collect(j, carry):
        yy = near(ny - 1 - j)
        wait(recv_px.at[yy, pl.ds(0, NX - 1)], part_x.at[yy])
        send_y[yy] = add([recv_px[yy, i].astype(f32) for i in range(NX)]).astype(bf16)

        @pl.when(j < ny - 1)
        def _():
            pltpu.make_async_remote_copy(
                src_ref=send_y.at[yy], dst_ref=recv_py.at[y], send_sem=send_sem.at[9],
                recv_sem=recv_sem.at[9], device_id=(r, yy * NX + x), device_id_type=MESH,
            ).start()
        return carry
    lax.fori_loop(0, ny, collect, 0)
    sent[9] = pending[9] = recv_py.at[pl.ds(0, ny - 1)]
    recv_py[y] = send_y[y]
    arrive(9)
    first_packed = add([recv_py[i].astype(f32) for i in range(ny)]) * inv_packed

    scaled[y, x] = jnp.concatenate(split(unpack(first_packed * inv_packed), 2), axis=1)
    scaled_on = spread(10, scaled, again_y, again_x)
    first = unpack(first_packed)
    first_sum = all_sum(12, "z", pack(full(first, first, ((0,), (0,)))), first_z)
    scaled_on()
    first_sum = all_sum(15, "y", first_sum(), first_y)

    def transposed(i, k):
        yy = near(i)
        left = scaled[yy].reshape(chunk, 2 * vec).T
        return dot(left, tile[k, yy])

    def chunk_there(i):
        yy = near(i)
        wait(scaled.at[yy, pl.ds(0, NX - 1)], again_x.at[yy])

    def gather(i, carry):
        chunk_there(i)
        for k in range(2):
            total_c[k] = total_c[k] + transposed(i, k)
        return carry
    chunk_there(0)
    for k in range(2):
        total_c[k] = transposed(0, k)
    lax.fori_loop(1, ny, gather, 0)
    for k in range(2):
        half_c[k] = total_c[k, :vec] + total_c[k, vec:]
    send(14, "c", lambda p: half_c.at[p], recv_c, recv_c)
    first_sum = all_sum(13, "xc", first_sum(), first_x)
    arrive(14)
    both = half_c[core] + recv_c[...]
    both = jnp.concatenate([both[:, :mid], both[:, mid:]], axis=0).T
    send_z[...] = both.reshape(send_z.shape)
    send(16, "z", lambda p: send_z.at[p], recv_z.at[z], recv_z.at[pl.ds(0, nz - 1)])
    recv_z[z] = send_z[z]
    inv_first = inverse_factor(unpack(first_sum()) / total)
    none = jnp.zeros_like(inv_first)
    twice = jnp.concatenate(
        [jnp.concatenate([inv_first, none], axis=1), jnp.concatenate([none, inv_first], axis=1)],
        axis=0,
    )
    basis_packed = full(first_packed, twice, ((1,), (1,)))

    def product_sums(left, right):
        both = full(left, right, ((0,), (0,)))
        return pack(both[:vec, :vec] + both[vec:, vec:])
    arrive(16)
    second_packed = add([recv_z[i] for i in range(nz)]) * inv_packed
    second_packed = full(second_packed, twice, ((1,), (1,)))

    whole[y, x] = second_packed
    send(20, "y", lambda p: whole.at[y, x], whole.at[y, x], whole.at[pl.ds(0, ny - 1), 0])
    gram = all_sum(17, "xc", product_sums(second_packed, second_packed), gram_x)
    ritz = all_sum(18, "z", product_sums(basis_packed, second_packed), ritz_z)
    gram = all_sum(19, "y", gram(), gram_y)
    ritz = all_sum(22, "xc", ritz(), ritz_x)
    arrive(20)
    send(21, "x", lambda p: whole.at[:, x], whole.at[:, x], whole.at[:, pl.ds(0, NX - 1)])
    gram = all_sum(23, "z", gram(), gram_z)
    ritz = all_sum(24, "y", ritz(), ritz_y)
    arrive(21)

    def prepare(yy, carry):
        parts = []
        for s in range(NX):
            block = whole[yy, s]
            parts += [block, pltpu.roll(block, vec, 1)]
        high, middle, low = split(jnp.concatenate(parts, axis=0).T[:vec], 3)
        columns = pl.ds(pl.multiple_of(yy * chunk, chunk), chunk)
        stack[:, columns] = jnp.concatenate([high, middle, low, high, middle, high], axis=0)
        return carry
    lax.fori_loop(0, ny, prepare, 0)
    last = inverse_factor(unpack(gram()) / total)
    high, middle, low = [part.astype(f32) for part in split(last, 3)]
    last = jnp.concatenate([high, high, high, middle, middle, low], axis=1).astype(bf16)
    block = min(4 * chunk, ny * chunk)
    for j in range(0, ny * chunk, block):
        out_ref[:, j:j + block] = dot(last, stack[:, j:j + block])
    ritz_ref[...] = unpack(ritz()) / total
    drain()


def hand_over(panels_ref, ritz_ref, panels_out, ritz_out, sems):
    copies = [
        pltpu.make_async_copy(panels_ref, panels_out, sems.at[0]),
        pltpu.make_async_copy(ritz_ref, ritz_out, sems.at[1]),
    ]
    for copy in copies:
        copy.start()
    for copy in copies:
        copy.wait()


def local(points, start_panel):
    nz = lax.axis_size("row") // 2
    ny = lax.axis_size("col") // NX
    rows, vec = start_panel.shape
    width = points.shape[1]
    chunk = NX * OWN
    mid = nz * HALF
    ncols = 2 * mid
    lines = 2 * ncols // LANES
    vmem = pltpu.VMEM
    dma = pltpu.SemaphoreType.DMA
    hbm = pl.BlockSpec(memory_space=pltpu.HBM)
    sums = [vmem((n, vec // 2, 2 * vec), f32) for n in (2 * NX, ny, nz)]
    out_shape = (
        jax.ShapeDtypeStruct((vec, rows), f32),
        jax.ShapeDtypeStruct((vec, vec), f32),
    )
    results = pl.pallas_call(
        functools.partial(kernel, nz, ny),
        out_shape=out_shape,
        in_specs=[hbm] * 2,
        out_specs=(pl.BlockSpec(memory_space=vmem),) * 2,
        scratch_shapes=[
            vmem(points.shape, f32),
            vmem((LANES, vec), f32),
            vmem((vec, LANES), f32),
            vmem((2, nz, HALF, LANES), f32),
            vmem((ny, NX, OWN, width), bf16),
            vmem((2, 2, nz, HALF, width), bf16),
            vmem((2, ny, chunk, ncols), bf16),
            vmem((2, 8, ncols), f32),
            vmem((lines, LANES), f32),
            vmem((2 * nz, lines, LANES), f32),
            vmem((2, ncols, LANES), f32),
            vmem((2, ncols, LANES), bf16),
            vmem((ny, NX, HALF, LANES), bf16),
            vmem((ny, NX, HALF, LANES), bf16),
            vmem((ny, HALF, LANES), bf16),
            vmem((ny, HALF, LANES), bf16),
            vmem((ny, NX, OWN, LANES), bf16),
            vmem((2, LANES, ncols), f32),
            vmem((2, vec, ncols), f32),
            vmem((vec, ncols), f32),
            vmem((nz, HALF, LANES), f32),
            vmem((nz, HALF, LANES), f32),
            *sums, *sums, *sums,
            vmem((ny, NX, HALF, LANES), f32),
            vmem((6 * vec, rows), bf16),
            dma, dma, dma((25,)), dma((25,)), dma((ny,)), dma((ny,)), dma((ny,)), dma((ny,)), dma((ny,)),
        ],
        compiler_params=pltpu.CompilerParams(
            collective_id=0, has_side_effects=True, vmem_limit_bytes=53 << 20
        ),
        name="embed",
    )(points, start_panel.T)
    panels, ritz_sum = pl.pallas_call(
        hand_over,
        out_shape=out_shape,
        in_specs=[pl.BlockSpec(memory_space=pl.ANY)] * 2,
        out_specs=(hbm,) * 2,
        scratch_shapes=[dma((2,))],
        compiler_params=pltpu.CompilerParams(vmem_limit_bytes=4 << 20),
        name="hand_over",
    )(*results)
    return panels.T, ritz_sum


def solution(mesh):
    in_specs = (P(("row", "col"), None), P("row", None))
    out_specs = (P("row", None), P())
    return jax.shard_map(local, mesh=mesh, in_specs=in_specs, out_specs=out_specs, check_vma=False)
```

```python
import functools
import math

import jax
import jax.numpy as jnp
from jax import lax
from jax.experimental import pallas as pl
from jax.experimental.pallas import tpu as pltpu
from jax.sharding import PartitionSpec as P

MESH = pl.DeviceIdType.MESH
NX = 4
HALF = 32
OWN = 2 * HALF
LANES = 128
SHARPNESS = 5.0
LOG2E = math.log2(math.e)
f32 = jnp.float32
bf16 = jnp.bfloat16


def dot(a, b, contract=((1,), (0,)), precision=None):
    return lax.dot_general(
        a, b, (contract, ((), ())), precision=precision, preferred_element_type=f32
    )


def full(a, b, contract=((1,), (0,))):
    return dot(a, b, contract, lax.Precision.HIGHEST)


def iota(shape, axis):
    return lax.broadcasted_iota(jnp.int32, shape, axis)


def add(parts):
    return functools.reduce(lambda a, b: a + b, parts)


def inverse_factor(gram, width=16):
    n = gram.shape[0]
    eye = jnp.where(iota((n, n), 0) == iota((n, n), 1), 1.0, 0.0).astype(f32)
    mat = jnp.concatenate([gram, eye], axis=1)
    done = []
    for b in range(0, n, width):
        m = n - b
        cols = [jnp.broadcast_to(mat[:, b + j:b + j + 1], (m, 2 * n)) for j in range(width)]
        rows = [mat[j:j + 1] for j in range(width)]
        for j in range(width):
            root = lax.rsqrt(cols[j][j:j + 1])
            cols[j], rows[j] = cols[j] * root, rows[j] * root
            for i in range(j + 1, width):
                factor = cols[j][i:i + 1]
                cols[i], rows[i] = cols[i] - factor * cols[j], rows[i] - factor * rows[j]
        done += rows
        mat = mat[width:]
        for j in range(width if m > width else 0):
            mat = mat - cols[j][width:] * rows[j]
    return jnp.concatenate(done, axis=0)[:, n:]


def pack(mat):
    n = mat.shape[0] // 2
    return jnp.concatenate([mat[:n], mat[n:]], axis=1)


def unpack(mat):
    n = mat.shape[1] // 2
    return jnp.concatenate([mat[:, :n], mat[:, n:]], axis=0)


def split(value, parts):
    out = []
    for _ in range(parts):
        out.append(value.astype(bf16))
        value = value - out[-1].astype(f32)
    return out


def far(i, me, n):
    return lax.rem(me + n // 2 + (1 - 2 * lax.rem(i, 2)) * ((i + 1) // 2), n)


def kernel(
    nz, ny, points_ref, start_ref, out_ref, ritz_ref,
    points, pair_rows, pair_cols, start, rowpts, colpts, tile, colsum, deg, deg_zc, inv_col,
    laid_out, panel, send_p, recv_px, send_y, recv_py, scaled, total_c, half_c, recv_c, send_z, recv_z,
    first_x, first_y, first_z, gram_x, gram_y, gram_z, ritz_x, ritz_y, ritz_z, whole, stack,
    load_sem, points_sem, send_sem, recv_sem, from_y, from_x, part_x, again_y, again_x,
):
    r, c = lax.axis_index("row"), lax.axis_index("col")
    z, core = r // 2, lax.rem(r, 2)
    y, x = c // NX, lax.rem(c, NX)
    axes = {
        "x": (NX, x, lambda p: (r, y * NX + p)),
        "y": (ny, y, lambda p: (r, p * NX + x)),
        "z": (nz, z, lambda p: (p * 2 + core, c)),
        "c": (2, core, lambda p: (z * 2 + p, c)),
        "xc": (2 * NX, x * 2 + core, lambda p: (z * 2 + lax.rem(p, 2), y * NX + p // 2)),
    }
    axes["zc"] = (2 * nz, r, lambda p: (p, c))
    axes["other core"] = (nz, z, lambda p: (p * 2 + 1 - core, c))
    beside = [lax.rem(y + step, ny) for step in ((1, ny - 1) if ny > 2 else range(1, ny))]
    for i, yy in enumerate(beside):
        axes[i] = (NX, x, lambda p, yy=yy: (r, yy * NX + p))
    met = ["xc", "y", "z", "other core", *range(len(beside))]
    count = sum(axes[axis][0] - 1 for axis in met)
    chunk = NX * OWN
    mid = nz * HALF
    ncols = 2 * mid
    total = 2 * ny * chunk * nz
    width = points_ref.shape[1]
    vec = ritz_ref.shape[0]

    load_points = pltpu.make_async_copy(points_ref, points, points_sem)
    load_points.start()
    here = pl.ds(pl.multiple_of(c // 2 * LANES, LANES), LANES)
    load = pltpu.make_async_copy(start_ref.at[:, here], pair_cols, load_sem)
    load.start()
    barrier = pltpu.get_barrier_semaphore()
    for axis in met:
        n, me, device = axes[axis]

        def greet(i, carry):
            pl.semaphore_signal(
                barrier, inc=1, device_id=device(far(i, me, n)), device_id_type=MESH
            )
            return carry
        lax.fori_loop(0, n - 1, greet, 0)

    sent = {}
    pending = {}

    def send(slot, axis, src, dst, got, recv=None):
        n, me, device = axes[axis]
        arrival = recv_sem.at[slot] if recv is None else recv

        def one(i, carry):
            p = far(i, me, n)
            pltpu.make_async_remote_copy(
                src_ref=src(p), dst_ref=dst, send_sem=send_sem.at[slot],
                recv_sem=arrival, device_id=device(p), device_id_type=MESH,
            ).start()
            return carry
        lax.fori_loop(0, n - 1, one, 0)
        sent[slot] = got
        if recv is None:
            pending[slot] = got

    def wait(ref, sem):
        pltpu.make_async_copy(ref, ref, sem).wait()

    def arrive(slot):
        wait(pending.pop(slot), recv_sem.at[slot])

    def drain():
        for slot in list(pending):
            arrive(slot)
        for slot, ref in sent.items():
            wait(ref, send_sem.at[slot])

    def all_sum(slot, axis, value, buf):
        n, me, _ = axes[axis]
        buf[me] = value
        send(slot, axis, lambda p: buf.at[me], buf.at[me], buf.at[pl.ds(0, n - 1)])

        def done():
            arrive(slot)
            return add([buf[i] for i in range(n)])
        return done

    def near(i):
        return lax.rem(y + 2 * ny + (2 * lax.rem(i, 2) - 1) * ((i + 1) // 2), ny)

    def spread(slot, buf, sems_y, sems_x):
        send(slot, "y", lambda p: buf.at[y, x], buf.at[y, x],
             buf.at[pl.ds(0, ny - 1), 0], sems_y.at[y])
        for axis in ("x", *range(len(beside))):
            send(slot + 1, axis, lambda p: buf.at[y, x], buf.at[y, x],
                 buf.at[:, pl.ds(0, NX - 1)], sems_x.at[y])

        def forward(i, carry):
            yy = near(i)
            wait(buf.at[yy, x], sems_y.at[yy])
            send(slot + 1, "x", lambda p: buf.at[yy, x], buf.at[yy, x],
                 buf.at[:, pl.ds(0, NX - 1)], sems_x.at[yy])
            return carry

        def on():
            lax.fori_loop(1 + len(beside), ny, forward, 0)
            for yy in beside:
                wait(buf.at[yy, x], sems_y.at[yy])
            sent[slot + 1] = buf.at[:, pl.ds(0, NX - 1)]
        return on

    shift = SHARPNESS * LOG2E
    load_points.wait()
    pts = points[...]
    unit = pts * lax.rsqrt(jnp.mean(pts * pts, axis=1, keepdims=True) + 1e-06)
    unit = (unit * math.sqrt(shift / width)).astype(bf16)
    rowpts[y, x] = unit
    colpts[core, :, z] = unit.reshape(2, HALF, width)
    colsum[...] = jnp.zeros_like(colsum)

    load.wait()
    pair_rows[...] = pair_cols[...].T
    odd = lax.rem(x, 2) * OWN
    start[core, z] = jnp.concatenate(
        [pair_rows[pl.ds(odd, HALF)], pair_rows[pl.ds(odd + HALF, HALF)]], axis=1
    )

    pl.semaphore_wait(barrier, count)
    rows_on = spread(0, rowpts, from_y, from_x)
    send(2, "z", lambda p: colpts.at[core, :, z], colpts.at[core, :, z],
         colpts.at[0, :, pl.ds(0, nz - 1)])
    rows_on()
    arrive(2)
    send(3, "c", lambda p: colpts.at[core], colpts.at[core], colpts.at[0])
    send(4, "z", lambda p: start.at[core, z], start.at[core, z], start.at[0, pl.ds(0, nz - 1)])

    def affinity(yy, k):
        left = rowpts[yy].reshape(chunk, width)
        right = colpts[k].reshape(ncols, width)
        value = jnp.exp2(dot(left, right, ((1,), (1,))) - shift)
        tile[k, yy] = value.astype(bf16)
        colsum[k] = colsum[k] + jnp.sum(value.reshape(chunk // 8, 8, ncols), axis=0)

    def chunk_here(i):
        yy = near(i)
        wait(rowpts.at[yy, pl.ds(0, NX - 1)], from_x.at[yy])
        return yy

    def near_half(i, carry):
        affinity(chunk_here(i), core)
        return carry

    def far_half(i, carry):
        affinity(near(i), 1 - core)
        return carry

    def both_halves(i, carry):
        yy = chunk_here(i)
        affinity(yy, core)
        affinity(yy, 1 - core)
        return carry
    early = ny - ny // 4
    lax.fori_loop(0, early, near_half, 0)
    arrive(3)
    lax.fori_loop(0, early, far_half, 0)
    lax.fori_loop(early, ny, both_halves, 0)
    lines = ncols // LANES
    for k in range(2):
        line = jnp.sum(colsum[k], axis=0, keepdims=True)
        for j in range(lines):
            deg[k * lines + j:k * lines + j + 1] = line[:, j * LANES:(j + 1) * LANES]

    degrees = all_sum(5, "zc", deg[...], deg_zc)
    arrive(4)
    send(6, "c", lambda p: start.at[core], start.at[core], start.at[0])
    arrive(6)
    low = iota((mid, LANES), 1) < vec
    for k in range(2):
        one = start[k].reshape(mid, LANES)
        two = pltpu.roll(one, vec, 1)
        laid_out[k, :mid] = jnp.where(low, one, two)
        laid_out[k, mid:] = jnp.where(low, two, one)
    inv_root = lax.rsqrt(degrees())
    for k in range(2):
        for j in range(lines):
            row = inv_root[k * lines + j:k * lines + j + 1]
            inv = jnp.broadcast_to(row, (LANES, LANES)).T
            part = slice(j * LANES, (j + 1) * LANES)
            inv_col[k, part] = inv
            panel[k, part] = (laid_out[k, part] * inv).astype(bf16)
    keep = iota((HALF, LANES), 1) < vec
    inv_packed = jnp.where(
        keep, inv_col[core, pl.ds(z * HALF, HALF)], inv_col[core, pl.ds(mid + z * HALF, HALF)]
    )

    pair = 2 if ny % 2 == 0 else 1

    def product(j):
        yy = near(ny - 1 - j)
        out = dot(tile[0, yy], panel[0]) + dot(tile[1, yy], panel[1])
        for s in range(NX):
            send_p[yy, s] = jnp.where(
                keep, out[s * OWN:s * OWN + HALF], out[s * OWN + HALF:(s + 1) * OWN]
            ).astype(bf16)

    def hand_on(j):
        yy = near(ny - 1 - j)
        send(8, "x", lambda p: send_p.at[yy, p], recv_px.at[yy, x],
             send_p.at[:, pl.ds(0, NX - 1)], part_x.at[yy])
        recv_px[yy, x] = send_p[yy, x]

    def products(j, carry):
        for b in range(pair):
            product(pair * j + b)
        for b in range(pair):
            hand_on(pair * j + b)
        return carry
    lax.fori_loop(0, ny // pair, products, 0)
    sent[8] = send_p.at[:, pl.ds(0, NX - 1)]

    def collect(j, carry):
        yy = near(ny - 1 - j)
        wait(recv_px.at[yy, pl.ds(0, NX - 1)], part_x.at[yy])
        send_y[yy] = add([recv_px[yy, i].astype(f32) for i in range(NX)]).astype(bf16)

        @pl.when(j < ny - 1)
        def _():
            pltpu.make_async_remote_copy(
                src_ref=send_y.at[yy], dst_ref=recv_py.at[y], send_sem=send_sem.at[9],
                recv_sem=recv_sem.at[9], device_id=(r, yy * NX + x), device_id_type=MESH,
            ).start()
        return carry
    lax.fori_loop(0, ny, collect, 0)
    sent[9] = pending[9] = recv_py.at[pl.ds(0, ny - 1)]
    recv_py[y] = send_y[y]
    arrive(9)
    first_packed = add([recv_py[i].astype(f32) for i in range(ny)]) * inv_packed

    scaled[y, x] = jnp.concatenate(split(unpack(first_packed * inv_packed), 2), axis=1)
    scaled_on = spread(10, scaled, again_y, again_x)
    first = unpack(first_packed)
    first_sum = all_sum(12, "z", pack(full(first, first, ((0,), (0,)))), first_z)
    scaled_on()
    first_sum = all_sum(15, "y", first_sum(), first_y)

    def transposed(i, k):
        yy = near(i)
        left = scaled[yy].reshape(chunk, 2 * vec).T
        return dot(left, tile[k, yy])

    def chunk_there(i):
        yy = near(i)
        wait(scaled.at[yy, pl.ds(0, NX - 1)], again_x.at[yy])

    def gather(i, carry):
        chunk_there(i)
        for k in range(2):
            total_c[k] = total_c[k] + transposed(i, k)
        return carry
    chunk_there(0)
    for k in range(2):
        total_c[k] = transposed(0, k)
    lax.fori_loop(1, ny - 1, gather, 0)

    def last_chunk(k):
        both = total_c[k] + transposed(ny - 1, k) if ny > 1 else total_c[k]
        half_c[k] = both[:vec] + both[vec:]
    if ny > 1:
        chunk_there(ny - 1)
    last_chunk(1 - core)
    send(14, "c", lambda p: half_c.at[p], recv_c, recv_c)
    last_chunk(core)
    first_sum = all_sum(13, "xc", first_sum(), first_x)
    arrive(14)
    both = half_c[core] + recv_c[...]
    both = jnp.concatenate([both[:, :mid], both[:, mid:]], axis=0).T
    send_z[...] = both.reshape(send_z.shape)
    send(16, "z", lambda p: send_z.at[p], recv_z.at[z], recv_z.at[pl.ds(0, nz - 1)])
    recv_z[z] = send_z[z]
    inv_first = inverse_factor(unpack(first_sum()) / total)
    none = jnp.zeros_like(inv_first)
    twice = jnp.concatenate(
        [jnp.concatenate([inv_first, none], axis=1), jnp.concatenate([none, inv_first], axis=1)],
        axis=0,
    )
    basis_packed = full(first_packed, twice, ((1,), (1,)))

    def product_sums(left, right):
        both = full(left, right, ((0,), (0,)))
        return pack(both[:vec, :vec] + both[vec:, vec:])
    arrive(16)
    second_packed = add([recv_z[i] for i in range(nz)]) * inv_packed
    second_packed = full(second_packed, twice, ((1,), (1,)))

    whole[y, x] = second_packed
    send(20, "y", lambda p: whole.at[y, x], whole.at[y, x], whole.at[pl.ds(0, ny - 1), 0])
    gram = all_sum(17, "xc", product_sums(second_packed, second_packed), gram_x)
    ritz = all_sum(18, "z", product_sums(basis_packed, second_packed), ritz_z)
    gram = all_sum(19, "y", gram(), gram_y)
    ritz = all_sum(22, "xc", ritz(), ritz_x)
    arrive(20)
    send(21, "x", lambda p: whole.at[:, x], whole.at[:, x], whole.at[:, pl.ds(0, NX - 1)])
    gram = all_sum(23, "z", gram(), gram_z)
    ritz = all_sum(24, "y", ritz(), ritz_y)
    arrive(21)

    def prepare(yy, carry):
        parts = []
        for s in range(NX):
            block = whole[yy, s]
            parts += [block, pltpu.roll(block, vec, 1)]
        high, middle, low = split(jnp.concatenate(parts, axis=0).T[:vec], 3)
        columns = pl.ds(pl.multiple_of(yy * chunk, chunk), chunk)
        stack[:, columns] = jnp.concatenate([high, middle, low, high, middle, high], axis=0)
        return carry
    lax.fori_loop(0, ny, prepare, 0)
    last = inverse_factor(unpack(gram()) / total)
    high, middle, low = [part.astype(f32) for part in split(last, 3)]
    last = jnp.concatenate([high, high, high, middle, middle, low], axis=1).astype(bf16)
    block = min(4 * chunk, ny * chunk)
    for j in range(0, ny * chunk, block):
        out_ref[:, j:j + block] = dot(last, stack[:, j:j + block])
    ritz_ref[...] = unpack(ritz()) / total
    drain()


def hand_over(panels_ref, ritz_ref, panels_out, ritz_out, sems):
    step = panels_ref.shape[0] // 4
    copies = [pltpu.make_async_copy(ritz_ref, ritz_out, sems.at[4])]
    for i in range(4):
        part = pl.ds(i * step, step)
        copies.append(pltpu.make_async_copy(panels_ref.at[part], panels_out.at[part], sems.at[i]))
    for copy in copies:
        copy.start()
    for copy in copies:
        copy.wait()


def local(points, start_panel):
    nz = lax.axis_size("row") // 2
    ny = lax.axis_size("col") // NX
    rows, vec = start_panel.shape
    width = points.shape[1]
    chunk = NX * OWN
    mid = nz * HALF
    ncols = 2 * mid
    lines = 2 * ncols // LANES
    vmem = pltpu.VMEM
    dma = pltpu.SemaphoreType.DMA
    hbm = pl.BlockSpec(memory_space=pltpu.HBM)
    sums = [vmem((n, vec // 2, 2 * vec), f32) for n in (2 * NX, ny, nz)]
    out_shape = (
        jax.ShapeDtypeStruct((vec, rows), f32),
        jax.ShapeDtypeStruct((vec, vec), f32),
    )
    results = pl.pallas_call(
        functools.partial(kernel, nz, ny),
        out_shape=out_shape,
        in_specs=[hbm] * 2,
        out_specs=(pl.BlockSpec(memory_space=vmem),) * 2,
        scratch_shapes=[
            vmem(points.shape, f32),
            vmem((LANES, vec), f32),
            vmem((vec, LANES), f32),
            vmem((2, nz, HALF, LANES), f32),
            vmem((ny, NX, OWN, width), bf16),
            vmem((2, 2, nz, HALF, width), bf16),
            vmem((2, ny, chunk, ncols), bf16),
            vmem((2, 8, ncols), f32),
            vmem((lines, LANES), f32),
            vmem((2 * nz, lines, LANES), f32),
            vmem((2, ncols, LANES), f32),
            vmem((2, ncols, LANES), f32),
            vmem((2, ncols, LANES), bf16),
            vmem((ny, NX, HALF, LANES), bf16),
            vmem((ny, NX, HALF, LANES), bf16),
            vmem((ny, HALF, LANES), bf16),
            vmem((ny, HALF, LANES), bf16),
            vmem((ny, NX, OWN, LANES), bf16),
            vmem((2, LANES, ncols), f32),
            vmem((2, vec, ncols), f32),
            vmem((vec, ncols), f32),
            vmem((nz, HALF, LANES), f32),
            vmem((nz, HALF, LANES), f32),
            *sums, *sums, *sums,
            vmem((ny, NX, HALF, LANES), f32),
            vmem((6 * vec, rows), bf16),
            dma, dma, dma((25,)), dma((25,)), dma((ny,)), dma((ny,)), dma((ny,)), dma((ny,)), dma((ny,)),
        ],
        compiler_params=pltpu.CompilerParams(
            collective_id=0, has_side_effects=True, vmem_limit_bytes=53 << 20
        ),
        name="embed",
    )(points, start_panel.T)
    panels, ritz_sum = pl.pallas_call(
        hand_over,
        out_shape=out_shape,
        in_specs=[pl.BlockSpec(memory_space=pl.ANY)] * 2,
        out_specs=(hbm,) * 2,
        scratch_shapes=[dma((5,))],
        compiler_params=pltpu.CompilerParams(vmem_limit_bytes=4 << 20),
        name="hand_over",
    )(*results)
    return panels.T, ritz_sum


def solution(mesh):
    in_specs = (P(("row", "col"), None), P("row", None))
    out_specs = (P("row", None), P())
    return jax.shard_map(local, mesh=mesh, in_specs=in_specs, out_specs=out_specs, check_vma=False)
```

```python
import functools
import math

import jax
import jax.numpy as jnp
from jax import lax
from jax.experimental import pallas as pl
from jax.experimental.pallas import tpu as pltpu
from jax.sharding import PartitionSpec as P

MESH = pl.DeviceIdType.MESH
NX = 4
HALF = 32
OWN = 2 * HALF
LANES = 128
SHARPNESS = 5.0
LOG2E = math.log2(math.e)
f32 = jnp.float32
bf16 = jnp.bfloat16


def dot(a, b, contract=((1,), (0,)), precision=None):
    return lax.dot_general(
        a, b, (contract, ((), ())), precision=precision, preferred_element_type=f32
    )


def full(a, b, contract=((1,), (0,))):
    return dot(a, b, contract, lax.Precision.HIGHEST)


def iota(shape, axis):
    return lax.broadcasted_iota(jnp.int32, shape, axis)


def add(parts):
    return functools.reduce(lambda a, b: a + b, parts)


def inverse_factor(gram, width=16):
    n = gram.shape[0]
    eye = jnp.where(iota((n, n), 0) == iota((n, n), 1), 1.0, 0.0).astype(f32)
    mat = jnp.concatenate([gram, eye], axis=1)
    done = []
    for b in range(0, n, width):
        m = n - b
        cols = [jnp.broadcast_to(mat[:, b + j:b + j + 1], (m, 2 * n)) for j in range(width)]
        rows = [mat[j:j + 1] for j in range(width)]
        for j in range(width):
            root = lax.rsqrt(cols[j][j:j + 1])
            cols[j], rows[j] = cols[j] * root, rows[j] * root
            for i in range(j + 1, width):
                factor = cols[j][i:i + 1]
                cols[i], rows[i] = cols[i] - factor * cols[j], rows[i] - factor * rows[j]
        done += rows
        mat = mat[width:]
        for j in range(width if m > width else 0):
            mat = mat - cols[j][width:] * rows[j]
    return jnp.concatenate(done, axis=0)[:, n:]


def pack(mat):
    n = mat.shape[0] // 2
    return jnp.concatenate([mat[:n], mat[n:]], axis=1)


def unpack(mat):
    n = mat.shape[1] // 2
    return jnp.concatenate([mat[:, :n], mat[:, n:]], axis=0)


def split(value, parts):
    out = []
    for _ in range(parts):
        out.append(value.astype(bf16))
        value = value - out[-1].astype(f32)
    return out


def far(i, me, n):
    return lax.rem(me + n // 2 + (1 - 2 * lax.rem(i, 2)) * ((i + 1) // 2), n)


def kernel(
    nz, ny, points_ref, start_ref, out_ref, ritz_ref,
    points, pair_rows, pair_cols, start, rowpts, colpts, tile, colsum, deg, deg_zc, inv_col,
    laid_out, panel, send_p, recv_px, send_y, recv_py, scaled, total_c, half_c, recv_c, send_z, recv_z,
    first_x, first_y, first_z, gram_x, gram_y, gram_z, ritz_x, ritz_y, ritz_z, whole, stack,
    load_sem, points_sem, send_sem, recv_sem, from_y, from_x, part_x, again_y, again_x,
):
    r, c = lax.axis_index("row"), lax.axis_index("col")
    z, core = r // 2, lax.rem(r, 2)
    y, x = c // NX, lax.rem(c, NX)
    axes = {
        "x": (NX, x, lambda p: (r, y * NX + p)),
        "y": (ny, y, lambda p: (r, p * NX + x)),
        "z": (nz, z, lambda p: (p * 2 + core, c)),
        "c": (2, core, lambda p: (z * 2 + p, c)),
        "xc": (2 * NX, x * 2 + core, lambda p: (z * 2 + lax.rem(p, 2), y * NX + p // 2)),
    }
    axes["zc"] = (2 * nz, r, lambda p: (p, c))
    axes["other core"] = (nz, z, lambda p: (p * 2 + 1 - core, c))
    steps = (ny // 2, 1, ny - 1) if ny % 2 == 0 and ny > 2 else range(1, ny)
    beside = [lax.rem(y + step, ny) for step in steps]
    for i, yy in enumerate(beside):
        axes[i] = (NX, x, lambda p, yy=yy: (r, yy * NX + p))
    met = ["xc", "y", "z", "other core", *range(len(beside))]
    count = sum(axes[axis][0] - 1 for axis in met)
    chunk = NX * OWN
    mid = nz * HALF
    ncols = 2 * mid
    total = 2 * ny * chunk * nz
    width = points_ref.shape[1]
    vec = ritz_ref.shape[0]

    load_points = pltpu.make_async_copy(points_ref, points, points_sem)
    load_points.start()
    here = pl.ds(pl.multiple_of(c // 2 * LANES, LANES), LANES)
    load = pltpu.make_async_copy(start_ref.at[:, here], pair_cols, load_sem)
    load.start()
    barrier = pltpu.get_barrier_semaphore()
    for axis in met:
        n, me, device = axes[axis]

        def greet(i, carry):
            pl.semaphore_signal(
                barrier, inc=1, device_id=device(far(i, me, n)), device_id_type=MESH
            )
            return carry
        lax.fori_loop(0, n - 1, greet, 0)

    sent = {}
    pending = {}

    def send(slot, axis, src, dst, got, recv=None):
        n, me, device = axes[axis]
        arrival = recv_sem.at[slot] if recv is None else recv

        def one(i, carry):
            p = far(i, me, n)
            pltpu.make_async_remote_copy(
                src_ref=src(p), dst_ref=dst, send_sem=send_sem.at[slot],
                recv_sem=arrival, device_id=device(p), device_id_type=MESH,
            ).start()
            return carry
        lax.fori_loop(0, n - 1, one, 0)
        sent[slot] = got
        if recv is None:
            pending[slot] = got

    def wait(ref, sem):
        pltpu.make_async_copy(ref, ref, sem).wait()

    def arrive(slot):
        wait(pending.pop(slot), recv_sem.at[slot])

    def drain():
        for slot in list(pending):
            arrive(slot)
        for slot, ref in sent.items():
            wait(ref, send_sem.at[slot])

    def all_sum(slot, axis, value, buf):
        n, me, _ = axes[axis]
        buf[me] = value
        send(slot, axis, lambda p: buf.at[me], buf.at[me], buf.at[pl.ds(0, n - 1)])

        def done():
            arrive(slot)
            return add([buf[i] for i in range(n)])
        return done

    def near(i):
        return lax.rem(y + 2 * ny + (2 * lax.rem(i, 2) - 1) * ((i + 1) // 2), ny)

    def spread(slot, buf, sems_y, sems_x):
        send(slot, "y", lambda p: buf.at[y, x], buf.at[y, x],
             buf.at[pl.ds(0, ny - 1), 0], sems_y.at[y])
        for axis in ("x", *range(len(beside))):
            send(slot + 1, axis, lambda p: buf.at[y, x], buf.at[y, x],
                 buf.at[:, pl.ds(0, NX - 1)], sems_x.at[y])

        def forward(i, carry):
            yy = near(i)
            wait(buf.at[yy, x], sems_y.at[yy])
            send(slot + 1, "x", lambda p: buf.at[yy, x], buf.at[yy, x],
                 buf.at[:, pl.ds(0, NX - 1)], sems_x.at[yy])
            return carry

        def on():
            lax.fori_loop(3, max(ny - 1, 3), forward, 0)
            for yy in beside:
                wait(buf.at[yy, x], sems_y.at[yy])
            sent[slot + 1] = buf.at[:, pl.ds(0, NX - 1)]
        return on

    shift = SHARPNESS * LOG2E
    load_points.wait()
    pts = points[...]
    unit = pts * lax.rsqrt(jnp.mean(pts * pts, axis=1, keepdims=True) + 1e-06)
    unit = (unit * math.sqrt(shift / width)).astype(bf16)
    rowpts[y, x] = unit
    colpts[core, :, z] = unit.reshape(2, HALF, width)
    colsum[...] = jnp.zeros_like(colsum)

    load.wait()
    pair_rows[...] = pair_cols[...].T
    odd = lax.rem(x, 2) * OWN
    start[core, z] = jnp.concatenate(
        [pair_rows[pl.ds(odd, HALF)], pair_rows[pl.ds(odd + HALF, HALF)]], axis=1
    )

    pl.semaphore_wait(barrier, count)
    rows_on = spread(0, rowpts, from_y, from_x)
    send(2, "z", lambda p: colpts.at[core, :, z], colpts.at[core, :, z],
         colpts.at[0, :, pl.ds(0, nz - 1)])
    rows_on()
    arrive(2)
    send(3, "c", lambda p: colpts.at[core], colpts.at[core], colpts.at[0])
    send(4, "z", lambda p: start.at[core, z], start.at[core, z], start.at[0, pl.ds(0, nz - 1)])

    def affinity(yy, k):
        left = rowpts[yy].reshape(chunk, width)
        right = colpts[k].reshape(ncols, width)
        value = jnp.exp2(dot(left, right, ((1,), (1,))) - shift)
        tile[k, yy] = value.astype(bf16)
        colsum[k] = colsum[k] + jnp.sum(value.reshape(chunk // 8, 8, ncols), axis=0)

    def chunk_here(i):
        yy = near(i)
        wait(rowpts.at[yy, pl.ds(0, NX - 1)], from_x.at[yy])
        return yy

    def near_half(i, carry):
        affinity(chunk_here(i), core)
        return carry

    def far_half(i, carry):
        affinity(near(i), 1 - core)
        return carry

    def both_halves(i, carry):
        yy = chunk_here(i)
        affinity(yy, core)
        affinity(yy, 1 - core)
        return carry
    early = ny - ny // 4
    lax.fori_loop(0, early, near_half, 0)
    arrive(3)
    lax.fori_loop(0, early, far_half, 0)
    lax.fori_loop(early, ny, both_halves, 0)
    lines = ncols // LANES
    for k in range(2):
        line = jnp.sum(colsum[k], axis=0, keepdims=True)
        for j in range(lines):
            deg[k * lines + j:k * lines + j + 1] = line[:, j * LANES:(j + 1) * LANES]

    degrees = all_sum(5, "zc", deg[...], deg_zc)
    arrive(4)
    send(6, "c", lambda p: start.at[core], start.at[core], start.at[0])
    arrive(6)
    low = iota((mid, LANES), 1) < vec
    for k in range(2):
        one = start[k].reshape(mid, LANES)
        two = pltpu.roll(one, vec, 1)
        laid_out[k, :mid] = jnp.where(low, one, two)
        laid_out[k, mid:] = jnp.where(low, two, one)
    inv_root = lax.rsqrt(degrees())
    for k in range(2):
        for j in range(lines):
            row = inv_root[k * lines + j:k * lines + j + 1]
            inv = jnp.broadcast_to(row, (LANES, LANES)).T
            part = slice(j * LANES, (j + 1) * LANES)
            inv_col[k, part] = inv
            panel[k, part] = (laid_out[k, part] * inv).astype(bf16)
    keep = iota((HALF, LANES), 1) < vec
    inv_packed = jnp.where(
        keep, inv_col[core, pl.ds(z * HALF, HALF)], inv_col[core, pl.ds(mid + z * HALF, HALF)]
    )

    pair = 2 if ny % 2 == 0 else 1

    def product(j):
        yy = near(ny - 1 - j)
        out = dot(tile[0, yy], panel[0]) + dot(tile[1, yy], panel[1])
        for s in range(NX):
            send_p[yy, s] = jnp.where(
                keep, out[s * OWN:s * OWN + HALF], out[s * OWN + HALF:(s + 1) * OWN]
            ).astype(bf16)

    def hand_on(j):
        yy = near(ny - 1 - j)
        send(8, "x", lambda p: send_p.at[yy, p], recv_px.at[yy, x],
             send_p.at[:, pl.ds(0, NX - 1)], part_x.at[yy])
        recv_px[yy, x] = send_p[yy, x]

    def products(j, carry):
        for b in range(pair):
            product(pair * j + b)
        for b in range(pair):
            hand_on(pair * j + b)
        return carry
    lax.fori_loop(0, ny // pair, products, 0)
    sent[8] = send_p.at[:, pl.ds(0, NX - 1)]

    def collect(j, carry):
        yy = near(ny - 1 - j)
        wait(recv_px.at[yy, pl.ds(0, NX - 1)], part_x.at[yy])
        send_y[yy] = add([recv_px[yy, i].astype(f32) for i in range(NX)]).astype(bf16)

        @pl.when(j < ny - 1)
        def _():
            pltpu.make_async_remote_copy(
                src_ref=send_y.at[yy], dst_ref=recv_py.at[y], send_sem=send_sem.at[9],
                recv_sem=recv_sem.at[9], device_id=(r, yy * NX + x), device_id_type=MESH,
            ).start()
        return carry
    lax.fori_loop(0, ny, collect, 0)
    sent[9] = pending[9] = recv_py.at[pl.ds(0, ny - 1)]
    recv_py[y] = send_y[y]
    arrive(9)
    first_packed = add([recv_py[i].astype(f32) for i in range(ny)]) * inv_packed

    scaled[y, x] = jnp.concatenate(split(unpack(first_packed * inv_packed), 2), axis=1)
    scaled_on = spread(10, scaled, again_y, again_x)
    first = unpack(first_packed)
    first_sum = all_sum(12, "z", pack(full(first, first, ((0,), (0,)))), first_z)
    scaled_on()
    first_sum = all_sum(15, "y", first_sum(), first_y)

    def transposed(i, k):
        yy = near(i)
        left = scaled[yy].reshape(chunk, 2 * vec).T
        return dot(left, tile[k, yy])

    def chunk_there(i):
        yy = near(i)
        wait(scaled.at[yy, pl.ds(0, NX - 1)], again_x.at[yy])

    def gather(i, carry):
        chunk_there(i)
        for k in range(2):
            total_c[k] = total_c[k] + transposed(i, k)
        return carry
    chunk_there(0)
    for k in range(2):
        total_c[k] = transposed(0, k)
    lax.fori_loop(1, ny - 1, gather, 0)

    def last_chunk(k):
        both = total_c[k] + transposed(ny - 1, k) if ny > 1 else total_c[k]
        half_c[k] = both[:vec] + both[vec:]
    if ny > 1:
        chunk_there(ny - 1)
    last_chunk(1 - core)
    send(14, "c", lambda p: half_c.at[p], recv_c, recv_c)
    last_chunk(core)
    first_sum = all_sum(13, "xc", first_sum(), first_x)
    arrive(14)
    both = half_c[core] + recv_c[...]
    both = jnp.concatenate([both[:, :mid], both[:, mid:]], axis=0).T
    send_z[...] = both.reshape(send_z.shape)
    send(16, "z", lambda p: send_z.at[p], recv_z.at[z], recv_z.at[pl.ds(0, nz - 1)])
    recv_z[z] = send_z[z]
    inv_first = inverse_factor(unpack(first_sum()) / total)
    none = jnp.zeros_like(inv_first)
    twice = jnp.concatenate(
        [jnp.concatenate([inv_first, none], axis=1), jnp.concatenate([none, inv_first], axis=1)],
        axis=0,
    )
    basis_packed = full(first_packed, twice, ((1,), (1,)))

    def product_sums(left, right):
        both = full(left, right, ((0,), (0,)))
        return pack(both[:vec, :vec] + both[vec:, vec:])
    arrive(16)
    second_packed = add([recv_z[i] for i in range(nz)]) * inv_packed
    second_packed = full(second_packed, twice, ((1,), (1,)))

    whole[y, x] = second_packed
    send(20, "y", lambda p: whole.at[y, x], whole.at[y, x], whole.at[pl.ds(0, ny - 1), 0])
    gram = all_sum(17, "xc", product_sums(second_packed, second_packed), gram_x)
    ritz = all_sum(18, "z", product_sums(basis_packed, second_packed), ritz_z)
    gram = all_sum(19, "y", gram(), gram_y)
    ritz = all_sum(22, "xc", ritz(), ritz_x)
    arrive(20)
    send(21, "x", lambda p: whole.at[:, x], whole.at[:, x], whole.at[:, pl.ds(0, NX - 1)])
    gram = all_sum(23, "z", gram(), gram_z)
    ritz = all_sum(24, "y", ritz(), ritz_y)
    arrive(21)

    def prepare(yy, carry):
        parts = []
        for s in range(NX):
            block = whole[yy, s]
            parts += [block, pltpu.roll(block, vec, 1)]
        high, middle, low = split(jnp.concatenate(parts, axis=0).T[:vec], 3)
        columns = pl.ds(pl.multiple_of(yy * chunk, chunk), chunk)
        stack[:, columns] = jnp.concatenate([high, middle, low, high, middle, high], axis=0)
        return carry
    lax.fori_loop(0, ny, prepare, 0)
    last = inverse_factor(unpack(gram()) / total)
    high, middle, low = [part.astype(f32) for part in split(last, 3)]
    last = jnp.concatenate([high, high, high, middle, middle, low], axis=1).astype(bf16)
    block = min(4 * chunk, ny * chunk)
    for j in range(0, ny * chunk, block):
        out_ref[:, j:j + block] = dot(last, stack[:, j:j + block])
    ritz_ref[...] = unpack(ritz()) / total
    drain()


def hand_over(panels_ref, ritz_ref, panels_out, ritz_out, sems):
    step = panels_ref.shape[0] // 4
    copies = [pltpu.make_async_copy(ritz_ref, ritz_out, sems.at[4])]
    for i in range(4):
        part = pl.ds(i * step, step)
        copies.append(pltpu.make_async_copy(panels_ref.at[part], panels_out.at[part], sems.at[i]))
    for copy in copies:
        copy.start()
    for copy in copies:
        copy.wait()


def local(points, start_panel):
    nz = lax.axis_size("row") // 2
    ny = lax.axis_size("col") // NX
    rows, vec = start_panel.shape
    width = points.shape[1]
    chunk = NX * OWN
    mid = nz * HALF
    ncols = 2 * mid
    lines = 2 * ncols // LANES
    vmem = pltpu.VMEM
    dma = pltpu.SemaphoreType.DMA
    hbm = pl.BlockSpec(memory_space=pltpu.HBM)
    sums = [vmem((n, vec // 2, 2 * vec), f32) for n in (2 * NX, ny, nz)]
    out_shape = (
        jax.ShapeDtypeStruct((vec, rows), f32),
        jax.ShapeDtypeStruct((vec, vec), f32),
    )
    results = pl.pallas_call(
        functools.partial(kernel, nz, ny),
        out_shape=out_shape,
        in_specs=[hbm] * 2,
        out_specs=(pl.BlockSpec(memory_space=vmem),) * 2,
        scratch_shapes=[
            vmem(points.shape, f32),
            vmem((LANES, vec), f32),
            vmem((vec, LANES), f32),
            vmem((2, nz, HALF, LANES), f32),
            vmem((ny, NX, OWN, width), bf16),
            vmem((2, 2, nz, HALF, width), bf16),
            vmem((2, ny, chunk, ncols), bf16),
            vmem((2, 8, ncols), f32),
            vmem((lines, LANES), f32),
            vmem((2 * nz, lines, LANES), f32),
            vmem((2, ncols, LANES), f32),
            vmem((2, ncols, LANES), f32),
            vmem((2, ncols, LANES), bf16),
            vmem((ny, NX, HALF, LANES), bf16),
            vmem((ny, NX, HALF, LANES), bf16),
            vmem((ny, HALF, LANES), bf16),
            vmem((ny, HALF, LANES), bf16),
            vmem((ny, NX, OWN, LANES), bf16),
            vmem((2, LANES, ncols), f32),
            vmem((2, vec, ncols), f32),
            vmem((vec, ncols), f32),
            vmem((nz, HALF, LANES), f32),
            vmem((nz, HALF, LANES), f32),
            *sums, *sums, *sums,
            vmem((ny, NX, HALF, LANES), f32),
            vmem((6 * vec, rows), bf16),
            dma, dma, dma((25,)), dma((25,)), dma((ny,)), dma((ny,)), dma((ny,)), dma((ny,)), dma((ny,)),
        ],
        compiler_params=pltpu.CompilerParams(
            collective_id=0, has_side_effects=True, vmem_limit_bytes=53 << 20
        ),
        name="embed",
    )(points, start_panel.T)
    panels, ritz_sum = pl.pallas_call(
        hand_over,
        out_shape=out_shape,
        in_specs=[pl.BlockSpec(memory_space=pl.ANY)] * 2,
        out_specs=(hbm,) * 2,
        scratch_shapes=[dma((5,))],
        compiler_params=pltpu.CompilerParams(vmem_limit_bytes=4 << 20),
        name="hand_over",
    )(*results)
    return panels.T, ritz_sum


def solution(mesh):
    in_specs = (P(("row", "col"), None), P("row", None))
    out_specs = (P("row", None), P())
    return jax.shard_map(local, mesh=mesh, in_specs=in_specs, out_specs=out_specs, check_vma=False)
```

```python
import functools
import math

import jax
import jax.numpy as jnp
from jax import lax
from jax.experimental import pallas as pl
from jax.experimental.pallas import tpu as pltpu
from jax.sharding import PartitionSpec as P

MESH = pl.DeviceIdType.MESH
NX = 4
HALF = 32
OWN = 2 * HALF
LANES = 128
SHARPNESS = 5.0
LOG2E = math.log2(math.e)
f32 = jnp.float32
bf16 = jnp.bfloat16


def dot(a, b, contract=((1,), (0,)), precision=None):
    return lax.dot_general(
        a, b, (contract, ((), ())), precision=precision, preferred_element_type=f32
    )


def full(a, b, contract=((1,), (0,))):
    return dot(a, b, contract, lax.Precision.HIGHEST)


def iota(shape, axis):
    return lax.broadcasted_iota(jnp.int32, shape, axis)


def add(parts):
    return functools.reduce(lambda a, b: a + b, parts)


def inverse_factor(gram, width=16):
    n = gram.shape[0]
    eye = jnp.where(iota((n, n), 0) == iota((n, n), 1), 1.0, 0.0).astype(f32)
    mat = jnp.concatenate([gram, eye], axis=1)
    done = []
    for b in range(0, n, width):
        m = n - b
        cols = [jnp.broadcast_to(mat[:, b + j:b + j + 1], (m, 2 * n)) for j in range(width)]
        rows = [mat[j:j + 1] for j in range(width)]
        for j in range(width):
            root = lax.rsqrt(cols[j][j:j + 1])
            cols[j], rows[j] = cols[j] * root, rows[j] * root
            for i in range(j + 1, width):
                factor = cols[j][i:i + 1]
                cols[i], rows[i] = cols[i] - factor * cols[j], rows[i] - factor * rows[j]
        done += rows
        mat = mat[width:]
        for j in range(width if m > width else 0):
            mat = mat - cols[j][width:] * rows[j]
    return jnp.concatenate(done, axis=0)[:, n:]


def pack(mat):
    n = mat.shape[0] // 2
    return jnp.concatenate([mat[:n], mat[n:]], axis=1)


def unpack(mat):
    n = mat.shape[1] // 2
    return jnp.concatenate([mat[:, :n], mat[:, n:]], axis=0)


def split(value, parts):
    out = []
    for _ in range(parts):
        out.append(value.astype(bf16))
        value = value - out[-1].astype(f32)
    return out


def far(i, me, n):
    return lax.rem(me + n // 2 + (1 - 2 * lax.rem(i, 2)) * ((i + 1) // 2), n)


def kernel(
    nz, ny, points_ref, start_ref, out_ref, ritz_ref,
    points, pair_rows, pair_cols, start, rowpts, colpts, tile, colsum, deg, deg_zc, inv_col,
    laid_out, panel, send_p, recv_px, send_y, recv_py, scaled, total_c, half_c, recv_c, send_z, recv_z,
    first_x, first_y, first_z, gram_x, gram_y, gram_z, ritz_x, ritz_y, ritz_z, gram_c, ritz_c, whole, stack,
    load_sem, points_sem, send_sem, recv_sem, from_y, from_x, part_x, again_y, again_x,
):
    r, c = lax.axis_index("row"), lax.axis_index("col")
    z, core = r // 2, lax.rem(r, 2)
    y, x = c // NX, lax.rem(c, NX)
    axes = {
        "x": (NX, x, lambda p: (r, y * NX + p)),
        "y": (ny, y, lambda p: (r, p * NX + x)),
        "z": (nz, z, lambda p: (p * 2 + core, c)),
        "c": (2, core, lambda p: (z * 2 + p, c)),
        "xc": (2 * NX, x * 2 + core, lambda p: (z * 2 + lax.rem(p, 2), y * NX + p // 2)),
    }
    axes["zc"] = (2 * nz, r, lambda p: (p, c))
    axes["other core"] = (nz, z, lambda p: (p * 2 + 1 - core, c))
    beside = [lax.rem(y + step, ny) for step in ((1, ny - 1) if ny > 2 else range(1, ny))]
    for i, yy in enumerate(beside):
        axes[i] = (NX, x, lambda p, yy=yy: (r, yy * NX + p))
    met = ["xc", "y", "z", "other core", *range(len(beside))]
    count = sum(axes[axis][0] - 1 for axis in met)
    chunk = NX * OWN
    mid = nz * HALF
    ncols = 2 * mid
    total = 2 * ny * chunk * nz
    width = points_ref.shape[1]
    vec = ritz_ref.shape[0]

    load_points = pltpu.make_async_copy(points_ref, points, points_sem)
    load_points.start()
    here = pl.ds(pl.multiple_of(c // 2 * LANES, LANES), LANES)
    load = pltpu.make_async_copy(start_ref.at[:, here], pair_cols, load_sem)
    load.start()
    barrier = pltpu.get_barrier_semaphore()
    for axis in met:
        n, me, device = axes[axis]

        def greet(i, carry):
            pl.semaphore_signal(
                barrier, inc=1, device_id=device(far(i, me, n)), device_id_type=MESH
            )
            return carry
        lax.fori_loop(0, n - 1, greet, 0)

    sent = {}
    pending = {}

    def send(slot, axis, src, dst, got, recv=None):
        n, me, device = axes[axis]
        arrival = recv_sem.at[slot] if recv is None else recv

        def one(i, carry):
            p = far(i, me, n)
            pltpu.make_async_remote_copy(
                src_ref=src(p), dst_ref=dst, send_sem=send_sem.at[slot],
                recv_sem=arrival, device_id=device(p), device_id_type=MESH,
            ).start()
            return carry
        lax.fori_loop(0, n - 1, one, 0)
        sent[slot] = got
        if recv is None:
            pending[slot] = got

    def wait(ref, sem):
        pltpu.make_async_copy(ref, ref, sem).wait()

    def arrive(slot):
        wait(pending.pop(slot), recv_sem.at[slot])

    def drain():
        for slot in list(pending):
            arrive(slot)
        for slot, ref in sent.items():
            wait(ref, send_sem.at[slot])

    def all_sum(slot, axis, value, buf):
        n, me, _ = axes[axis]
        buf[me] = value
        send(slot, axis, lambda p: buf.at[me], buf.at[me], buf.at[pl.ds(0, n - 1)])

        def done():
            arrive(slot)
            return add([buf[i] for i in range(n)])
        return done

    def near(i):
        return lax.rem(y + 2 * ny + (2 * lax.rem(i, 2) - 1) * ((i + 1) // 2), ny)

    def spread(slot, buf, sems_y, sems_x):
        send(slot, "y", lambda p: buf.at[y, x], buf.at[y, x],
             buf.at[pl.ds(0, ny - 1), 0], sems_y.at[y])
        for axis in ("x", *range(len(beside))):
            send(slot + 1, axis, lambda p: buf.at[y, x], buf.at[y, x],
                 buf.at[:, pl.ds(0, NX - 1)], sems_x.at[y])

        def forward(i, carry):
            yy = near(i)
            wait(buf.at[yy, x], sems_y.at[yy])
            send(slot + 1, "x", lambda p: buf.at[yy, x], buf.at[yy, x],
                 buf.at[:, pl.ds(0, NX - 1)], sems_x.at[yy])
            return carry

        def on():
            lax.fori_loop(1 + len(beside), ny, forward, 0)
            for yy in beside:
                wait(buf.at[yy, x], sems_y.at[yy])
            sent[slot + 1] = buf.at[:, pl.ds(0, NX - 1)]
        return on

    shift = SHARPNESS * LOG2E
    load_points.wait()
    pts = points[...]
    unit = pts * lax.rsqrt(jnp.mean(pts * pts, axis=1, keepdims=True) + 1e-06)
    unit = (unit * math.sqrt(shift / width)).astype(bf16)
    rowpts[y, x] = unit
    colpts[core, :, z] = unit.reshape(2, HALF, width)
    colsum[...] = jnp.zeros_like(colsum)

    load.wait()
    pair_rows[...] = pair_cols[...].T
    odd = lax.rem(x, 2) * OWN
    start[core, z] = jnp.concatenate(
        [pair_rows[pl.ds(odd, HALF)], pair_rows[pl.ds(odd + HALF, HALF)]], axis=1
    )

    pl.semaphore_wait(barrier, count)
    rows_on = spread(0, rowpts, from_y, from_x)
    send(2, "z", lambda p: colpts.at[core, :, z], colpts.at[core, :, z],
         colpts.at[0, :, pl.ds(0, nz - 1)])
    rows_on()
    arrive(2)
    send(3, "c", lambda p: colpts.at[core], colpts.at[core], colpts.at[0])
    send(4, "z", lambda p: start.at[core, z], start.at[core, z], start.at[0, pl.ds(0, nz - 1)])

    def affinity(yy, k):
        left = rowpts[yy].reshape(chunk, width)
        right = colpts[k].reshape(ncols, width)
        value = jnp.exp2(dot(left, right, ((1,), (1,))) - shift)
        tile[k, yy] = value.astype(bf16)
        colsum[k] = colsum[k] + jnp.sum(value.reshape(chunk // 8, 8, ncols), axis=0)

    def chunk_here(i):
        yy = near(i)
        wait(rowpts.at[yy, pl.ds(0, NX - 1)], from_x.at[yy])
        return yy

    def near_half(i, carry):
        affinity(chunk_here(i), core)
        return carry

    def far_half(i, carry):
        affinity(near(i), 1 - core)
        return carry

    def both_halves(i, carry):
        yy = chunk_here(i)
        affinity(yy, core)
        affinity(yy, 1 - core)
        return carry
    early = ny - ny // 4
    lax.fori_loop(0, early, near_half, 0)
    arrive(3)
    lax.fori_loop(0, early, far_half, 0)
    lax.fori_loop(early, ny, both_halves, 0)
    lines = ncols // LANES
    for k in range(2):
        line = jnp.sum(colsum[k], axis=0, keepdims=True)
        for j in range(lines):
            deg[k * lines + j:k * lines + j + 1] = line[:, j * LANES:(j + 1) * LANES]

    degrees = all_sum(5, "zc", deg[...], deg_zc)
    arrive(4)
    send(6, "c", lambda p: start.at[core], start.at[core], start.at[0])
    arrive(6)
    low = iota((mid, LANES), 1) < vec
    for k in range(2):
        one = start[k].reshape(mid, LANES)
        two = pltpu.roll(one, vec, 1)
        laid_out[k, :mid] = jnp.where(low, one, two)
        laid_out[k, mid:] = jnp.where(low, two, one)
    inv_root = lax.rsqrt(degrees())
    for k in range(2):
        for j in range(lines):
            row = inv_root[k * lines + j:k * lines + j + 1]
            inv = jnp.broadcast_to(row, (LANES, LANES)).T
            part = slice(j * LANES, (j + 1) * LANES)
            inv_col[k, part] = inv
            panel[k, part] = (laid_out[k, part] * inv).astype(bf16)
    keep = iota((HALF, LANES), 1) < vec
    inv_packed = jnp.where(
        keep, inv_col[core, pl.ds(z * HALF, HALF)], inv_col[core, pl.ds(mid + z * HALF, HALF)]
    )

    pair = 2 if ny % 2 == 0 else 1

    def product(j):
        yy = near(ny - 1 - j)
        out = dot(tile[0, yy], panel[0]) + dot(tile[1, yy], panel[1])
        for s in range(NX):
            send_p[yy, s] = jnp.where(
                keep, out[s * OWN:s * OWN + HALF], out[s * OWN + HALF:(s + 1) * OWN]
            ).astype(bf16)

    def hand_on(j):
        yy = near(ny - 1 - j)
        send(8, "x", lambda p: send_p.at[yy, p], recv_px.at[yy, x],
             send_p.at[:, pl.ds(0, NX - 1)], part_x.at[yy])
        recv_px[yy, x] = send_p[yy, x]

    def products(j, carry):
        for b in range(pair):
            product(pair * j + b)
        for b in range(pair):
            hand_on(pair * j + b)
        return carry
    lax.fori_loop(0, ny // pair, products, 0)
    sent[8] = send_p.at[:, pl.ds(0, NX - 1)]

    def collect(j, carry):
        yy = near(ny - 1 - j)
        wait(recv_px.at[yy, pl.ds(0, NX - 1)], part_x.at[yy])
        send_y[yy] = add([recv_px[yy, i].astype(f32) for i in range(NX)]).astype(bf16)

        @pl.when(j < ny - 1)
        def _():
            pltpu.make_async_remote_copy(
                src_ref=send_y.at[yy], dst_ref=recv_py.at[y], send_sem=send_sem.at[9],
                recv_sem=recv_sem.at[9], device_id=(r, yy * NX + x), device_id_type=MESH,
            ).start()
        return carry
    lax.fori_loop(0, ny, collect, 0)
    sent[9] = pending[9] = recv_py.at[pl.ds(0, ny - 1)]
    recv_py[y] = send_y[y]
    arrive(9)
    first_packed = add([recv_py[i].astype(f32) for i in range(ny)]) * inv_packed

    scaled[y, x] = jnp.concatenate(split(unpack(first_packed * inv_packed), 2), axis=1)
    scaled_on = spread(10, scaled, again_y, again_x)
    first = unpack(first_packed)
    first_sum = all_sum(12, "z", pack(full(first, first, ((0,), (0,)))), first_z)
    scaled_on()
    first_sum = all_sum(15, "y", first_sum(), first_y)

    def transposed(i, k):
        yy = near(i)
        left = scaled[yy].reshape(chunk, 2 * vec).T
        return dot(left, tile[k, yy])

    def chunk_there(i):
        yy = near(i)
        wait(scaled.at[yy, pl.ds(0, NX - 1)], again_x.at[yy])

    def gather(i, carry):
        chunk_there(i)
        for k in range(2):
            total_c[k] = total_c[k] + transposed(i, k)
        return carry
    chunk_there(0)
    for k in range(2):
        total_c[k] = transposed(0, k)
    lax.fori_loop(1, ny - 1, gather, 0)

    def last_chunk(k):
        both = total_c[k] + transposed(ny - 1, k) if ny > 1 else total_c[k]
        half_c[k] = both[:vec] + both[vec:]
    if ny > 1:
        chunk_there(ny - 1)
    last_chunk(1 - core)
    send(14, "c", lambda p: half_c.at[p], recv_c, recv_c)
    last_chunk(core)
    first_sum = all_sum(13, "xc", first_sum(), first_x)
    arrive(14)
    both = half_c[core] + recv_c[...]
    both = jnp.concatenate([both[:, :mid], both[:, mid:]], axis=0).T
    send_z[...] = both.reshape(send_z.shape)
    send(16, "z", lambda p: send_z.at[p], recv_z.at[z], recv_z.at[pl.ds(0, nz - 1)])
    recv_z[z] = send_z[z]
    inv_first = inverse_factor(unpack(first_sum()) / total)
    none = jnp.zeros_like(inv_first)
    twice = jnp.concatenate(
        [jnp.concatenate([inv_first, none], axis=1), jnp.concatenate([none, inv_first], axis=1)],
        axis=0,
    )
    basis_packed = full(first_packed, twice, ((1,), (1,)))

    def product_sums(left, right):
        both = full(left, right, ((0,), (0,)))
        return pack(both[:vec, :vec] + both[vec:, vec:])
    arrive(16)
    second_packed = add([recv_z[i] for i in range(nz)]) * inv_packed
    second_packed = full(second_packed, twice, ((1,), (1,)))

    whole[y, x] = second_packed
    send(20, "y", lambda p: whole.at[y, x], whole.at[y, x], whole.at[pl.ds(0, ny - 1), 0])
    gram = all_sum(17, "xc", product_sums(second_packed, second_packed), gram_x)
    ritz = all_sum(22, "xc", product_sums(basis_packed, second_packed), ritz_x)

    def my_half(value):
        n = value.shape[0] // 2
        return jnp.where(core == 0, value[:n], value[n:])

    def join_halves(slot, value, buf):
        buf[core] = value
        send(slot, "c", lambda p: buf.at[core], buf.at[core], buf.at[0])

        def done():
            arrive(slot)
            return jnp.concatenate([buf[0], buf[1]], axis=0)
        return done
    gram = all_sum(19, "y", my_half(gram()), gram_y)
    ritz = all_sum(18, "z", my_half(ritz()), ritz_z)
    arrive(20)
    send(21, "x", lambda p: whole.at[:, x], whole.at[:, x], whole.at[:, pl.ds(0, NX - 1)])
    gram = all_sum(23, "z", gram(), gram_z)
    ritz = all_sum(24, "y", ritz(), ritz_y)
    arrive(21)

    def prepare(yy, carry):
        parts = []
        for s in range(NX):
            block = whole[yy, s]
            parts += [block, pltpu.roll(block, vec, 1)]
        high, middle, low = split(jnp.concatenate(parts, axis=0).T[:vec], 3)
        columns = pl.ds(pl.multiple_of(yy * chunk, chunk), chunk)
        stack[:, columns] = jnp.concatenate([high, middle, low, high, middle, high], axis=0)
        return carry
    lax.fori_loop(0, ny, prepare, 0)
    gram = join_halves(25, gram(), gram_c)
    last = inverse_factor(unpack(gram()) / total)
    high, middle, low = [part.astype(f32) for part in split(last, 3)]
    last = jnp.concatenate([high, high, high, middle, middle, low], axis=1).astype(bf16)
    block = min(4 * chunk, ny * chunk)
    for j in range(0, ny * chunk, block):
        out_ref[:, j:j + block] = dot(last, stack[:, j:j + block])
    ritz = join_halves(26, ritz(), ritz_c)
    ritz_ref[...] = unpack(ritz()) / total
    drain()


def hand_over(panels_ref, ritz_ref, panels_out, ritz_out, sems):
    step = panels_ref.shape[0] // 4
    copies = [pltpu.make_async_copy(ritz_ref, ritz_out, sems.at[4])]
    for i in range(4):
        part = pl.ds(i * step, step)
        copies.append(pltpu.make_async_copy(panels_ref.at[part], panels_out.at[part], sems.at[i]))
    for copy in copies:
        copy.start()
    for copy in copies:
        copy.wait()


def local(points, start_panel):
    nz = lax.axis_size("row") // 2
    ny = lax.axis_size("col") // NX
    rows, vec = start_panel.shape
    width = points.shape[1]
    chunk = NX * OWN
    mid = nz * HALF
    ncols = 2 * mid
    lines = 2 * ncols // LANES
    vmem = pltpu.VMEM
    dma = pltpu.SemaphoreType.DMA
    hbm = pl.BlockSpec(memory_space=pltpu.HBM)
    sums = [vmem((n, vec // 2, 2 * vec), f32) for n in (2 * NX, ny, nz)]
    second_sums = [sums[0], *[vmem((n, vec // 4, 2 * vec), f32) for n in (ny, nz)]]
    out_shape = (
        jax.ShapeDtypeStruct((vec, rows), f32),
        jax.ShapeDtypeStruct((vec, vec), f32),
    )
    results = pl.pallas_call(
        functools.partial(kernel, nz, ny),
        out_shape=out_shape,
        in_specs=[hbm] * 2,
        out_specs=(pl.BlockSpec(memory_space=vmem),) * 2,
        scratch_shapes=[
            vmem(points.shape, f32),
            vmem((LANES, vec), f32),
            vmem((vec, LANES), f32),
            vmem((2, nz, HALF, LANES), f32),
            vmem((ny, NX, OWN, width), bf16),
            vmem((2, 2, nz, HALF, width), bf16),
            vmem((2, ny, chunk, ncols), bf16),
            vmem((2, 8, ncols), f32),
            vmem((lines, LANES), f32),
            vmem((2 * nz, lines, LANES), f32),
            vmem((2, ncols, LANES), f32),
            vmem((2, ncols, LANES), f32),
            vmem((2, ncols, LANES), bf16),
            vmem((ny, NX, HALF, LANES), bf16),
            vmem((ny, NX, HALF, LANES), bf16),
            vmem((ny, HALF, LANES), bf16),
            vmem((ny, HALF, LANES), bf16),
            vmem((ny, NX, OWN, LANES), bf16),
            vmem((2, LANES, ncols), f32),
            vmem((2, vec, ncols), f32),
            vmem((vec, ncols), f32),
            vmem((nz, HALF, LANES), f32),
            vmem((nz, HALF, LANES), f32),
            *sums, *second_sums, *second_sums, *[vmem((2, vec // 4, 2 * vec), f32)] * 2,
            vmem((ny, NX, HALF, LANES), f32),
            vmem((6 * vec, rows), bf16),
            dma, dma, dma((27,)), dma((27,)), dma((ny,)), dma((ny,)), dma((ny,)), dma((ny,)), dma((ny,)),
        ],
        compiler_params=pltpu.CompilerParams(
            collective_id=0, has_side_effects=True, vmem_limit_bytes=53 << 20
        ),
        name="embed",
    )(points, start_panel.T)
    panels, ritz_sum = pl.pallas_call(
        hand_over,
        out_shape=out_shape,
        in_specs=[pl.BlockSpec(memory_space=pl.ANY)] * 2,
        out_specs=(hbm,) * 2,
        scratch_shapes=[dma((5,))],
        compiler_params=pltpu.CompilerParams(vmem_limit_bytes=4 << 20),
        name="hand_over",
    )(*results)
    return panels.T, ritz_sum


def solution(mesh):
    in_specs = (P(("row", "col"), None), P("row", None))
    out_specs = (P("row", None), P())
    return jax.shard_map(local, mesh=mesh, in_specs=in_specs, out_specs=out_specs, check_vma=False)
```

```python
import functools
import math

import jax
import jax.numpy as jnp
from jax import lax
from jax.experimental import pallas as pl
from jax.experimental.pallas import tpu as pltpu
from jax.sharding import PartitionSpec as P

MESH = pl.DeviceIdType.MESH
NX = 4
HALF = 32
OWN = 2 * HALF
LANES = 128
SHARPNESS = 5.0
LOG2E = math.log2(math.e)
f32 = jnp.float32
bf16 = jnp.bfloat16


def dot(a, b, contract=((1,), (0,)), precision=None):
    return lax.dot_general(
        a, b, (contract, ((), ())), precision=precision, preferred_element_type=f32
    )


def full(a, b, contract=((1,), (0,))):
    return dot(a, b, contract, lax.Precision.HIGHEST)


def iota(shape, axis):
    return lax.broadcasted_iota(jnp.int32, shape, axis)


def add(parts):
    return functools.reduce(lambda a, b: a + b, parts)


def inverse_factor(gram, width=16):
    n = gram.shape[0]
    eye = jnp.where(iota((n, n), 0) == iota((n, n), 1), 1.0, 0.0).astype(f32)
    mat = jnp.concatenate([gram, eye], axis=1)
    done = []
    for b in range(0, n, width):
        m = n - b
        cols = [jnp.broadcast_to(mat[:, b + j:b + j + 1], (m, 2 * n)) for j in range(width)]
        rows = [mat[j:j + 1] for j in range(width)]
        for j in range(width):
            root = lax.rsqrt(cols[j][j:j + 1])
            cols[j], rows[j] = cols[j] * root, rows[j] * root
            for i in range(j + 1, width):
                factor = cols[j][i:i + 1]
                cols[i], rows[i] = cols[i] - factor * cols[j], rows[i] - factor * rows[j]
        done += rows
        mat = mat[width:]
        for j in range(width if m > width else 0):
            mat = mat - cols[j][width:] * rows[j]
    return jnp.concatenate(done, axis=0)[:, n:]


def pack(mat):
    n = mat.shape[0] // 2
    return jnp.concatenate([mat[:n], mat[n:]], axis=1)


def unpack(mat):
    n = mat.shape[1] // 2
    return jnp.concatenate([mat[:, :n], mat[:, n:]], axis=0)


def split(value, parts):
    out = []
    for _ in range(parts):
        out.append(value.astype(bf16))
        value = value - out[-1].astype(f32)
    return out


def far(i, me, n):
    return lax.rem(me + n // 2 + (1 - 2 * lax.rem(i, 2)) * ((i + 1) // 2), n)


def kernel(
    nz, ny, points_ref, start_ref, out_ref, ritz_ref,
    points, pair_rows, pair_cols, start, rowpts, colpts, tile, colsum, deg, deg_zc, inv_col,
    laid_out, panel, send_p, recv_px, send_y, recv_py, scaled, total_c, half_c, recv_c, send_z, recv_z,
    first_x, first_y, first_z, gram_x, gram_y, gram_z, ritz_x, ritz_y, ritz_z, whole, stack,
    load_sem, points_sem, send_sem, recv_sem, from_y, from_x, part_x, again_y, again_x,
):
    r, c = lax.axis_index("row"), lax.axis_index("col")
    z, core = r // 2, lax.rem(r, 2)
    y, x = c // NX, lax.rem(c, NX)
    axes = {
        "x": (NX, x, lambda p: (r, y * NX + p)),
        "y": (ny, y, lambda p: (r, p * NX + x)),
        "z": (nz, z, lambda p: (p * 2 + core, c)),
        "c": (2, core, lambda p: (z * 2 + p, c)),
        "xc": (2 * NX, x * 2 + core, lambda p: (z * 2 + lax.rem(p, 2), y * NX + p // 2)),
    }
    axes["zc"] = (2 * nz, r, lambda p: (p, c))
    axes["other core"] = (nz, z, lambda p: (p * 2 + 1 - core, c))
    met = ("xc", "y", "z", "other core")
    count = sum(axes[axis][0] - 1 for axis in met)
    chunk = NX * OWN
    mid = nz * HALF
    ncols = 2 * mid
    total = 2 * ny * chunk * nz
    width = points_ref.shape[1]
    vec = ritz_ref.shape[0]

    load_points = pltpu.make_async_copy(points_ref, points, points_sem)
    load_points.start()
    here = pl.ds(pl.multiple_of(c // 2 * LANES, LANES), LANES)
    load = pltpu.make_async_copy(start_ref.at[:, here], pair_cols, load_sem)
    load.start()
    barrier = pltpu.get_barrier_semaphore()
    for axis in met:
        n, me, device = axes[axis]

        def greet(i, carry):
            pl.semaphore_signal(
                barrier, inc=1, device_id=device(far(i, me, n)), device_id_type=MESH
            )
            return carry
        lax.fori_loop(0, n - 1, greet, 0)

    sent = {}
    pending = {}

    def send(slot, axis, src, dst, got, recv=None):
        n, me, device = axes[axis]
        arrival = recv_sem.at[slot] if recv is None else recv

        def one(i, carry):
            p = far(i, me, n)
            pltpu.make_async_remote_copy(
                src_ref=src(p), dst_ref=dst, send_sem=send_sem.at[slot],
                recv_sem=arrival, device_id=device(p), device_id_type=MESH,
            ).start()
            return carry
        lax.fori_loop(0, n - 1, one, 0)
        sent[slot] = got
        if recv is None:
            pending[slot] = got

    def wait(ref, sem):
        pltpu.make_async_copy(ref, ref, sem).wait()

    def arrive(slot):
        wait(pending.pop(slot), recv_sem.at[slot])

    def drain():
        for slot in list(pending):
            arrive(slot)
        for slot, ref in sent.items():
            wait(ref, send_sem.at[slot])

    def all_sum(slot, axis, value, buf):
        n, me, _ = axes[axis]
        buf[me] = value
        send(slot, axis, lambda p: buf.at[me], buf.at[me], buf.at[pl.ds(0, n - 1)])

        def done():
            arrive(slot)
            return add([buf[i] for i in range(n)])
        return done

    def near(i):
        return lax.rem(y + 2 * ny + (2 * lax.rem(i, 2) - 1) * ((i + 1) // 2), ny)

    def spread(slot, buf, sems_y, sems_x):
        send(slot, "y", lambda p: buf.at[y, x], buf.at[y, x],
             buf.at[pl.ds(0, ny - 1), 0], sems_y.at[y])
        send(slot + 1, "x", lambda p: buf.at[y, x], buf.at[y, x],
             buf.at[:, pl.ds(0, NX - 1)], sems_x.at[y])

        def forward(i, carry):
            yy = near(i)
            wait(buf.at[yy, x], sems_y.at[yy])
            send(slot + 1, "x", lambda p: buf.at[yy, x], buf.at[yy, x],
                 buf.at[:, pl.ds(0, NX - 1)], sems_x.at[yy])
            return carry

        def on():
            lax.fori_loop(1, ny, forward, 0)
            sent[slot + 1] = buf.at[:, pl.ds(0, NX - 1)]
        return on

    shift = SHARPNESS * LOG2E
    load_points.wait()
    pts = points[...]
    unit = pts * lax.rsqrt(jnp.mean(pts * pts, axis=1, keepdims=True) + 1e-06)
    unit = (unit * math.sqrt(shift / width)).astype(bf16)
    rowpts[y, x] = unit
    colpts[core, :, z] = unit.reshape(2, HALF, width)
    colsum[...] = jnp.zeros_like(colsum)

    load.wait()
    pair_rows[...] = pair_cols[...].T
    odd = lax.rem(x, 2) * OWN
    start[core, z] = jnp.concatenate(
        [pair_rows[pl.ds(odd, HALF)], pair_rows[pl.ds(odd + HALF, HALF)]], axis=1
    )

    pl.semaphore_wait(barrier, count)
    rows_on = spread(0, rowpts, from_y, from_x)
    send(2, "z", lambda p: colpts.at[core, :, z], colpts.at[core, :, z],
         colpts.at[0, :, pl.ds(0, nz - 1)])
    rows_on()
    arrive(2)
    send(3, "c", lambda p: colpts.at[core], colpts.at[core], colpts.at[0])
    send(4, "z", lambda p: start.at[core, z], start.at[core, z], start.at[0, pl.ds(0, nz - 1)])

    def affinity(yy, k):
        left = rowpts[yy].reshape(chunk, width)
        right = colpts[k].reshape(ncols, width)
        value = jnp.exp2(dot(left, right, ((1,), (1,))) - shift)
        tile[k, yy] = value.astype(bf16)
        colsum[k] = colsum[k] + jnp.sum(value.reshape(chunk // 8, 8, ncols), axis=0)

    def chunk_here(i):
        yy = near(i)
        wait(rowpts.at[yy, pl.ds(0, NX - 1)], from_x.at[yy])
        return yy

    def near_half(i, carry):
        affinity(chunk_here(i), core)
        return carry

    def far_half(i, carry):
        affinity(near(i), 1 - core)
        return carry

    def both_halves(i, carry):
        yy = chunk_here(i)
        affinity(yy, core)
        affinity(yy, 1 - core)
        return carry
    early = ny - ny // 4
    lax.fori_loop(0, early, near_half, 0)
    arrive(3)
    lax.fori_loop(0, early, far_half, 0)
    lax.fori_loop(early, ny, both_halves, 0)
    lines = ncols // LANES
    for k in range(2):
        line = jnp.sum(colsum[k], axis=0, keepdims=True)
        for j in range(lines):
            deg[k * lines + j:k * lines + j + 1] = line[:, j * LANES:(j + 1) * LANES]

    degrees = all_sum(5, "zc", deg[...], deg_zc)
    arrive(4)
    send(6, "c", lambda p: start.at[core], start.at[core], start.at[0])
    arrive(6)
    low = iota((mid, LANES), 1) < vec
    for k in range(2):
        one = start[k].reshape(mid, LANES)
        two = pltpu.roll(one, vec, 1)
        laid_out[k, :mid] = jnp.where(low, one, two)
        laid_out[k, mid:] = jnp.where(low, two, one)
    inv_root = lax.rsqrt(degrees())
    for k in range(2):
        for j in range(lines):
            row = inv_root[k * lines + j:k * lines + j + 1]
            inv = jnp.broadcast_to(row, (LANES, LANES)).T
            part = slice(j * LANES, (j + 1) * LANES)
            inv_col[k, part] = inv
            panel[k, part] = (laid_out[k, part] * inv).astype(bf16)
    keep = iota((HALF, LANES), 1) < vec
    inv_packed = jnp.where(
        keep, inv_col[core, pl.ds(z * HALF, HALF)], inv_col[core, pl.ds(mid + z * HALF, HALF)]
    )

    pair = 2 if ny % 2 == 0 else 1

    def product(j):
        yy = near(ny - 1 - j)
        out = dot(tile[0, yy], panel[0]) + dot(tile[1, yy], panel[1])
        for s in range(NX):
            send_p[yy, s] = jnp.where(
                keep, out[s * OWN:s * OWN + HALF], out[s * OWN + HALF:(s + 1) * OWN]
            ).astype(bf16)

    def hand_on(j):
        yy = near(ny - 1 - j)
        send(8, "x", lambda p: send_p.at[yy, p], recv_px.at[yy, x],
             send_p.at[:, pl.ds(0, NX - 1)], part_x.at[yy])
        recv_px[yy, x] = send_p[yy, x]

    def products(j, carry):
        for b in range(pair):
            product(pair * j + b)
        for b in range(pair):
            hand_on(pair * j + b)
        return carry
    lax.fori_loop(0, ny // pair, products, 0)
    sent[8] = send_p.at[:, pl.ds(0, NX - 1)]

    def collect(j, carry):
        yy = near(ny - 1 - j)
        wait(recv_px.at[yy, pl.ds(0, NX - 1)], part_x.at[yy])
        send_y[yy] = add([recv_px[yy, i].astype(f32) for i in range(NX)]).astype(bf16)

        @pl.when(j < ny - 1)
        def _():
            pltpu.make_async_remote_copy(
                src_ref=send_y.at[yy], dst_ref=recv_py.at[y], send_sem=send_sem.at[9],
                recv_sem=recv_sem.at[9], device_id=(r, yy * NX + x), device_id_type=MESH,
            ).start()
        return carry
    lax.fori_loop(0, ny, collect, 0)
    sent[9] = pending[9] = recv_py.at[pl.ds(0, ny - 1)]
    recv_py[y] = send_y[y]
    arrive(9)
    first_packed = add([recv_py[i].astype(f32) for i in range(ny)]) * inv_packed

    scaled[y, x] = jnp.concatenate(split(unpack(first_packed * inv_packed), 2), axis=1)
    scaled_on = spread(10, scaled, again_y, again_x)
    first = unpack(first_packed)
    first_sum = all_sum(12, "z", pack(full(first, first, ((0,), (0,)))), first_z)
    scaled_on()
    first_sum = all_sum(15, "y", first_sum(), first_y)

    def transposed(i, k):
        yy = near(i)
        left = scaled[yy].reshape(chunk, 2 * vec).T
        return dot(left, tile[k, yy])

    def chunk_there(i):
        yy = near(i)
        wait(scaled.at[yy, pl.ds(0, NX - 1)], again_x.at[yy])

    def gather(i, carry):
        chunk_there(i)
        for k in range(2):
            total_c[k] = total_c[k] + transposed(i, k)
        return carry
    chunk_there(0)
    for k in range(2):
        total_c[k] = transposed(0, k)
    lax.fori_loop(1, ny - 1, gather, 0)

    def last_chunk(k):
        both = total_c[k] + transposed(ny - 1, k) if ny > 1 else total_c[k]
        half_c[k] = both[:vec] + both[vec:]
    if ny > 1:
        chunk_there(ny - 1)
    last_chunk(1 - core)
    send(14, "c", lambda p: half_c.at[p], recv_c, recv_c)
    last_chunk(core)
    first_sum = all_sum(13, "xc", first_sum(), first_x)
    arrive(14)
    both = half_c[core] + recv_c[...]
    both = jnp.concatenate([both[:, :mid], both[:, mid:]], axis=0).T
    send_z[...] = both.reshape(send_z.shape)
    send(16, "z", lambda p: send_z.at[p], recv_z.at[z], recv_z.at[pl.ds(0, nz - 1)])
    recv_z[z] = send_z[z]
    inv_first = inverse_factor(unpack(first_sum()) / total)
    none = jnp.zeros_like(inv_first)
    twice = jnp.concatenate(
        [jnp.concatenate([inv_first, none], axis=1), jnp.concatenate([none, inv_first], axis=1)],
        axis=0,
    )
    basis_packed = full(first_packed, twice, ((1,), (1,)))

    def product_sums(left, right):
        both = full(left, right, ((0,), (0,)))
        return pack(both[:vec, :vec] + both[vec:, vec:])
    arrive(16)
    second_packed = add([recv_z[i] for i in range(nz)]) * inv_packed
    second_packed = full(second_packed, twice, ((1,), (1,)))

    whole[y, x] = second_packed
    send(20, "y", lambda p: whole.at[y, x], whole.at[y, x], whole.at[pl.ds(0, ny - 1), 0])
    gram = all_sum(17, "xc", product_sums(second_packed, second_packed), gram_x)
    ritz = all_sum(18, "z", product_sums(basis_packed, second_packed), ritz_z)
    gram = all_sum(19, "y", gram(), gram_y)
    ritz = all_sum(22, "xc", ritz(), ritz_x)
    arrive(20)
    send(21, "x", lambda p: whole.at[:, x], whole.at[:, x], whole.at[:, pl.ds(0, NX - 1)])
    gram = all_sum(23, "z", gram(), gram_z)
    ritz = all_sum(24, "y", ritz(), ritz_y)
    arrive(21)

    def prepare(yy, carry):
        parts = []
        for s in range(NX):
            block = whole[yy, s]
            parts += [block, pltpu.roll(block, vec, 1)]
        high, middle, low = split(jnp.concatenate(parts, axis=0).T[:vec], 3)
        columns = pl.ds(pl.multiple_of(yy * chunk, chunk), chunk)
        stack[:, columns] = jnp.concatenate([high, middle, low, high, middle, high], axis=0)
        return carry
    lax.fori_loop(0, ny, prepare, 0)
    last = inverse_factor(unpack(gram()) / total)
    high, middle, low = [part.astype(f32) for part in split(last, 3)]
    last = jnp.concatenate([high, high, high, middle, middle, low], axis=1).astype(bf16)
    block = min(4 * chunk, ny * chunk)
    for j in range(0, ny * chunk, block):
        out_ref[:, j:j + block] = dot(last, stack[:, j:j + block])
    ritz_ref[...] = unpack(ritz()) / total
    drain()


def hand_over(panels_ref, ritz_ref, panels_out, ritz_out, sems):
    step = panels_ref.shape[0] // 4
    copies = [pltpu.make_async_copy(ritz_ref, ritz_out, sems.at[4])]
    for i in range(4):
        part = pl.ds(i * step, step)
        copies.append(pltpu.make_async_copy(panels_ref.at[part], panels_out.at[part], sems.at[i]))
    for copy in copies:
        copy.start()
    for copy in copies:
        copy.wait()


def local(points, start_panel):
    nz = lax.axis_size("row") // 2
    ny = lax.axis_size("col") // NX
    rows, vec = start_panel.shape
    width = points.shape[1]
    chunk = NX * OWN
    mid = nz * HALF
    ncols = 2 * mid
    lines = 2 * ncols // LANES
    vmem = pltpu.VMEM
    dma = pltpu.SemaphoreType.DMA
    hbm = pl.BlockSpec(memory_space=pltpu.HBM)
    sums = [vmem((n, vec // 2, 2 * vec), f32) for n in (2 * NX, ny, nz)]
    out_shape = (
        jax.ShapeDtypeStruct((vec, rows), f32),
        jax.ShapeDtypeStruct((vec, vec), f32),
    )
    results = pl.pallas_call(
        functools.partial(kernel, nz, ny),
        out_shape=out_shape,
        in_specs=[hbm] * 2,
        out_specs=(pl.BlockSpec(memory_space=vmem),) * 2,
        scratch_shapes=[
            vmem(points.shape, f32),
            vmem((LANES, vec), f32),
            vmem((vec, LANES), f32),
            vmem((2, nz, HALF, LANES), f32),
            vmem((ny, NX, OWN, width), bf16),
            vmem((2, 2, nz, HALF, width), bf16),
            vmem((2, ny, chunk, ncols), bf16),
            vmem((2, 8, ncols), f32),
            vmem((lines, LANES), f32),
            vmem((2 * nz, lines, LANES), f32),
            vmem((2, ncols, LANES), f32),
            vmem((2, ncols, LANES), f32),
            vmem((2, ncols, LANES), bf16),
            vmem((ny, NX, HALF, LANES), bf16),
            vmem((ny, NX, HALF, LANES), bf16),
            vmem((ny, HALF, LANES), bf16),
            vmem((ny, HALF, LANES), bf16),
            vmem((ny, NX, OWN, LANES), bf16),
            vmem((2, LANES, ncols), f32),
            vmem((2, vec, ncols), f32),
            vmem((vec, ncols), f32),
            vmem((nz, HALF, LANES), f32),
            vmem((nz, HALF, LANES), f32),
            *sums, *sums, *sums,
            vmem((ny, NX, HALF, LANES), f32),
            vmem((6 * vec, rows), bf16),
            dma, dma, dma((25,)), dma((25,)), dma((ny,)), dma((ny,)), dma((ny,)), dma((ny,)), dma((ny,)),
        ],
        compiler_params=pltpu.CompilerParams(
            collective_id=0, has_side_effects=True, vmem_limit_bytes=53 << 20
        ),
        name="embed",
    )(points, start_panel.T)
    panels, ritz_sum = pl.pallas_call(
        hand_over,
        out_shape=out_shape,
        in_specs=[pl.BlockSpec(memory_space=pl.ANY)] * 2,
        out_specs=(hbm,) * 2,
        scratch_shapes=[dma((5,))],
        compiler_params=pltpu.CompilerParams(vmem_limit_bytes=4 << 20),
        name="hand_over",
    )(*results)
    return panels.T, ritz_sum


def solution(mesh):
    in_specs = (P(("row", "col"), None), P("row", None))
    out_specs = (P("row", None), P())
    return jax.shard_map(local, mesh=mesh, in_specs=in_specs, out_specs=out_specs, check_vma=False)
```
